256 devices in a mesh: dp: 8 (over z_hi, x), space: 32 (over y, z_lo, core).
Axes of the slice: x: 4, y: 4, z: 8 (z_hi: 2, z_lo: 4; z = z_hi * 4 + z_lo), core: 2. Of those that a mesh axis runs over, the one named last changes fastest.
Arguments:
- inputs: bfloat16 [16, 96, 180, 768], P('dp', 'space'), may hold values from -6 to 6
- cotangent: bfloat16 [16, 96, 180, 768], P('dp', 'space'), may hold values from -6 to 6
- kept_modes: int32 [8, 96, 96], P(None, None, 'space'), may hold values 0 or 1
- pad_rows: int32 [1], replicated, may hold values from 0 to 8
- weight_one: bfloat16 [2, 8, 96, 96], replicated, may hold values from -0.4375 to 0.4375
- bias_one: float32 [2, 8, 96], replicated, may hold values from -3 to 3
- weight_two: bfloat16 [2, 8, 96, 96], replicated, may hold values from -0.4375 to 0.4375
- bias_two: float32 [2, 8, 96], replicated, may hold values from -2 to 2
Outputs:
- output: bfloat16 [16, 96, 180, 768], P('dp', 'space')
- grad_in: bfloat16 [16, 96, 180, 768], P('dp', 'space')
- grad_weight_one: float32 [2, 8, 96, 96], replicated
- grad_bias_one: float32 [2, 8, 96], replicated
- grad_weight_two: float32 [2, 8, 96, 96], replicated
- grad_bias_two: float32 [2, 8, 96], replicated
The draws below stay inside these ranges and needn't reach their ends.
Inputs may be any that keep to these rules, and one draw needn't show every extreme that they name: kept_modes holds only 0 and 1.
All inputs are finite; a program needn't handle non-finite values. No bound on the sum of `kept_modes` on one device may be relied on, other than what follows from the above.
Results may differ from the reference program's by a relative error of at most 0.012.
Values may be sent and summed in bfloat16 or wider, within the bound.
A program may use at most 128 MiB of HBM per device.

```python
import jax
import jax.numpy as jnp
from jax import lax

H = 96
W = 180
C = 768
NB = 8
BS = 96
KW = 91
KWP = 96
IMAGES = 16


def with_ends(array, stream_key, smallest, top_value):
    longest = array.shape.index(max(array.shape))
    spots = []
    for shift in (0, 1):
        where = [jax.random.randint(jax.random.fold_in(stream_key, axis), (), 0, length) for axis, length in enumerate(array.shape)]
        where[longest] = (where[longest] + shift) % array.shape[longest]
        spots.append(tuple(where))
    return array.at[spots[0]].set(smallest).at[spots[1]].set(top_value)


def block_scale(rng, dims, shards, low, high):
    gain, own = 1.0, jax.random.fold_in(rng, 6)
    for axis_at, blocks in shards:
        heights = jnp.exp(jax.random.uniform(jax.random.fold_in(own, axis_at), (blocks,), jnp.float32, low / len(shards), high / len(shards)))
        gain = gain * jnp.repeat(heights, dims[axis_at] // blocks).reshape([-1 if axis == axis_at else 1 for axis in range(len(dims))])
    return gain


def bell_draw(rng, extent, scale, bound, cuts=(), kind=jnp.bfloat16):
    factor_of = block_scale(rng, extent, cuts, -0.22, 0.18) if cuts else 1.0
    entries = jax.random.normal(rng, extent, jnp.float32) * scale * factor_of
    return jnp.minimum(jnp.maximum(entries, -bound), bound).astype(kind)


def setup_inputs(seed: int = 0) -> dict:
    streams_of = jax.random.split(jax.random.key(seed), 9)
    inputs = bell_draw(streams_of[0], (IMAGES, H, W, C), 1.0, 6.0, ((0, 8), (1, 32)))
    cotangent = bell_draw(streams_of[1], (IMAGES, H, W, C), 1.0, 6.0, ((0, 8), (1, 32)))
    kept_modes = with_ends((jax.random.randint(streams_of[2], (NB, H, KWP), 0, 4) < 3).astype(jnp.int32), jax.random.fold_in(streams_of[2], 1), 0, 1)
    pad_rows = jax.random.randint(streams_of[3], (1,), 0, 9).astype(jnp.int32)
    weight_one = bell_draw(streams_of[4], (2, NB, BS, BS), (2 * BS) ** -0.5, 0.4375)
    bias_one = bell_draw(streams_of[5], (2, NB, BS), 0.5, 3.0, (), jnp.float32)
    weight_two = bell_draw(streams_of[6], (2, NB, BS, BS), (2 * BS) ** -0.5, 0.4375)
    bias_two = bell_draw(streams_of[7], (2, NB, BS), 0.3, 2.0, (), jnp.float32)
    return {"inputs": inputs, "cotangent": cotangent, "kept_modes": kept_modes, "pad_rows": pad_rows, "weight_one": weight_one, "bias_one": bias_one, "weight_two": weight_two, "bias_two": bias_two}


shrink = 0.25
gelu_scale = 0.7978845608028654
gelu_cubic = 0.044715
highest = lax.Precision.HIGHEST

def gelu_value(value):
    return 0.5 * value * (1.0 + jnp.tanh(gelu_scale * (value + gelu_cubic * value * value * value)))

def gelu_slope(value):
    tangent = jnp.tanh(gelu_scale * (value + gelu_cubic * value * value * value))
    inner = gelu_scale * (1.0 + 3.0 * gelu_cubic * value * value)
    return 0.5 * (1.0 + tangent) + 0.5 * value * (1.0 - tangent * tangent) * inner

def longitude_tables(width, padded):
    wavenum = jnp.arange(padded, dtype=jnp.int32)[:, None]
    column = jnp.arange(width, dtype=jnp.int32)[None, :]
    phase = 2.0 * jnp.pi / width * (wavenum * column % width).astype(jnp.float32)
    scaling = (wavenum < width // 2 + 1).astype(jnp.float32) / jnp.sqrt(jnp.float32(width))
    double = jnp.where(jnp.logical_or(wavenum == 0, 2 * wavenum == width), 1.0, 2.0).astype(jnp.float32)
    cosine = jnp.cos(phase) * scaling
    sine = jnp.sin(phase) * scaling
    forward = jnp.concatenate([cosine, -sine], 0).astype(jnp.bfloat16)
    inverse = jnp.concatenate([double * cosine, -double * sine], 0).astype(jnp.bfloat16)
    return (forward, inverse)

def latitude_table(length, sign):
    row = jnp.arange(length, dtype=jnp.int32)[:, None]
    column = jnp.arange(length, dtype=jnp.int32)[None, :]
    phase = 2.0 * jnp.pi / length * (row * column % length).astype(jnp.float32)
    scaling = 1.0 / jnp.sqrt(jnp.float32(length))
    cosine = jnp.cos(phase) * scaling
    sine = sign * jnp.sin(phase) * scaling
    upper = jnp.stack([cosine, sine], -1)
    lower = jnp.stack([-sine, cosine], -1)
    return jnp.stack([upper, lower], 0).astype(jnp.bfloat16)

def complex_matrix(weights):
    real_part, imag_part = (weights[0], weights[1])
    from_real = jnp.stack([real_part, imag_part], 2)
    from_imag = jnp.stack([-imag_part, real_part], 2)
    return jnp.stack([from_real, from_imag], 1)

def weight_grad(big):
    real_part = big[:, 0, :, 0, :] + big[:, 1, :, 1, :]
    imag_part = big[:, 0, :, 1, :] - big[:, 1, :, 0, :]
    return jnp.stack([real_part, imag_part], 0)

def product(form, left, right):
    return jnp.einsum(form, left.astype(jnp.float32), right.astype(jnp.float32), precision=highest)

def reference(inputs, cotangent, kept_modes, pad_rows, weight_one, bias_one, weight_two, bias_two):
    forward_lon, inverse_lon = longitude_tables(W, KWP)
    lat_forward = latitude_table(H, 1.0)
    lat_inverse = latitude_table(H, -1.0)
    big_one = complex_matrix(weight_one)
    big_two = complex_matrix(weight_two)
    valid = (jnp.arange(H, dtype=jnp.int32) < H - pad_rows[0]).astype(jnp.bfloat16)[:, None, None]
    wavenum = jnp.arange(KWP, dtype=jnp.int32)
    keep = kept_modes.astype(jnp.float32) * (wavenum < KW).astype(jnp.float32)[None, None, :]
    keep = jnp.transpose(keep, (1, 2, 0))[None, :, :, :, None]

    def one_image(carry, pair):
        image, cot = pair
        masked = image * valid
        spec = product('hwc,kw->hkc', masked, forward_lon).astype(jnp.bfloat16).reshape(H, 2, KWP, C)
        spectrum = product('pqhr,hrkc->pqkc', lat_forward, spec).astype(jnp.bfloat16).reshape(2, H, KWP, NB, BS)
        pre_one = product('rhknc,nrcpd->phknd', spectrum, big_one) + bias_one[:, None, None]
        hidden = gelu_value(pre_one).astype(jnp.bfloat16)
        pre_two = product('rhknc,nrcpd->phknd', hidden, big_two) + bias_two[:, None, None]
        tangent = jnp.tanh(pre_two / shrink)
        shrunk = pre_two - shrink * tangent
        filtered = (shrunk * keep).astype(jnp.bfloat16).reshape(2, H, KWP, C)
        back_lat = product('phqr,rqkc->hpkc', lat_inverse, filtered).astype(jnp.bfloat16).reshape(H, 2 * KWP, C)
        field = product('hkc,kw->hwc', back_lat, inverse_lon)
        output = ((image.astype(jnp.float32) + field) * valid.astype(jnp.float32)).astype(jnp.bfloat16)
        gated = cot * valid
        cot_spec = product('hwc,kw->hkc', gated, inverse_lon).astype(jnp.bfloat16).reshape(H, 2, KWP, C)
        d_filtered = product('pqhr,hrkc->pqkc', lat_forward, cot_spec).reshape(2, H, KWP, NB, BS)
        d_two = (d_filtered * keep * (tangent * tangent)).astype(jnp.bfloat16)
        grad_two = product('rhknc,phknd->nrcpd', hidden, d_two)
        bias_grad_two = lax.optimization_barrier(jnp.sum(d_two.astype(jnp.float32), axis=(1, 2)))
        d_hidden = product('phknd,nrcpd->rhknc', d_two, big_two)
        d_one = (d_hidden * gelu_slope(pre_one)).astype(jnp.bfloat16)
        grad_one = product('rhknc,phknd->nrcpd', spectrum, d_one)
        bias_grad_one = lax.optimization_barrier(jnp.sum(d_one.astype(jnp.float32), axis=(1, 2)))
        d_spec = product('phknd,nrcpd->rhknc', d_one, big_one).astype(jnp.bfloat16).reshape(2, H, KWP, C)
        d_lat = product('phqr,rqkc->hpkc', lat_inverse, d_spec).astype(jnp.bfloat16).reshape(H, 2 * KWP, C)
        d_field = product('hkc,kw->hwc', d_lat, forward_lon)
        grad_in = (gated.astype(jnp.float32) + d_field * valid.astype(jnp.float32)).astype(jnp.bfloat16)
        carry = (carry[0] + grad_one, carry[1] + bias_grad_one, carry[2] + grad_two, carry[3] + bias_grad_two)
        return (carry, (output, grad_in))
    zero_big = jnp.zeros((NB, 2, BS, 2, BS), jnp.float32)
    zero_bias = jnp.zeros((2, NB, BS), jnp.float32)
    totals, stacked = lax.scan(one_image, (zero_big, zero_bias, zero_big, zero_bias), (inputs, cotangent))
    scaling = 1.0 / (IMAGES * H)
    return (stacked[0], stacked[1], weight_grad(totals[0]) * scaling, totals[1] * scaling, weight_grad(totals[2]) * scaling, totals[3] * scaling)
```

```python
import numpy as np

import jax
import jax.numpy as jnp
from jax import lax
from jax.experimental import pallas as pl
from jax.experimental.pallas import tpu as pltpu
from jax.sharding import PartitionSpec as P

shrink = 0.25
gelu_scale = 0.7978845608028654
gelu_cubic = 0.044715

H = 96
W = 180
WP = 192
C = 768
HC = 384
NB = 8
BS = 96
KWP = 96
CHIPS = 16
IMAGES = 16
MESH = pl.DeviceIdType.MESH
f32 = jnp.float32
bf16 = jnp.bfloat16


def longitude_parts():
    wavenum = np.arange(KWP)[:, None]
    column = np.arange(W)[None, :]
    phase = np.float32(2.0 * np.pi / W) * (wavenum * column % W).astype(np.float32)
    scaling = (wavenum < W // 2 + 1).astype(np.float32) / np.sqrt(np.float32(W))
    double = np.where((wavenum == 0) | (2 * wavenum == W), 1.0, 2.0).astype(np.float32)
    cosine = np.cos(phase) * scaling
    sine = np.sin(phase) * scaling
    forward = np.stack([cosine, -sine])
    inverse = np.stack([double * cosine, -double * sine])
    return forward, inverse


def latitude_parts(sign):
    row = np.arange(H)[:, None]
    column = np.arange(H)[None, :]
    phase = np.float32(2.0 * np.pi / H) * (row * column % H).astype(np.float32)
    scaling = np.float32(1.0) / np.sqrt(np.float32(H))
    cosine = np.cos(phase) * scaling
    sine = np.float32(sign) * np.sin(phase) * scaling
    upper = np.stack([cosine, sine], -1)
    lower = np.stack([-sine, cosine], -1)
    return np.stack([upper, lower], 0)


def to_spectrum_table(part):
    out = np.zeros((3, 16, 4, 2, 2, 4, WP), np.float32)
    grouped = part.reshape(2, 16, 3, 2, W)
    for jj in range(4):
        out[:, :, jj, :, :, jj, :W] = grouped.transpose(2, 1, 0, 3, 4)
    return out.reshape(3, 256, 4 * WP)


def lat_tables():
    forward = latitude_parts(1.0)
    inverse = latitude_parts(-1.0)
    ahead = np.zeros((2, 2, 2, H, 16, 2, 6, 2, 2), np.float32)
    back = np.zeros((16, 2, 6, 2, 2, 2, 2, 2, H), np.float32)
    split = forward.reshape(2, H, 16, 6, 2)
    isplit = inverse.reshape(2, 16, 6, H, 2)
    for b in range(2):
        for kk in range(2):
            ahead[:, b, kk, :, :, b, :, :, kk] = split
            back[:, b, :, :, kk, :, b, kk, :] = isplit.transpose(1, 2, 0, 4, 3)
    return ahead.reshape(768, 768), back.reshape(768, 768)


def gelu_both(value):
    tangent = jnp.tanh(gelu_scale * (value + gelu_cubic * value * value * value))
    inner = gelu_scale * (1.0 + 3.0 * gelu_cubic * value * value)
    half = 0.5 * (1.0 + tangent)
    return value * half, half + 0.5 * value * (1.0 - tangent * tangent) * inner


def dot(left, right):
    return jnp.dot(left, right, preferred_element_type=f32)


def kernel(
    x_in, c_in, kept_in, w_one, w_two, b_in, ft_in, tt_in, lf_in, li_in,
    out_x, out_c, gw_one, gb_one, gw_two, gb_two,
    xs, fts, tts, lfs, lis, wraw, wd, keeps,
    send, got, facc, spec, hid, slope, kt, tmp, fil, dtwo, gacc, bacc,
    gp, gy, s_one, gx, s_two, gz, fx, fy, fc,
    load_sem, xin_send, xin_recv, ssem, rsem, oloc, osend, orecv, gsend, grecv,
):
    me = lax.axis_index("space")
    dp = lax.axis_index("dp")
    core = lax.rem(me, 2)
    other = 1 - core
    m = me // 2
    y = m // 4
    z = lax.rem(m, 4)
    zh = dp // 4
    x = lax.rem(dp, 4)
    buddy = (dp, 2 * m + other)
    mine = pl.ds(pl.multiple_of(core * HC, 128), HC)
    theirs = pl.ds(pl.multiple_of(other * HC, 128), HC)

    def load(src, dst, at):
        return pltpu.make_async_copy(src, dst, load_sem.at[at])

    own = []
    for v, ref in ((0, x_in), (1, c_in)):
        for b in range(2):
            own.append(load(ref.at[b, :, :, mine], xs.at[v, pl.ds(b * 6 + 3 * core, 3)], 2 * v + b))
    kept_own = load(kept_in.at[:, :, mine], keeps.at[pl.ds(3 * core, 3)], 4)
    tables = [
        load(ft_in.at[0], fts.at[0], 5),
        load(ft_in.at[1], fts.at[1], 6),
        load(lf_in, lfs, 7),
        load(w_one, wraw.at[0], 8),
        load(w_two, wraw.at[1], 11),
        load(li_in, lis, 9),
        load(tt_in, tts, 10),
    ]
    for copy in own[:2] + tables[:1] + own[2:] + tables[1:2] + [kept_own] + tables[2:]:
        copy.start()

    barrier = pltpu.get_barrier_semaphore()

    def greet_group(i, carry):
        peer = 2 * lax.rem(m + i, CHIPS) + core
        pl.semaphore_signal(barrier, inc=1, device_id=(dp, peer), device_id_type=MESH)
        return carry

    lax.fori_loop(1, CHIPS, greet_group, 0)
    pl.semaphore_signal(barrier, inc=1, device_id=buddy, device_id_type=MESH)
    for i in range(1, 4):
        pl.semaphore_signal(
            barrier, inc=1, device_id=(zh * 4 + lax.rem(x + i, 4), me), device_id_type=MESH
        )
    for i in range(4):
        far = (lax.rem(dp + 4, 8), 2 * (y * 4 + lax.rem(z + i, 4)) + core)
        pl.semaphore_signal(barrier, inc=1, device_id=far, device_id_type=MESH)
    pl.semaphore_wait(barrier, 15 + 1 + 3 + 4)

    swaps = []
    for v, ref in ((0, x_in), (1, c_in)):
        for b in range(2):
            swaps.append(
                pltpu.make_async_remote_copy(
                    src_ref=ref.at[b, :, :, theirs],
                    dst_ref=xs.at[v, pl.ds(b * 6 + 3 * core, 3)],
                    send_sem=xin_send.at[2 * v + b],
                    recv_sem=xin_recv.at[2 * v + b],
                    device_id=buddy,
                    device_id_type=MESH,
                )
            )
    swaps.append(
        pltpu.make_async_remote_copy(
            src_ref=kept_in.at[:, :, theirs],
            dst_ref=keeps.at[pl.ds(3 * core, 3)],
            send_sem=xin_send.at[4],
            recv_sem=xin_recv.at[4],
            device_id=buddy,
            device_id_type=MESH,
        )
    )
    for copy in swaps:
        copy.start()

    def send_chunk(phase, a):
        def one(i, carry):
            peer = lax.rem(m + i, CHIPS)
            pltpu.make_async_remote_copy(
                src_ref=send.at[phase, a, peer],
                dst_ref=got.at[phase, a, m],
                send_sem=ssem.at[phase, a],
                recv_sem=rsem.at[phase, a],
                device_id=(dp, 2 * peer + core),
                device_id_type=MESH,
            ).start()
            return carry

        lax.fori_loop(1, CHIPS, one, 0)

    def wait_chunk(phase, a, sem):
        whole = got.at[phase, a, pl.ds(0, 15)]
        pltpu.make_async_copy(whole, whole, sem.at[phase, a]).wait()

    def to_spectrum(v):
        def one(a, carry):
            for t in range(3):
                field = xs[v, 4 * t : 4 * t + 4].reshape(768, HC)
                result = dot(fts[v, a], field).astype(bf16).reshape(16, 16, HC)
                send[v, a, :, 16 * t : 16 * t + 16, :] = result
            send_chunk(v, a)
            got[v, a, m] = send[v, a, m]
            return carry

        lax.fori_loop(0, 3, one, 0)

    for v in range(2):
        for b in range(2):
            own[2 * v + b].wait()
            swaps[2 * v + b].wait()
        tables[v].wait()
        to_spectrum(v)

    gacc[...] = jnp.zeros_like(gacc)
    bacc[...] = jnp.zeros_like(bacc)
    for copy in [kept_own, swaps[4]] + tables[2:]:
        copy.wait()
    lane = lax.broadcasted_iota(jnp.int32, (BS, HC), 1)
    line = lax.broadcasted_iota(jnp.int32, (BS, HC), 0)
    for mat in range(2):
        for n in range(4):
            select = jnp.where(lane == line + BS * n, 1.0, 0.0).astype(bf16)
            real = dot(wraw[mat, 0, 4 * core + n], select)
            imag = dot(wraw[mat, 1, 4 * core + n], select)
            up, down = BS * n, HC + BS * n
            wd[mat, up : up + BS, :HC] = real.astype(bf16)
            wd[mat, up : up + BS, HC:] = imag.astype(bf16)
            wd[mat, down : down + BS, :HC] = (-imag).astype(bf16)
            wd[mat, down : down + BS, HC:] = real.astype(bf16)

    def spectral(phase, a, half):
        field = got[phase, a].reshape(768, HC)
        return dot(lfs[half * HC : half * HC + HC, :], field)

    def unspectral(phase, a):
        for t in range(2):
            result = dot(lis[t * HC : t * HC + HC, :], fil[...]).astype(bf16)
            send[phase, a, 8 * t : 8 * t + 8] = result.reshape(8, 48, HC)
        got[phase, a, m] = send[phase, a, m]

    def product(left, mat):
        for n in range(3):
            tmp[:, 256 * n : 256 * n + 256] = dot(left, wd[mat, :, 256 * n : 256 * n + 256])

    def product_turned(left, mat):
        for n in range(3):
            tmp[:, 256 * n : 256 * n + 256] = lax.dot_general(
                left,
                wd[mat, 256 * n : 256 * n + 256, :],
                (((1,), (1,)), ((), ())),
                preferred_element_type=f32,
            )

    def rows_of(step):
        return pl.ds(pl.multiple_of(step * 32, 32), 32)

    def kept_rows(a, step):
        kk = lax.rem(step // 3, 2)
        q = pl.multiple_of(lax.rem(step, 3) * 32, 32)
        return keeps[2 * a + kk, pl.ds(q, 32), :].astype(f32)

    def forward(a, carry):
        wait_chunk(0, a, rsem)
        for p in range(2):
            spec[a, :, p * HC : p * HC + HC] = spectral(0, a, p).astype(bf16)
        product(spec[a], 0)

        def gelu_rows(step, carry):
            rows = rows_of(step)
            for p in range(2):
                part = slice(p * HC, p * HC + HC)
                value, tilt = gelu_both(tmp[rows, part] + b_in[0, core, p])
                hid[a, rows, part] = value.astype(bf16)
                slope[a, rows, part] = tilt
            return carry

        lax.fori_loop(0, 12, gelu_rows, 0)
        product(hid[a], 1)

        def shrink_rows(step, carry):
            rows = rows_of(step)
            kept = kept_rows(a, step)
            for p in range(2):
                part = slice(p * HC, p * HC + HC)
                value = tmp[rows, part] + b_in[1, core, p]
                tangent = jnp.tanh(value * (1.0 / shrink))
                filtered = (value - shrink * tangent) * kept
                fil[pl.ds(pl.multiple_of(p * HC + step * 32, 32), 32), :] = filtered.astype(bf16)
                kt[a, rows, part] = kept * (tangent * tangent)
            return carry

        lax.fori_loop(0, 12, shrink_rows, 0)
        unspectral(2, a)
        return carry

    lax.fori_loop(0, 3, forward, 0)
    send_chunk(2, 0)

    def add_grad(mat, left, right):
        for n in range(3):
            part = slice(256 * n, 256 * n + 256)
            gacc[mat, :, part] += lax.dot_general(
                left, right[:, part], (((0,), (0,)), ((), ())), preferred_element_type=f32
            )

    def backward(a, carry):
        wait_chunk(1, a, rsem)
        for p in range(2):
            tmp[:, p * HC : p * HC + HC] = spectral(1, a, p)

        def scaled_rows(mat, scale):
            def one(step, carry):
                rows = rows_of(step)
                for p in range(2):
                    part = slice(p * HC, p * HC + HC)
                    value = (tmp[rows, part] * scale[a, rows, part]).astype(bf16)
                    dtwo[rows, part] = value
                    bacc[mat, :, part] += value.astype(f32).reshape(4, 8, HC).sum(0)
                return carry

            lax.fori_loop(0, 12, one, 0)

        scaled_rows(1, kt)
        add_grad(1, hid[a], dtwo[...])
        product_turned(dtwo[...], 1)
        scaled_rows(0, slope)
        add_grad(0, spec[a], dtwo[...])
        product_turned(dtwo[...], 0)
        for p in range(2):
            fil[p * HC : p * HC + HC, :] = tmp[:, p * HC : p * HC + HC].astype(bf16)
        unspectral(3, a)
        return carry

    lax.fori_loop(0, 3, backward, 0)

    for mat in range(2):
        for n in range(4):
            start = BS * n // 128 * 128
            shift = BS * n - start
            window = 256 if shift + BS > 128 else 128
            up = slice(BS * n, BS * n + BS)
            down = slice(HC + BS * n, HC + BS * n + BS)
            left = slice(start, start + window)
            right = slice(HC + start, HC + start + window)

            def align(value):
                if shift:
                    value = pltpu.roll(value, window - shift, 1)
                return value[:, :128]

            gp[n, 2 * mat, :BS, :] = align(gacc[mat, up, left] + gacc[mat, down, right])
            gp[n, 2 * mat + 1, :BS, :] = align(gacc[mat, up, right] - gacc[mat, down, left])
            gp[n, 2 * mat, BS:, :] = align(bacc[mat, :, left])
            gp[n, 2 * mat + 1, BS:, :] = align(bacc[mat, :, right])

    def gather(count, source, target, device, at):
        def copy(i):
            return pltpu.make_async_remote_copy(
                src_ref=source(i),
                dst_ref=target,
                send_sem=gsend.at[at],
                recv_sem=grecv.at[at],
                device_id=device(i),
                device_id_type=MESH,
            )

        for i in range(count):
            copy(i).start()

    def settle(part, at):
        pltpu.make_async_copy(part, part, grecv.at[at]).wait()

    def row_peer(i):
        return lax.rem(y + 1 + i, 4)

    def x_peer(i):
        return lax.rem(x + 1 + i, 4)

    def row_device(i):
        return (dp, 2 * (row_peer(i) * 4 + z) + core)

    def x_device(i):
        return (zh * 4 + x_peer(i), me)

    def z_device(i):
        if i < 3:
            return (dp, 2 * (y * 4 + lax.rem(z + 1 + i, 4)) + core)
        return (lax.rem(dp + 4, 8), 2 * (y * 4 + lax.rem(z + i - 3, 4)) + core)

    gather(3, lambda i: gp.at[row_peer(i)], gy.at[y], row_device, 0)
    send_chunk(2, 1)
    gy[y] = gp[y]
    settle(gy.at[pl.ds(0, 3)], 0)
    s_one[...] = (gy[0] + gy[1]) + (gy[2] + gy[3])
    gather(3, lambda i: s_one.at[x_peer(i)], gx.at[x], x_device, 1)
    send_chunk(2, 2)
    gx[x] = s_one[x]
    settle(gx.at[pl.ds(0, 3)], 1)
    s_two[...] = (gx[0] + gx[1]) + (gx[2] + gx[3])
    gather(7, lambda i: s_two, gz.at[zh * 4 + z], z_device, 2)
    send_chunk(3, 0)
    gz[zh * 4 + z] = s_two[...]
    settle(gz.at[pl.ds(0, 7)], 2)
    total = gz[0]
    for i in range(1, 8):
        total = total + gz[i]
    fx[x] = total * (1.0 / (IMAGES * H))
    gather(3, lambda i: fx.at[x], fx.at[x], x_device, 3)
    send_chunk(3, 1)
    settle(fx.at[pl.ds(0, 3)], 3)
    fy[y] = fx[...]
    gather(3, lambda i: fy.at[y], fy.at[y], row_device, 4)
    send_chunk(3, 2)
    settle(fy.at[pl.ds(0, 3)], 4)
    gather(1, lambda i: fy, fc, lambda i: buddy, 5)

    def leave(v):
        def part(a, carry):
            wait_chunk(2 + v, a, rsem)

            def one(t, carry):
                piece = got[2 + v, a, :, pl.ds(pl.multiple_of(16 * t, 16), 16), :]
                piece = piece.reshape(256, HC)
                for j in range(4):
                    rows = pl.ds(j * WP, WP)
                    facc[t, rows, :] += dot(tts[1 - v, a, j * WP : j * WP + WP, :], piece)
                return carry

            lax.fori_loop(0, 3, one, 0)
            return carry

        def begin(t, carry):
            facc[t] = xs[v, pl.ds(4 * t, 4)].reshape(768, HC).astype(f32)
            return carry

        def finish(t, carry):
            xs[v, pl.ds(4 * t, 4)] = facc[t].astype(bf16).reshape(4, WP, HC)
            return carry

        lax.fori_loop(0, 3, begin, 0)
        lax.fori_loop(0, 3, part, 0)
        lax.fori_loop(0, 3, finish, 0)
        ref = (out_x, out_c)[v]
        copies = []
        for b in range(2):
            copies.append(
                pltpu.make_async_remote_copy(
                    src_ref=xs.at[v, pl.ds(b * 6 + 3 * other, 3)],
                    dst_ref=ref.at[b, :, :, mine],
                    send_sem=osend.at[2 * v + b],
                    recv_sem=orecv.at[2 * v + b],
                    device_id=buddy,
                    device_id_type=MESH,
                )
            )
            copies[-1].start()
        for b in range(2):
            copies.append(
                pltpu.make_async_copy(
                    xs.at[v, pl.ds(b * 6 + 3 * core, 3)], ref.at[b, :, :, mine], oloc.at[2 * v + b]
                )
            )
            copies[-1].start()
        return copies

    leaving = leave(0)

    settle(fc, 5)
    for half, held in ((core, fy), (other, fc)):

        def one(n, carry):
            for mat, (weight, bias) in enumerate(((gw_one, gb_one), (gw_two, gb_two))):
                for p in range(2):
                    weight[p, 4 * half + n] = held[n, 2 * mat + p, :BS, :BS]
                    bias[p, 4 * half + n] = held[n, 2 * mat + p, BS:, :BS].sum(0, keepdims=True)
            return carry

        lax.fori_loop(0, 4, one, 0)

    leaving += leave(1)
    for copy in leaving:
        copy.wait()

    def sent(i, carry):
        wait_chunk(i // 3, lax.rem(i, 3), ssem)
        return carry

    lax.fori_loop(0, 12, sent, 0)
    for at, part in (
        (0, gy.at[pl.ds(0, 3)]),
        (1, gx.at[pl.ds(0, 3)]),
        (2, gz.at[pl.ds(0, 7)]),
        (3, fx.at[pl.ds(0, 3)]),
        (4, fy.at[pl.ds(0, 3)]),
        (5, fc),
    ):
        pltpu.make_async_copy(part, part, gsend.at[at]).wait()


def mix(x_pad, c_pad, kept, w_one, w_two, bias):
    forward_lon, inverse_lon = longitude_parts()
    ahead = np.stack([to_spectrum_table(forward_lon), to_spectrum_table(inverse_lon)])
    lf, li = lat_tables()
    as_bf16 = lambda table: jnp.asarray(table.astype(jnp.bfloat16))
    tables = (as_bf16(ahead), as_bf16(ahead.transpose(0, 1, 3, 2)), as_bf16(lf), as_bf16(li))
    anywhere = pl.BlockSpec(memory_space=pl.ANY)
    vmem = pl.BlockSpec(memory_space=pltpu.VMEM)
    dma = pltpu.SemaphoreType.DMA
    return pl.pallas_call(
        kernel,
        out_shape=(
            jax.ShapeDtypeStruct(x_pad.shape, bf16),
            jax.ShapeDtypeStruct(c_pad.shape, bf16),
            jax.ShapeDtypeStruct((2, NB, BS, BS), f32),
            jax.ShapeDtypeStruct((2, NB, 1, BS), f32),
            jax.ShapeDtypeStruct((2, NB, BS, BS), f32),
            jax.ShapeDtypeStruct((2, NB, 1, BS), f32),
        ),
        in_specs=[anywhere] * 5 + [vmem] + [anywhere] * 4,
        out_specs=(anywhere, anywhere, vmem, vmem, vmem, vmem),
        scratch_shapes=[
            pltpu.VMEM((2, 12, WP, HC), bf16),
            pltpu.VMEM((2, 3, 256, 768), bf16),
            pltpu.VMEM((2, 3, 768, 256), bf16),
            pltpu.VMEM((768, 768), bf16),
            pltpu.VMEM((768, 768), bf16),
            pltpu.VMEM((2, 2, NB, BS, BS), bf16),
            pltpu.VMEM((2, 768, 768), bf16),
            pltpu.VMEM((6, H, HC), bf16),
            pltpu.VMEM((4, 3, CHIPS, 48, HC), bf16),
            pltpu.VMEM((4, 3, CHIPS, 48, HC), bf16),
            pltpu.VMEM((3, 768, HC), f32),
            pltpu.VMEM((3, HC, 768), bf16),
            pltpu.VMEM((3, HC, 768), bf16),
            pltpu.VMEM((3, HC, 768), f32),
            pltpu.VMEM((3, HC, 768), f32),
            pltpu.VMEM((HC, 768), f32),
            pltpu.VMEM((768, HC), bf16),
            pltpu.VMEM((HC, 768), bf16),
            pltpu.VMEM((2, 768, 768), f32),
            pltpu.VMEM((2, 8, 768), f32),
            pltpu.VMEM((4, 4, 104, 128), f32),
            pltpu.VMEM((4, 4, 104, 128), f32),
            pltpu.VMEM((4, 104, 128), f32),
            pltpu.VMEM((4, 104, 128), f32),
            pltpu.VMEM((104, 128), f32),
            pltpu.VMEM((8, 104, 128), f32),
            pltpu.VMEM((4, 104, 128), f32),
            pltpu.VMEM((4, 4, 104, 128), f32),
            pltpu.VMEM((4, 4, 104, 128), f32),
            dma((12,)),
            dma((5,)),
            dma((5,)),
            dma((4, 3)),
            dma((4, 3)),
            dma((4,)),
            dma((4,)),
            dma((4,)),
            dma((6,)),
            dma((6,)),
        ],
        compiler_params=pltpu.CompilerParams(
            collective_id=0, has_side_effects=True, vmem_limit_bytes=61 * 2**20
        ),
    )(x_pad, c_pad, kept, w_one, w_two, bias, *tables)


def on_device(inputs, cotangent, kept_modes, pad_rows, weight_one, bias_one, weight_two, bias_two):
    rows = inputs.shape[1]
    local_modes = kept_modes.shape[2]
    place = lax.axis_index("space")
    row_ids = place * rows + jnp.arange(rows, dtype=jnp.int32)
    valid = (row_ids < H - pad_rows[0]).astype(bf16)[None, :, None, None]
    mode_ids = place * local_modes + jnp.arange(local_modes, dtype=jnp.int32)
    kept = kept_modes * (mode_ids < W // 2 + 1).astype(jnp.int32)[None, None, :]
    kept = jnp.transpose(kept, (2, 1, 0)).astype(bf16)
    kept = jnp.broadcast_to(kept[..., None], (local_modes, H, NB, BS)).reshape(local_modes, H, C)
    margin = ((0, 0), (0, 0), (0, WP - W), (0, 0))
    x_pad = jnp.pad(inputs * valid, margin)
    c_pad = jnp.pad(cotangent * valid, margin)
    bias = jnp.stack([bias_one.reshape(2, 2, HC), bias_two.reshape(2, 2, HC)])
    bias = jnp.transpose(bias, (0, 2, 1, 3))[:, :, :, None, :]
    out_x, out_c, gw_one, gb_one, gw_two, gb_two = mix(
        x_pad, c_pad, kept, weight_one, weight_two, bias
    )
    return (
        out_x[:, :, :W] * valid,
        out_c[:, :, :W] * valid,
        gw_one,
        gb_one[:, :, 0],
        gw_two,
        gb_two[:, :, 0],
    )


def solution(mesh):
    placed = (
        P("dp", "space", None, None),
        P("dp", "space", None, None),
        P(None, None, "space"),
        P(),
        P(),
        P(),
        P(),
        P(),
    )
    return jax.shard_map(
        on_device,
        mesh=mesh,
        in_specs=placed,
        out_specs=(P("dp", "space", None, None), P("dp", "space", None, None), P(), P(), P(), P()),
        check_vma=False,
    )
```

```python
import numpy as np

import jax
import jax.numpy as jnp
from jax import lax
from jax.experimental import pallas as pl
from jax.experimental.pallas import tpu as pltpu
from jax.sharding import PartitionSpec as P

shrink = 0.25
gelu_scale = 0.7978845608028654
gelu_cubic = 0.044715

H = 96
W = 180
WIDE = 768
C = 768
HC = 384
NB = 8
BS = 96
KWP = 96
CHIPS = 16
IMAGES = 16
MESH = pl.DeviceIdType.MESH
f32 = jnp.float32
bf16 = jnp.bfloat16


def longitude_parts():
    wavenum = np.arange(KWP)[:, None]
    column = np.arange(W)[None, :]
    phase = np.float32(2.0 * np.pi / W) * (wavenum * column % W).astype(np.float32)
    scaling = (wavenum < W // 2 + 1).astype(np.float32) / np.sqrt(np.float32(W))
    double = np.where((wavenum == 0) | (2 * wavenum == W), 1.0, 2.0).astype(np.float32)
    cosine = np.cos(phase) * scaling
    sine = np.sin(phase) * scaling
    forward = np.stack([cosine, -sine])
    inverse = np.stack([double * cosine, -double * sine])
    return forward, inverse


def latitude_parts(sign):
    row = np.arange(H)[:, None]
    column = np.arange(H)[None, :]
    phase = np.float32(2.0 * np.pi / H) * (row * column % H).astype(np.float32)
    scaling = np.float32(1.0) / np.sqrt(np.float32(H))
    cosine = np.cos(phase) * scaling
    sine = np.float32(sign) * np.sin(phase) * scaling
    upper = np.stack([cosine, sine], -1)
    lower = np.stack([-sine, cosine], -1)
    return np.stack([upper, lower], 0)


def to_spectrum_table(part):
    out = np.zeros((3, 16, 2, 2, 2, 2, 2, W, 2), np.float32)
    grouped = part.reshape(2, 16, 3, 2, W).transpose(2, 1, 0, 3, 4)
    for jj in range(2):
        for b in range(2):
            out[:, :, jj, b, :, :, jj, :, b] = grouped
    out = out.reshape(3, 256, 4 * W)
    return np.pad(out, ((0, 0), (0, 0), (0, WIDE - 4 * W)))


def lat_tables():
    forward = latitude_parts(1.0)
    inverse = latitude_parts(-1.0)
    ahead = np.zeros((2, 2, 2, H, 16, 6, 2, 2, 2), np.float32)
    back = np.zeros((16, 6, 2, 2, 2, 2, 2, 2, H), np.float32)
    split = forward.reshape(2, H, 16, 6, 2)
    isplit = inverse.reshape(2, 16, 6, H, 2)
    for b in range(2):
        for kk in range(2):
            ahead[:, b, kk, :, :, :, b, :, kk] = split
            back[:, :, b, :, kk, :, b, kk, :] = isplit.transpose(1, 2, 0, 4, 3)
    return ahead.reshape(768, 768), back.reshape(768, 768)


def gelu_both(value):
    tangent = jnp.tanh(gelu_scale * (value + gelu_cubic * value * value * value))
    inner = gelu_scale * (1.0 + 3.0 * gelu_cubic * value * value)
    half = 0.5 * (1.0 + tangent)
    return value * half, half + 0.5 * value * (1.0 - tangent * tangent) * inner


def dot(left, right):
    return jnp.dot(left, right, preferred_element_type=f32)


def kernel(
    x_in, c_in, kept_in, pad_in, w_one, w_two, b_one, b_two, ft_in, tt_in, lf_in, li_in,
    out_x, out_c, gw_one, gb_one, gw_two, gb_two,
    xs, fts, tts, lfs, lis, wraw, wd, kraw, keeps, brow,
    send, got, facc, spec, hid, slope, kt, tmp, fil, dtwo, gacc, bacc,
    gp, gr, s_two, gz, s_three, fin, fy, fc,
    load_sem, xown, xin_send, xin_recv, ssem, rsem, oloc, osend, orecv, gsend, grecv,
):
    me = lax.axis_index("space")
    dp = lax.axis_index("dp")
    core = lax.rem(me, 2)
    other = 1 - core
    m = me // 2
    y = m // 4
    z = lax.rem(m, 4)
    zh = dp // 4
    x = lax.rem(dp, 4)
    depth = zh * 4 + z
    buddy = (dp, 2 * m + other)

    def tile(which, l):
        return pl.ds(pl.multiple_of(which * HC + l * 128, 128), 128)

    def row_slot(v, j6, l):
        return xs.at[v, j6 // 2, l, pl.ds(lax.rem(j6, 2) * W, W)]

    def row_slots(v, j6):
        return xs.at[v, j6 // 2, :, pl.ds(lax.rem(j6, 2) * W, W)]

    def load(src, dst, at):
        return pltpu.make_async_copy(src, dst, load_sem.at[at])

    def start_own(v, ref):
        for j in range(3):
            for l in range(3):
                pltpu.make_async_copy(
                    ref.at[j, :, :, tile(core, l)], row_slot(v, 3 * core + j, l), xown.at[v, j]
                ).start()

    kept_own = load(kept_in, kraw.at[pl.ds(3 * core, 3)], 0)
    tables = [
        load(ft_in.at[0], fts.at[0], 1),
        load(ft_in.at[1], fts.at[1], 2),
        load(lf_in, lfs, 3),
        load(w_one, wraw.at[0], 4),
        load(w_two, wraw.at[1], 5),
        load(li_in, lis, 6),
        load(tt_in, tts, 7),
    ]
    start_own(0, x_in)
    tables[0].start()
    start_own(1, c_in)
    for copy in tables[1:2] + [kept_own] + tables[2:]:
        copy.start()

    barrier = pltpu.get_barrier_semaphore()

    def greet(device):
        pl.semaphore_signal(barrier, inc=1, device_id=device, device_id_type=MESH)

    def greet_group(i, carry):
        greet((dp, 2 * lax.rem(m + i, CHIPS) + core))
        return carry

    def plane_device(i):
        row = lax.rem(y + i // 4, 4)
        return (zh * 4 + lax.rem(x + lax.rem(i, 4), 4), 2 * (row * 4 + z) + core)

    def greet_plane(i, carry):
        greet(plane_device(4 * (i // 3) + lax.rem(i, 3) + 1))
        return carry

    lax.fori_loop(1, CHIPS, greet_group, 0)
    greet(buddy)
    lax.fori_loop(0, 12, greet_plane, 0)
    for i in range(4):
        greet((lax.rem(dp + 4, 8), 2 * (y * 4 + lax.rem(z + i, 4)) + core))
    pl.semaphore_wait(barrier, 15 + 1 + 12 + 4)

    def swap(v, ref):
        for j in range(3):
            for l in range(3):
                pltpu.make_async_remote_copy(
                    src_ref=ref.at[j, :, :, tile(other, l)],
                    dst_ref=row_slot(v, 3 * core + j, l),
                    send_sem=xin_send.at[v, j],
                    recv_sem=xin_recv.at[v, j],
                    device_id=buddy,
                    device_id_type=MESH,
                ).start()

    kept_swap = pltpu.make_async_remote_copy(
        src_ref=kept_in,
        dst_ref=kraw.at[pl.ds(3 * core, 3)],
        send_sem=xin_send.at[2, 0],
        recv_sem=xin_recv.at[2, 0],
        device_id=buddy,
        device_id_type=MESH,
    )
    swap(0, x_in)
    swap(1, c_in)
    kept_swap.start()
    xs[:, :, :, 2 * W :] = jnp.zeros((2, 3, 3, WIDE // 2 - 2 * W, 2, 128), bf16)

    def row_valid(j6):
        return jnp.where(6 * m + j6 < H - pad_in[0], 1.0, 0.0).astype(f32)

    def field(v, t):
        return jnp.concatenate([xs.at[v, t, l].reshape(WIDE, 128)[...] for l in range(3)], axis=1)

    def send_chunk(phase, a):
        def one(i, carry):
            peer = lax.rem(m + i, CHIPS)
            pltpu.make_async_remote_copy(
                src_ref=send.at[phase, a, peer],
                dst_ref=got.at[phase, a, m],
                send_sem=ssem.at[phase, a],
                recv_sem=rsem.at[phase, a],
                device_id=(dp, 2 * peer + core),
                device_id_type=MESH,
            ).start()
            return carry

        lax.fori_loop(1, CHIPS, one, 0)

    def wait_chunk(phase, a, sem):
        whole = got.at[phase, a, pl.ds(0, 15)]
        pltpu.make_async_copy(whole, whole, sem.at[phase, a]).wait()

    def to_spectrum(v):
        line = lax.broadcasted_iota(jnp.int32, (256, HC), 0)
        second = lax.rem(line // 8, 2) == 1

        def one(a, carry):
            for t in range(3):
                result = dot(fts[v, a], field(v, t))
                result = result * jnp.where(second, row_valid(2 * t + 1), row_valid(2 * t))
                send[v, a, :, 16 * t : 16 * t + 16, :] = result.astype(bf16).reshape(16, 16, HC)
            send_chunk(v, a)
            got[v, a, m] = send[v, a, m]
            return carry

        lax.fori_loop(0, 3, one, 0)

    for v in range(2):
        for j in range(3):
            here, there = row_slots(v, 3 * core + j), row_slots(v, 3 * other + j)
            pltpu.make_async_copy(here, here, xown.at[v, j]).wait()
            pltpu.make_async_copy(there, there, xin_recv.at[v, j]).wait()
        tables[v].wait()
        to_spectrum(v)

    gacc[...] = jnp.zeros_like(gacc)
    bacc[...] = jnp.zeros_like(bacc)
    for copy in [kept_own, kept_swap] + tables[2:]:
        copy.wait()
    lane = lax.broadcasted_iota(jnp.int32, (BS, HC), 1)
    line = lax.broadcasted_iota(jnp.int32, (BS, HC), 0)
    for mat in range(2):
        for n in range(4):
            select = jnp.where(lane == line + BS * n, 1.0, 0.0).astype(bf16)
            real = dot(wraw[mat, 0, 4 * core + n], select)
            imag = dot(wraw[mat, 1, 4 * core + n], select)
            up, down = BS * n, HC + BS * n
            wd[mat, up : up + BS, :HC] = real.astype(bf16)
            wd[mat, up : up + BS, HC:] = imag.astype(bf16)
            wd[mat, down : down + BS, :HC] = (-imag).astype(bf16)
            wd[mat, down : down + BS, HC:] = real.astype(bf16)

    lane = lax.broadcasted_iota(jnp.int32, (NB, HC), 1)
    block = lax.broadcasted_iota(jnp.int32, (NB, HC), 0) - 4 * core
    spread = (lane >= BS * block) & (lane < BS * block + BS)
    for slot in range(6):
        bits = kraw[slot].astype(f32).astype(bf16)
        wide = lax.dot_general(
            bits,
            jnp.where(spread, 1.0, 0.0).astype(bf16),
            (((0,), (0,)), ((), ())),
            preferred_element_type=f32,
        )
        real_mode = jnp.where(6 * m + slot < W // 2 + 1, 1.0, 0.0).astype(f32)
        keeps[slot] = (wide * real_mode).astype(bf16)
    lane = lax.broadcasted_iota(jnp.int32, (BS, HC), 1)
    tiled = sum(jnp.where(lane == line + BS * n, 1.0, 0.0).astype(f32) for n in range(4))
    for mat, ref in enumerate((b_one, b_two)):
        for p in range(2):
            copies = jnp.dot(
                ref[p], tiled, precision=lax.Precision.HIGHEST, preferred_element_type=f32
            )
            brow[mat, p] = jnp.where(spread, copies, 0.0).sum(0, keepdims=True)

    def spectral(phase, a, half):
        held = got[phase, a].reshape(768, HC)
        return dot(lfs[half * HC : half * HC + HC, :], held)

    def unspectral(phase, a):
        for t in range(2):
            result = dot(lis[t * HC : t * HC + HC, :], fil[...]).astype(bf16)
            send[phase, a, 8 * t : 8 * t + 8] = result.reshape(8, 48, HC)
        got[phase, a, m] = send[phase, a, m]

    def product(left, mat):
        for n in range(3):
            tmp[:, 256 * n : 256 * n + 256] = dot(left, wd[mat, :, 256 * n : 256 * n + 256])

    def product_turned(left, mat):
        for n in range(3):
            tmp[:, 256 * n : 256 * n + 256] = lax.dot_general(
                left,
                wd[mat, 256 * n : 256 * n + 256, :],
                (((1,), (1,)), ((), ())),
                preferred_element_type=f32,
            )

    def rows_of(step):
        return pl.ds(pl.multiple_of(step * 32, 32), 32)

    def kept_rows(a, step):
        kk = lax.rem(step // 3, 2)
        q = pl.multiple_of(lax.rem(step, 3) * 32, 32)
        return keeps[2 * a + kk, pl.ds(q, 32), :].astype(f32)

    def forward(a, carry):
        wait_chunk(0, a, rsem)
        for p in range(2):
            spec[a, :, p * HC : p * HC + HC] = spectral(0, a, p).astype(bf16)
        product(spec[a], 0)

        def gelu_rows(step, carry):
            rows = rows_of(step)
            for p in range(2):
                part = slice(p * HC, p * HC + HC)
                value, tilt = gelu_both(tmp[rows, part] + brow[0, p])
                hid[a, rows, part] = value.astype(bf16)
                slope[a, rows, part] = tilt
            return carry

        lax.fori_loop(0, 12, gelu_rows, 0)
        product(hid[a], 1)

        def shrink_rows(step, carry):
            rows = rows_of(step)
            kept = kept_rows(a, step)
            for p in range(2):
                part = slice(p * HC, p * HC + HC)
                value = tmp[rows, part] + brow[1, p]
                tangent = jnp.tanh(value * (1.0 / shrink))
                filtered = (value - shrink * tangent) * kept
                fil[pl.ds(pl.multiple_of(p * HC + step * 32, 32), 32), :] = filtered.astype(bf16)
                kt[a, rows, part] = kept * (tangent * tangent)
            return carry

        lax.fori_loop(0, 12, shrink_rows, 0)
        unspectral(2, a)
        return carry

    lax.fori_loop(0, 3, forward, 0)
    send_chunk(2, 0)

    def add_grad(mat, left, right):
        for n in range(3):
            part = slice(256 * n, 256 * n + 256)
            gacc[mat, :, part] += lax.dot_general(
                left, right[:, part], (((0,), (0,)), ((), ())), preferred_element_type=f32
            )

    def backward(a, carry):
        wait_chunk(1, a, rsem)
        for p in range(2):
            tmp[:, p * HC : p * HC + HC] = spectral(1, a, p)

        def scaled_rows(mat, scale):
            def one(step, carry):
                rows = rows_of(step)
                for p in range(2):
                    part = slice(p * HC, p * HC + HC)
                    value = (tmp[rows, part] * scale[a, rows, part]).astype(bf16)
                    dtwo[rows, part] = value
                    bacc[mat, :, part] += value.astype(f32).reshape(4, 8, HC).sum(0)
                return carry

            lax.fori_loop(0, 12, one, 0)

        scaled_rows(1, kt)
        add_grad(1, hid[a], dtwo[...])
        product_turned(dtwo[...], 1)
        scaled_rows(0, slope)
        add_grad(0, spec[a], dtwo[...])
        product_turned(dtwo[...], 0)
        for p in range(2):
            fil[p * HC : p * HC + HC, :] = tmp[:, p * HC : p * HC + HC].astype(bf16)
        unspectral(3, a)
        return carry

    lax.fori_loop(0, 3, backward, 0)

    gp[:, :, 104:, :] = jnp.zeros((4, 4, 24, 128), f32)
    for mat in range(2):
        for n in range(4):
            start = BS * n // 128 * 128
            shift = BS * n - start
            window = 256 if shift + BS > 128 else 128
            up = slice(BS * n, BS * n + BS)
            down = slice(HC + BS * n, HC + BS * n + BS)
            left = slice(start, start + window)
            right = slice(HC + start, HC + start + window)

            def align(value):
                if shift:
                    value = pltpu.roll(value, window - shift, 1)
                return value[:, :128]

            gp[n, 2 * mat, :BS, :] = align(gacc[mat, up, left] + gacc[mat, down, right])
            gp[n, 2 * mat + 1, :BS, :] = align(gacc[mat, up, right] - gacc[mat, down, left])
            gp[n, 2 * mat, BS:104, :] = align(bacc[mat, :, left])
            gp[n, 2 * mat + 1, BS:104, :] = align(bacc[mat, :, right])

    def gather(count, source, target, device, at):
        def one(i, carry):
            pltpu.make_async_remote_copy(
                src_ref=source(i),
                dst_ref=target,
                send_sem=gsend.at[at],
                recv_sem=grecv.at[at],
                device_id=device(i),
                device_id_type=MESH,
            ).start()
            return carry

        lax.fori_loop(1, count + 1, one, 0)

    def settle(part, at):
        pltpu.make_async_copy(part, part, grecv.at[at]).wait()

    def depth_of(i):
        return lax.rem(depth + i, 8)

    def depth_device(i):
        at = depth_of(i)
        return (4 * (at // 4) + x, 2 * (y * 4 + lax.rem(at, 4)) + core)

    def depth_rows(i):
        return pl.ds(pl.multiple_of(16 * i, 16), 16)

    gather(
        15,
        lambda i: gp.at[lax.rem(y + i // 4, 4), lax.rem(x + lax.rem(i, 4), 4)],
        gr.at[4 * y + x],
        plane_device,
        0,
    )
    send_chunk(2, 1)
    gr[4 * y + x] = gp[y, x]
    settle(gr.at[pl.ds(0, 15)], 0)
    total = gr[0]
    for i in range(1, 16):
        total = total + gr[i]
    s_two[...] = total
    gather(7, lambda i: s_two.at[depth_rows(depth_of(i))], gz.at[depth], depth_device, 1)
    send_chunk(2, 2)
    gz[depth] = s_two[depth_rows(depth), :]
    settle(gz.at[pl.ds(0, 7)], 1)
    total = gz[0]
    for i in range(1, 8):
        total = total + gz[i]
    s_three[...] = total * (1.0 / (IMAGES * H))
    gather(7, lambda i: s_three, fin.at[depth], depth_device, 2)
    send_chunk(3, 0)
    fin[depth] = s_three[...]
    settle(fin.at[pl.ds(0, 7)], 2)
    fy[y, x] = fin[...].reshape(128, 128)
    gather(15, lambda i: fy.at[y, x], fy.at[y, x], plane_device, 3)
    send_chunk(3, 1)
    settle(gr.at[pl.ds(0, 15)], 3)
    gather(1, lambda i: fy, fc, lambda i: buddy, 4)
    send_chunk(3, 2)

    def leave(v):
        ref = (out_x, out_c)[v]

        def add(t, a):
            piece = got[2 + v, a, :, pl.ds(pl.multiple_of(16 * t, 16), 16), :]
            piece = piece.reshape(256, HC)
            for n in range(4):
                rows = slice(n * 192, n * 192 + 192)
                facc[t, rows, :] += dot(tts[1 - v, a, rows, :], piece)

        def begin(t, carry):
            for l in range(3):
                part = xs.at[v, t, l].reshape(WIDE, 128)[...]
                facc[t, :, 128 * l : 128 * l + 128] = part.astype(f32)
            return carry

        lax.fori_loop(0, 3, begin, 0)
        for a in range(2):
            wait_chunk(2 + v, a, rsem)

            def one(t, carry):
                add(t, a)
                return carry

            lax.fori_loop(0, 3, one, 0)
        wait_chunk(2 + v, 2, rsem)

        def away(j6):
            j = j6 - 3 * other
            for l in range(3):
                pltpu.make_async_remote_copy(
                    src_ref=row_slot(v, j6, l),
                    dst_ref=ref.at[j, :, :, tile(core, l)],
                    send_sem=osend.at[v, j],
                    recv_sem=orecv.at[v, j],
                    device_id=buddy,
                    device_id_type=MESH,
                ).start()

        def stay(j6):
            j = j6 - 3 * core
            for l in range(3):
                pltpu.make_async_copy(
                    row_slot(v, j6, l), ref.at[j, :, :, tile(core, l)], oloc.at[v, j]
                ).start()

        for step in range(3):
            t = step * core + (2 - step) * other
            add(t, 2)
            for jj in range(2):
                rows = slice(jj * 2 * W, jj * 2 * W + 2 * W)
                scale = row_valid(2 * t + jj)
                for l in range(3):
                    part = facc[t, rows, 128 * l : 128 * l + 128] * scale
                    xs.at[v, t, l].reshape(WIDE, 128)[rows, :] = part.astype(bf16)
            if step == 0:
                away(2 * t)
                away(2 * t + 1)
            elif step == 1:
                away(2 * t + other)
                stay(2 * t + core)
            else:
                stay(2 * t)
                stay(2 * t + 1)

    def left(v):
        ref = (out_x, out_c)[v]
        for j in range(3):
            gone, arrived = ref.at[j, :, :, mine], ref.at[j, :, :, theirs]
            pltpu.make_async_copy(gone, gone, oloc.at[v, j]).wait()
            pltpu.make_async_copy(arrived, arrived, orecv.at[v, j]).wait()
            pltpu.make_async_copy(gone, gone, osend.at[v, j]).wait()

    mine = pl.ds(pl.multiple_of(core * HC, 128), HC)
    theirs = pl.ds(pl.multiple_of(other * HC, 128), HC)
    leave(0)

    settle(fc, 4)
    for half, held in ((core, fy), (other, fc)):

        def one(n, carry):
            for mat, (weight, bias) in enumerate(((gw_one, gb_one), (gw_two, gb_two))):
                for p in range(2):
                    weight[p, 4 * half + n] = held[n, 2 * mat + p, :BS, :BS]
                    bias[p, 4 * half + n] = held[n, 2 * mat + p, BS:104, :BS].sum(0, keepdims=True)
            return carry

        lax.fori_loop(0, 4, one, 0)

    leave(1)

    def sent(i, carry):
        wait_chunk(i // 3, lax.rem(i, 3), ssem)
        return carry

    lax.fori_loop(0, 12, sent, 0)
    for v in range(2):
        for j in range(3):
            there = row_slots(v, 3 * core + j)
            pltpu.make_async_copy(there, there, xin_send.at[v, j]).wait()
    for at, part in (
        (0, gr.at[pl.ds(0, 15)]),
        (1, gz.at[pl.ds(0, 7)]),
        (2, fin.at[pl.ds(0, 7)]),
        (3, gr.at[pl.ds(0, 15)]),
        (4, fc),
    ):
        pltpu.make_async_copy(part, part, gsend.at[at]).wait()
    left(0)
    left(1)


def mix(x_wide, c_wide, kept, pad_rows, w_one, w_two, b_one, b_two):
    forward_lon, inverse_lon = longitude_parts()
    ahead = np.stack([to_spectrum_table(forward_lon), to_spectrum_table(inverse_lon)])
    lf, li = lat_tables()
    as_bf16 = lambda table: jnp.asarray(table.astype(jnp.bfloat16))
    tables = (as_bf16(ahead), as_bf16(ahead.transpose(0, 1, 3, 2)), as_bf16(lf), as_bf16(li))
    anywhere = pl.BlockSpec(memory_space=pl.ANY)
    vmem = pl.BlockSpec(memory_space=pltpu.VMEM)
    dma = pltpu.SemaphoreType.DMA
    return pl.pallas_call(
        kernel,
        out_shape=(
            jax.ShapeDtypeStruct(x_wide.shape, bf16),
            jax.ShapeDtypeStruct(c_wide.shape, bf16),
            jax.ShapeDtypeStruct((2, NB, BS, BS), f32),
            jax.ShapeDtypeStruct((2, NB, 1, BS), f32),
            jax.ShapeDtypeStruct((2, NB, BS, BS), f32),
            jax.ShapeDtypeStruct((2, NB, 1, BS), f32),
        ),
        in_specs=[anywhere] * 3
        + [pl.BlockSpec(memory_space=pltpu.SMEM)]
        + [anywhere] * 2
        + [vmem] * 2
        + [anywhere] * 4,
        out_specs=(anywhere, anywhere, vmem, vmem, vmem, vmem),
        scratch_shapes=[
            pltpu.VMEM((2, 3, 3, WIDE // 2, 2, 128), bf16),
            pltpu.VMEM((2, 3, 256, WIDE), bf16),
            pltpu.VMEM((2, 3, WIDE, 256), bf16),
            pltpu.VMEM((768, 768), bf16),
            pltpu.VMEM((768, 768), bf16),
            pltpu.VMEM((2, 2, NB, BS, BS), bf16),
            pltpu.VMEM((2, 768, 768), bf16),
            pltpu.VMEM((6, NB, H), jnp.int32),
            pltpu.VMEM((6, H, HC), bf16),
            pltpu.VMEM((2, 2, 1, HC), f32),
            pltpu.VMEM((4, 3, CHIPS, 48, HC), bf16),
            pltpu.VMEM((4, 3, CHIPS, 48, HC), bf16),
            pltpu.VMEM((3, WIDE, HC), f32),
            pltpu.VMEM((3, HC, 768), bf16),
            pltpu.VMEM((3, HC, 768), bf16),
            pltpu.VMEM((3, HC, 768), f32),
            pltpu.VMEM((3, HC, 768), f32),
            pltpu.VMEM((HC, 768), f32),
            pltpu.VMEM((768, HC), bf16),
            pltpu.VMEM((HC, 768), bf16),
            pltpu.VMEM((2, 768, 768), f32),
            pltpu.VMEM((2, 8, 768), f32),
            pltpu.VMEM((4, 4, 128, 128), f32),
            pltpu.VMEM((16, 128, 128), f32),
            pltpu.VMEM((128, 128), f32),
            pltpu.VMEM((8, 16, 128), f32),
            pltpu.VMEM((16, 128), f32),
            pltpu.VMEM((8, 16, 128), f32),
            pltpu.VMEM((4, 4, 128, 128), f32),
            pltpu.VMEM((4, 4, 128, 128), f32),
            dma((8,)),
            dma((2, 3)),
            dma((3, 3)),
            dma((3, 3)),
            dma((4, 3)),
            dma((4, 3)),
            dma((2, 3)),
            dma((2, 3)),
            dma((2, 3)),
            dma((5,)),
            dma((5,)),
        ],
        compiler_params=pltpu.CompilerParams(
            collective_id=0, has_side_effects=True, vmem_limit_bytes=61 * 2**20
        ),
    )(x_wide, c_wide, kept, pad_rows, w_one, w_two, b_one, b_two, *tables)


def on_device(inputs, cotangent, kept_modes, pad_rows, weight_one, bias_one, weight_two, bias_two):
    wide = lambda array: jnp.transpose(array, (1, 2, 0, 3))
    out_x, out_c, gw_one, gb_one, gw_two, gb_two = mix(
        wide(inputs),
        wide(cotangent),
        jnp.transpose(kept_modes, (2, 0, 1)),
        pad_rows,
        weight_one,
        weight_two,
        bias_one,
        bias_two,
    )
    narrow = lambda array: jnp.transpose(array, (2, 0, 1, 3))
    return narrow(out_x), narrow(out_c), gw_one, gb_one[:, :, 0], gw_two, gb_two[:, :, 0]


def solution(mesh):
    placed = (
        P("dp", "space", None, None),
        P("dp", "space", None, None),
        P(None, None, "space"),
        P(),
        P(),
        P(),
        P(),
        P(),
    )
    return jax.shard_map(
        on_device,
        mesh=mesh,
        in_specs=placed,
        out_specs=(P("dp", "space", None, None), P("dp", "space", None, None), P(), P(), P(), P()),
        check_vma=False,
    )
```

```python
import numpy as np

import jax
import jax.numpy as jnp
from jax import lax
from jax.experimental import pallas as pl
from jax.experimental.pallas import tpu as pltpu
from jax.sharding import PartitionSpec as P

shrink = 0.25
gelu_scale = 0.7978845608028654
gelu_cubic = 0.044715

H = 96
W = 180
WIDE = 768
C = 768
HC = 384
NB = 8
BS = 96
KWP = 96
CHIPS = 16
IMAGES = 16
MESH = pl.DeviceIdType.MESH
f32 = jnp.float32
bf16 = jnp.bfloat16


def longitude_parts():
    wavenum = np.arange(KWP)[:, None]
    column = np.arange(W)[None, :]
    phase = np.float32(2.0 * np.pi / W) * (wavenum * column % W).astype(np.float32)
    scaling = (wavenum < W // 2 + 1).astype(np.float32) / np.sqrt(np.float32(W))
    double = np.where((wavenum == 0) | (2 * wavenum == W), 1.0, 2.0).astype(np.float32)
    cosine = np.cos(phase) * scaling
    sine = np.sin(phase) * scaling
    forward = np.stack([cosine, -sine])
    inverse = np.stack([double * cosine, -double * sine])
    return forward, inverse


def latitude_parts(sign):
    row = np.arange(H)[:, None]
    column = np.arange(H)[None, :]
    phase = np.float32(2.0 * np.pi / H) * (row * column % H).astype(np.float32)
    scaling = np.float32(1.0) / np.sqrt(np.float32(H))
    cosine = np.cos(phase) * scaling
    sine = np.float32(sign) * np.sin(phase) * scaling
    upper = np.stack([cosine, sine], -1)
    lower = np.stack([-sine, cosine], -1)
    return np.stack([upper, lower], 0)


def to_spectrum_table(part):
    out = np.zeros((3, 16, 2, 2, 2, 2, 2, W, 2), np.float32)
    grouped = part.reshape(2, 16, 3, 2, W).transpose(2, 1, 0, 3, 4)
    for jj in range(2):
        for b in range(2):
            out[:, :, jj, b, :, :, jj, :, b] = grouped
    out = out.reshape(3, 256, 4 * W)
    return np.pad(out, ((0, 0), (0, 0), (0, WIDE - 4 * W)))


def lat_tables():
    forward = latitude_parts(1.0)
    inverse = latitude_parts(-1.0)
    ahead = np.zeros((2, 2, 2, H, 16, 6, 2, 2, 2), np.float32)
    back = np.zeros((16, 6, 2, 2, 2, 2, 2, 2, H), np.float32)
    split = forward.reshape(2, H, 16, 6, 2)
    isplit = inverse.reshape(2, 16, 6, H, 2)
    for b in range(2):
        for kk in range(2):
            ahead[:, b, kk, :, :, :, b, :, kk] = split
            back[:, :, b, :, kk, :, b, kk, :] = isplit.transpose(1, 2, 0, 4, 3)
    return ahead.reshape(768, 768), back.reshape(768, 768)


def gelu_both(value):
    tangent = jnp.tanh(gelu_scale * (value + gelu_cubic * value * value * value))
    inner = gelu_scale * (1.0 + 3.0 * gelu_cubic * value * value)
    half = 0.5 * (1.0 + tangent)
    return value * half, half + 0.5 * value * (1.0 - tangent * tangent) * inner


def dot(left, right):
    return jnp.dot(left, right, preferred_element_type=f32)


def kernel(
    x_in, c_in, kept_in, pad_in, w_one, w_two, b_one, b_two, ft_in, tt_in, lf_in, li_in,
    out_x, out_c, out_g,
    xs, fts, tts, lfs, lis, wraw, wd, kraw, keeps, brow,
    send, got, facc, spec, hid, slope, kt, tmp, fil, dtwo, gacc, bacc,
    gp, gr, s_two, gz, s_three, fin, fy,
    load_sem, xown, xin_send, xin_recv, ssem, rsem, oloc, osend, orecv, gsend, grecv, gloc,
):
    me = lax.axis_index("space")
    dp = lax.axis_index("dp")
    core = lax.rem(me, 2)
    other = 1 - core
    m = me // 2
    y = m // 4
    z = lax.rem(m, 4)
    zh = dp // 4
    x = lax.rem(dp, 4)
    depth = zh * 4 + z
    buddy = (dp, 2 * m + other)

    def tile(which, l):
        return pl.ds(pl.multiple_of(which * HC + l * 128, 128), 128)

    def row_slot(v, j6, l):
        return xs.at[v, j6 // 2, l, pl.ds(lax.rem(j6, 2) * W, W)]

    def row_slots(v, j6):
        return xs.at[v, j6 // 2, :, pl.ds(lax.rem(j6, 2) * W, W)]

    def load(src, dst, at):
        return pltpu.make_async_copy(src, dst, load_sem.at[at])

    def start_own(v, ref):
        for j in range(3):
            for l in range(3):
                pltpu.make_async_copy(
                    ref.at[j, :, :, tile(core, l)], row_slot(v, 3 * core + j, l), xown.at[v, j]
                ).start()

    kept_own = load(kept_in, kraw.at[pl.ds(3 * core, 3)], 0)
    tables = [
        load(ft_in.at[0], fts.at[0], 1),
        load(ft_in.at[1], fts.at[1], 2),
        load(lf_in, lfs, 3),
        load(w_one, wraw.at[0], 4),
        load(w_two, wraw.at[1], 5),
        load(li_in, lis, 6),
        load(tt_in, tts, 7),
    ]
    start_own(0, x_in)
    tables[0].start()
    start_own(1, c_in)
    for copy in tables[1:2] + [kept_own] + tables[2:]:
        copy.start()

    barrier = pltpu.get_barrier_semaphore()

    def greet(device):
        pl.semaphore_signal(barrier, inc=1, device_id=device, device_id_type=MESH)

    def greet_group(i, carry):
        greet((dp, 2 * lax.rem(m + i, CHIPS) + core))
        return carry

    def plane_device(i):
        row = lax.rem(y + i // 4, 4)
        return (zh * 4 + lax.rem(x + lax.rem(i, 4), 4), 2 * (row * 4 + z) + core)

    def greet_plane(i, carry):
        greet(plane_device(4 * (i // 3) + lax.rem(i, 3) + 1))
        return carry

    lax.fori_loop(1, CHIPS, greet_group, 0)
    greet(buddy)
    lax.fori_loop(0, 12, greet_plane, 0)
    for i in range(4):
        greet((lax.rem(dp + 4, 8), 2 * (y * 4 + lax.rem(z + i, 4)) + core))
    pl.semaphore_wait(barrier, 15 + 1 + 12 + 4)

    def swap(v, ref):
        for j in range(3):
            for l in range(3):
                pltpu.make_async_remote_copy(
                    src_ref=ref.at[j, :, :, tile(other, l)],
                    dst_ref=row_slot(v, 3 * core + j, l),
                    send_sem=xin_send.at[v, j],
                    recv_sem=xin_recv.at[v, j],
                    device_id=buddy,
                    device_id_type=MESH,
                ).start()

    kept_swap = pltpu.make_async_remote_copy(
        src_ref=kept_in,
        dst_ref=kraw.at[pl.ds(3 * core, 3)],
        send_sem=xin_send.at[2, 0],
        recv_sem=xin_recv.at[2, 0],
        device_id=buddy,
        device_id_type=MESH,
    )
    swap(0, x_in)
    swap(1, c_in)
    kept_swap.start()
    xs[:, :, :, 2 * W :] = jnp.zeros((2, 3, 3, WIDE // 2 - 2 * W, 2, 128), bf16)

    def row_valid(j6):
        return jnp.where(6 * m + j6 < H - pad_in[0], 1.0, 0.0).astype(f32)

    def field(v, t):
        return jnp.concatenate([xs.at[v, t, l].reshape(WIDE, 128)[...] for l in range(3)], axis=1)

    def send_chunk(phase, a, first=1, last=CHIPS, beside=None):
        def one(i, carry):
            peer = lax.rem(m + i, CHIPS)
            pltpu.make_async_remote_copy(
                src_ref=send.at[phase, a, peer],
                dst_ref=got.at[phase, a, m],
                send_sem=ssem.at[phase, a],
                recv_sem=rsem.at[phase, a],
                device_id=(dp, 2 * peer + core),
                device_id_type=MESH,
            ).start()
            if beside is not None:
                beside(i)
            return carry

        lax.fori_loop(first, last, one, 0)

    def wait_chunk(phase, a, sem):
        whole = got.at[phase, a, pl.ds(0, 15)]
        pltpu.make_async_copy(whole, whole, sem.at[phase, a]).wait()

    def to_spectrum(v):
        line = lax.broadcasted_iota(jnp.int32, (256, HC), 0)
        second = lax.rem(line // 8, 2) == 1

        def one(a, carry):
            for t in range(3):
                result = dot(fts[v, a], field(v, t))
                result = result * jnp.where(second, row_valid(2 * t + 1), row_valid(2 * t))
                send[v, a, :, 16 * t : 16 * t + 16, :] = result.astype(bf16).reshape(16, 16, HC)
            send_chunk(v, a)
            got[v, a, m] = send[v, a, m]
            return carry

        lax.fori_loop(0, 3, one, 0)

    for v in range(2):
        for j in range(3):
            here, there = row_slots(v, 3 * core + j), row_slots(v, 3 * other + j)
            pltpu.make_async_copy(here, here, xown.at[v, j]).wait()
            pltpu.make_async_copy(there, there, xin_recv.at[v, j]).wait()
        tables[v].wait()
        to_spectrum(v)

    gacc[...] = jnp.zeros_like(gacc)
    bacc[...] = jnp.zeros_like(bacc)
    for copy in [kept_own, kept_swap] + tables[2:]:
        copy.wait()
    lane = lax.broadcasted_iota(jnp.int32, (BS, HC), 1)
    line = lax.broadcasted_iota(jnp.int32, (BS, HC), 0)
    for mat in range(2):
        for n in range(4):
            select = jnp.where(lane == line + BS * n, 1.0, 0.0).astype(bf16)
            real = dot(wraw[mat, 0, 4 * core + n], select)
            imag = dot(wraw[mat, 1, 4 * core + n], select)
            up, down = BS * n, HC + BS * n
            wd[mat, up : up + BS, :HC] = real.astype(bf16)
            wd[mat, up : up + BS, HC:] = imag.astype(bf16)
            wd[mat, down : down + BS, :HC] = (-imag).astype(bf16)
            wd[mat, down : down + BS, HC:] = real.astype(bf16)

    lane = lax.broadcasted_iota(jnp.int32, (NB, HC), 1)
    block = lax.broadcasted_iota(jnp.int32, (NB, HC), 0) - 4 * core
    spread = (lane >= BS * block) & (lane < BS * block + BS)
    for slot in range(6):
        bits = kraw[slot].astype(f32).astype(bf16)
        wide = lax.dot_general(
            bits,
            jnp.where(spread, 1.0, 0.0).astype(bf16),
            (((0,), (0,)), ((), ())),
            preferred_element_type=f32,
        )
        real_mode = jnp.where(6 * m + slot < W // 2 + 1, 1.0, 0.0).astype(f32)
        keeps[slot] = (wide * real_mode).astype(bf16)
    lane = lax.broadcasted_iota(jnp.int32, (BS, HC), 1)
    tiled = sum(jnp.where(lane == line + BS * n, 1.0, 0.0).astype(f32) for n in range(4))
    for mat, ref in enumerate((b_one, b_two)):
        for p in range(2):
            copies = jnp.dot(
                ref[p], tiled, precision=lax.Precision.HIGHEST, preferred_element_type=f32
            )
            brow[mat, p] = jnp.where(spread, copies, 0.0).sum(0, keepdims=True)

    def spectral(phase, a, half):
        held = got[phase, a].reshape(768, HC)
        return dot(lfs[half * HC : half * HC + HC, :], held)

    def unspectral(phase, a):
        for t in range(2):
            result = dot(lis[t * HC : t * HC + HC, :], fil[...]).astype(bf16)
            send[phase, a, 8 * t : 8 * t + 8] = result.reshape(8, 48, HC)
        got[phase, a, m] = send[phase, a, m]

    def product(left, mat):
        for n in range(3):
            tmp[:, 256 * n : 256 * n + 256] = dot(left, wd[mat, :, 256 * n : 256 * n + 256])

    def product_turned(left, mat):
        for n in range(3):
            tmp[:, 256 * n : 256 * n + 256] = lax.dot_general(
                left,
                wd[mat, 256 * n : 256 * n + 256, :],
                (((1,), (1,)), ((), ())),
                preferred_element_type=f32,
            )

    def rows_of(step):
        return pl.ds(pl.multiple_of(step * 32, 32), 32)

    def kept_rows(a, step):
        kk = lax.rem(step // 3, 2)
        q = pl.multiple_of(lax.rem(step, 3) * 32, 32)
        return keeps[2 * a + kk, pl.ds(q, 32), :].astype(f32)

    def forward(a, carry):
        wait_chunk(0, a, rsem)
        for p in range(2):
            spec[a, :, p * HC : p * HC + HC] = spectral(0, a, p).astype(bf16)
        product(spec[a], 0)

        def gelu_rows(step, carry):
            rows = rows_of(step)
            for p in range(2):
                part = slice(p * HC, p * HC + HC)
                value, tilt = gelu_both(tmp[rows, part] + brow[0, p])
                hid[a, rows, part] = value.astype(bf16)
                slope[a, rows, part] = tilt
            return carry

        lax.fori_loop(0, 12, gelu_rows, 0)
        product(hid[a], 1)

        def shrink_rows(step, carry):
            rows = rows_of(step)
            kept = kept_rows(a, step)
            for p in range(2):
                part = slice(p * HC, p * HC + HC)
                value = tmp[rows, part] + brow[1, p]
                tangent = jnp.tanh(value * (1.0 / shrink))
                filtered = (value - shrink * tangent) * kept
                fil[pl.ds(pl.multiple_of(p * HC + step * 32, 32), 32), :] = filtered.astype(bf16)
                kt[a, rows, part] = kept * (tangent * tangent)
            return carry

        lax.fori_loop(0, 12, shrink_rows, 0)
        unspectral(2, a)
        return carry

    lax.fori_loop(0, 3, forward, 0)
    send_chunk(2, 0)
    send_chunk(2, 1, 1, 8)

    def add_grad(mat, left, right):
        for n in range(3):
            part = slice(256 * n, 256 * n + 256)
            gacc[mat, :, part] += lax.dot_general(
                left, right[:, part], (((0,), (0,)), ((), ())), preferred_element_type=f32
            )

    def backward(a, carry):
        wait_chunk(1, a, rsem)
        for p in range(2):
            tmp[:, p * HC : p * HC + HC] = spectral(1, a, p)

        def scaled_rows(mat, scale):
            def one(step, carry):
                rows = rows_of(step)
                for p in range(2):
                    part = slice(p * HC, p * HC + HC)
                    value = (tmp[rows, part] * scale[a, rows, part]).astype(bf16)
                    dtwo[rows, part] = value
                    bacc[mat, :, part] += value.astype(f32).reshape(4, 8, HC).sum(0)
                return carry

            lax.fori_loop(0, 12, one, 0)

        scaled_rows(1, kt)
        add_grad(1, hid[a], dtwo[...])
        product_turned(dtwo[...], 1)
        scaled_rows(0, slope)
        add_grad(0, spec[a], dtwo[...])
        product_turned(dtwo[...], 0)
        for p in range(2):
            fil[p * HC : p * HC + HC, :] = tmp[:, p * HC : p * HC + HC].astype(bf16)
        unspectral(3, a)
        return carry

    lax.fori_loop(0, 3, backward, 0)

    first_row = lax.broadcasted_iota(jnp.int32, (128 - BS, 128), 0) == 0
    for mat in range(2):
        for n in range(4):
            start = BS * n // 128 * 128
            shift = BS * n - start
            window = 256 if shift + BS > 128 else 128
            up = slice(BS * n, BS * n + BS)
            down = slice(HC + BS * n, HC + BS * n + BS)
            left = slice(start, start + window)
            right = slice(HC + start, HC + start + window)

            def align(value):
                if shift:
                    value = pltpu.roll(value, window - shift, 1)
                return value[:, :128]

            gp[n, 2 * mat, :BS, :] = align(gacc[mat, up, left] + gacc[mat, down, right]).astype(bf16)
            gp[n, 2 * mat + 1, :BS, :] = align(gacc[mat, up, right] - gacc[mat, down, left]).astype(bf16)
            for p, part in enumerate((left, right)):
                summed = align(bacc[mat, :, part]).sum(0, keepdims=True)
                gp[n, 2 * mat + p, BS:, :] = jnp.where(first_row, summed, 0.0).astype(bf16)

    def message(i, source, target, device, at):
        pltpu.make_async_remote_copy(
            src_ref=source,
            dst_ref=target,
            send_sem=gsend.at[at],
            recv_sem=grecv.at[at],
            device_id=device,
            device_id_type=MESH,
        ).start()

    def to_depths(source, target, at):
        def one(i, carry):
            message(i, source(i), target, depth_device(i), at)
            return carry

        lax.fori_loop(1, 8, one, 0)

    def settle(part, at):
        pltpu.make_async_copy(part, part, grecv.at[at]).wait()

    def depth_of(i):
        return lax.rem(depth + i, 8)

    def depth_device(i):
        at = depth_of(i)
        return (4 * (at // 4) + x, 2 * (y * 4 + lax.rem(at, 4)) + core)

    def depth_rows(i):
        return pl.ds(pl.multiple_of(16 * i, 16), 16)

    def to_owner(i):
        row, column = lax.rem(y + i // 4, 4), lax.rem(x + lax.rem(i, 4), 4)
        message(i, gp.at[row, column], gr.at[4 * y + x], plane_device(i), 0)

    def from_owner(i):
        message(i, fy.at[y, x], fy.at[y, x], plane_device(i), 3)

    lax.fori_loop(1, 8, lambda i, carry: (to_owner(i), carry)[1], 0)
    send_chunk(2, 1, 8, CHIPS, to_owner)
    send_chunk(2, 2)
    gr[4 * y + x] = gp[y, x]
    settle(gr.at[pl.ds(0, 15)], 0)
    total = gr[0].astype(f32)
    for i in range(1, 16):
        total = total + gr[i].astype(f32)
    s_two[...] = total
    to_depths(lambda i: s_two.at[depth_rows(depth_of(i))], gz.at[depth], 1)
    send_chunk(3, 0)
    gz[depth] = s_two[depth_rows(depth), :]
    settle(gz.at[pl.ds(0, 7)], 1)
    total = gz[0]
    for i in range(1, 8):
        total = total + gz[i]
    s_three[...] = total * (1.0 / (IMAGES * H))
    to_depths(lambda i: s_three, fin.at[depth], 2)
    send_chunk(3, 1)
    fin[depth] = s_three[...]
    settle(fin.at[pl.ds(0, 7)], 2)
    fy[y, x] = fin[...].reshape(128, 128).astype(bf16)
    send_chunk(3, 2, 1, CHIPS, from_owner)

    def leave(v):
        ref = (out_x, out_c)[v]

        def add(t, a):
            piece = got[2 + v, a, :, pl.ds(pl.multiple_of(16 * t, 16), 16), :]
            piece = piece.reshape(256, HC)
            for n in range(4):
                rows = slice(n * 192, n * 192 + 192)
                facc[t, rows, :] += dot(tts[1 - v, a, rows, :], piece)

        def begin(t, carry):
            for l in range(3):
                part = xs.at[v, t, l].reshape(WIDE, 128)[...]
                facc[t, :, 128 * l : 128 * l + 128] = part.astype(f32)
            return carry

        lax.fori_loop(0, 3, begin, 0)
        for a in range(2):
            wait_chunk(2 + v, a, rsem)

            def one(t, carry):
                add(t, a)
                return carry

            lax.fori_loop(0, 3, one, 0)
        wait_chunk(2 + v, 2, rsem)

        def away(j6):
            j = j6 - 3 * other
            for l in range(3):
                pltpu.make_async_remote_copy(
                    src_ref=row_slot(v, j6, l),
                    dst_ref=ref.at[j, :, :, tile(core, l)],
                    send_sem=osend.at[v, j],
                    recv_sem=orecv.at[v, j],
                    device_id=buddy,
                    device_id_type=MESH,
                ).start()

        def stay(j6):
            j = j6 - 3 * core
            for l in range(3):
                pltpu.make_async_copy(
                    row_slot(v, j6, l), ref.at[j, :, :, tile(core, l)], oloc.at[v, j]
                ).start()

        for step in range(3):
            t = step * core + (2 - step) * other
            add(t, 2)
            for jj in range(2):
                rows = slice(jj * 2 * W, jj * 2 * W + 2 * W)
                scale = row_valid(2 * t + jj)
                for l in range(3):
                    part = facc[t, rows, 128 * l : 128 * l + 128] * scale
                    xs.at[v, t, l].reshape(WIDE, 128)[rows, :] = part.astype(bf16)
            if step == 0:
                away(2 * t)
                away(2 * t + 1)
            elif step == 1:
                away(2 * t + other)
                stay(2 * t + core)
            else:
                stay(2 * t)
                stay(2 * t + 1)

    def left(v):
        ref = (out_x, out_c)[v]
        for j in range(3):
            gone, arrived = ref.at[j, :, :, mine], ref.at[j, :, :, theirs]
            pltpu.make_async_copy(gone, gone, oloc.at[v, j]).wait()
            pltpu.make_async_copy(arrived, arrived, orecv.at[v, j]).wait()
            pltpu.make_async_copy(gone, gone, osend.at[v, j]).wait()

    mine = pl.ds(pl.multiple_of(core * HC, 128), HC)
    theirs = pl.ds(pl.multiple_of(other * HC, 128), HC)
    leave(0)

    settle(gr.at[pl.ds(0, 15)], 3)
    fy_away = pltpu.make_async_remote_copy(
        src_ref=fy,
        dst_ref=out_g.at[core],
        send_sem=gsend.at[4],
        recv_sem=grecv.at[4],
        device_id=buddy,
        device_id_type=MESH,
    )
    fy_away.start()
    fy_stays = pltpu.make_async_copy(fy, out_g.at[core], gloc)
    fy_stays.start()

    leave(1)

    def sent(i, carry):
        wait_chunk(i // 3, lax.rem(i, 3), ssem)
        return carry

    lax.fori_loop(0, 12, sent, 0)
    for v in range(2):
        for j in range(3):
            there = row_slots(v, 3 * core + j)
            pltpu.make_async_copy(there, there, xin_send.at[v, j]).wait()
    for at, part in (
        (0, gr.at[pl.ds(0, 15)]),
        (1, gz.at[pl.ds(0, 7)]),
        (2, fin.at[pl.ds(0, 7)]),
        (3, gr.at[pl.ds(0, 15)]),
    ):
        pltpu.make_async_copy(part, part, gsend.at[at]).wait()
    left(0)
    left(1)
    fy_away.wait()
    fy_stays.wait()


def mix(x_wide, c_wide, kept, pad_rows, w_one, w_two, b_one, b_two):
    forward_lon, inverse_lon = longitude_parts()
    ahead = np.stack([to_spectrum_table(forward_lon), to_spectrum_table(inverse_lon)])
    lf, li = lat_tables()
    as_bf16 = lambda table: jnp.asarray(table.astype(jnp.bfloat16))
    tables = (as_bf16(ahead), as_bf16(ahead.transpose(0, 1, 3, 2)), as_bf16(lf), as_bf16(li))
    anywhere = pl.BlockSpec(memory_space=pl.ANY)
    vmem = pl.BlockSpec(memory_space=pltpu.VMEM)
    dma = pltpu.SemaphoreType.DMA
    return pl.pallas_call(
        kernel,
        out_shape=(
            jax.ShapeDtypeStruct(x_wide.shape, bf16),
            jax.ShapeDtypeStruct(c_wide.shape, bf16),
            jax.ShapeDtypeStruct((2, 4, 4, 128, 128), bf16),
        ),
        in_specs=[anywhere] * 3
        + [pl.BlockSpec(memory_space=pltpu.SMEM)]
        + [anywhere] * 2
        + [vmem] * 2
        + [anywhere] * 4,
        out_specs=(anywhere, anywhere, anywhere),
        scratch_shapes=[
            pltpu.VMEM((2, 3, 3, WIDE // 2, 2, 128), bf16),
            pltpu.VMEM((2, 3, 256, WIDE), bf16),
            pltpu.VMEM((2, 3, WIDE, 256), bf16),
            pltpu.VMEM((768, 768), bf16),
            pltpu.VMEM((768, 768), bf16),
            pltpu.VMEM((2, 2, NB, BS, BS), bf16),
            pltpu.VMEM((2, 768, 768), bf16),
            pltpu.VMEM((6, NB, H), jnp.int32),
            pltpu.VMEM((6, H, HC), bf16),
            pltpu.VMEM((2, 2, 1, HC), f32),
            pltpu.VMEM((4, 3, CHIPS, 48, HC), bf16),
            pltpu.VMEM((4, 3, CHIPS, 48, HC), bf16),
            pltpu.VMEM((3, WIDE, HC), f32),
            pltpu.VMEM((3, HC, 768), bf16),
            pltpu.VMEM((3, HC, 768), bf16),
            pltpu.VMEM((3, HC, 768), f32),
            pltpu.VMEM((3, HC, 768), f32),
            pltpu.VMEM((HC, 768), f32),
            pltpu.VMEM((768, HC), bf16),
            pltpu.VMEM((HC, 768), bf16),
            pltpu.VMEM((2, 768, 768), f32),
            pltpu.VMEM((2, 8, 768), f32),
            pltpu.VMEM((4, 4, 128, 128), bf16),
            pltpu.VMEM((16, 128, 128), bf16),
            pltpu.VMEM((128, 128), f32),
            pltpu.VMEM((8, 16, 128), f32),
            pltpu.VMEM((16, 128), f32),
            pltpu.VMEM((8, 16, 128), f32),
            pltpu.VMEM((4, 4, 128, 128), bf16),
            dma((8,)),
            dma((2, 3)),
            dma((3, 3)),
            dma((3, 3)),
            dma((4, 3)),
            dma((4, 3)),
            dma((2, 3)),
            dma((2, 3)),
            dma((2, 3)),
            dma((5,)),
            dma((5,)),
            dma,
        ],
        compiler_params=pltpu.CompilerParams(
            collective_id=0, has_side_effects=True, vmem_limit_bytes=61 * 2**20
        ),
    )(x_wide, c_wide, kept, pad_rows, w_one, w_two, b_one, b_two, *tables)


def finish(
    x_ref, c_ref, g_ref, out_x, out_c, gw_one, gb_one, gw_two, gb_two,
    held, parts, weights, biases, in_sem, out_sem, g_sem,
):
    loads, stores = [], []
    for v, (source, target) in enumerate(((x_ref, out_x), (c_ref, out_c))):
        for j in range(3):
            loads.append(pltpu.make_async_copy(source.at[j], held.at[v, j], in_sem.at[v, j]))
            stores.append(pltpu.make_async_copy(held.at[v, j], target.at[j], out_sem.at[v, j]))
    load_parts = pltpu.make_async_copy(g_ref, parts, g_sem.at[0])
    load_parts.start()
    for copy in loads:
        copy.start()
    load_parts.wait()
    for mat, (weight, bias) in enumerate(((gw_one, gb_one), (gw_two, gb_two))):
        for p in range(2):
            for n in range(NB):
                block = parts[n // 4, n % 4, 2 * mat + p].astype(f32)
                weights[mat, p, n] = block[:BS, :BS]
                biases[mat, p, n : n + 1, :] = block[BS : BS + 1, :BS]
        stores.append(pltpu.make_async_copy(weights.at[mat], weight, g_sem.at[1 + mat]))
        stores[-1].start()
        stores.append(pltpu.make_async_copy(biases.at[mat], bias, g_sem.at[3 + mat]))
        stores[-1].start()
    for load, store in zip(loads, stores):
        load.wait()
        store.start()
    for store in stores:
        store.wait()


def settle_outputs(out_x, out_c, out_g):
    anywhere = pl.BlockSpec(memory_space=pl.ANY)
    return pl.pallas_call(
        finish,
        out_shape=(
            jax.ShapeDtypeStruct(out_x.shape, bf16),
            jax.ShapeDtypeStruct(out_c.shape, bf16),
            jax.ShapeDtypeStruct((2, NB, BS, BS), f32),
            jax.ShapeDtypeStruct((2, NB, BS), f32),
            jax.ShapeDtypeStruct((2, NB, BS, BS), f32),
            jax.ShapeDtypeStruct((2, NB, BS), f32),
        ),
        in_specs=[anywhere] * 3,
        out_specs=(anywhere,) * 6,
        scratch_shapes=[
            pltpu.VMEM((2,) + out_x.shape, bf16),
            pltpu.VMEM(out_g.shape, bf16),
            pltpu.VMEM((2, 2, NB, BS, BS), f32),
            pltpu.VMEM((2, 2, NB, BS), f32),
            pltpu.SemaphoreType.DMA((2, 3)),
            pltpu.SemaphoreType.DMA((2, 3)),
            pltpu.SemaphoreType.DMA((5,)),
        ],
        compiler_params=pltpu.CompilerParams(vmem_limit_bytes=60 * 2**20),
    )(out_x, out_c, out_g)


def on_device(inputs, cotangent, kept_modes, pad_rows, weight_one, bias_one, weight_two, bias_two):
    wide = lambda array: jnp.transpose(array, (1, 2, 0, 3))
    out_x, out_c, gw_one, gb_one, gw_two, gb_two = settle_outputs(
        *mix(
            wide(inputs),
            wide(cotangent),
            jnp.transpose(kept_modes, (2, 0, 1)),
            pad_rows,
            weight_one,
            weight_two,
            bias_one,
            bias_two,
        )
    )
    narrow = lambda array: jnp.transpose(array, (2, 0, 1, 3))
    return narrow(out_x), narrow(out_c), gw_one, gb_one, gw_two, gb_two


def solution(mesh):
    placed = (
        P("dp", "space", None, None),
        P("dp", "space", None, None),
        P(None, None, "space"),
        P(),
        P(),
        P(),
        P(),
        P(),
    )
    return jax.shard_map(
        on_device,
        mesh=mesh,
        in_specs=placed,
        out_specs=(P("dp", "space", None, None), P("dp", "space", None, None), P(), P(), P(), P()),
        check_vma=False,
    )
```

```python
import numpy as np

import jax
import jax.numpy as jnp
from jax import lax
from jax.experimental import pallas as pl
from jax.experimental.pallas import tpu as pltpu
from jax.sharding import PartitionSpec as P

shrink = 0.25
gelu_scale = 0.7978845608028654
gelu_cubic = 0.044715

H = 96
W = 180
WP = 192
C = 768
HC = 384
NB = 8
BS = 96
KWP = 96
CHIPS = 16
DEVICES = 32
IMAGES = 16
MESH = pl.DeviceIdType.MESH
f32 = jnp.float32
bf16 = jnp.bfloat16


def longitude_parts():
    wavenum = np.arange(KWP)[:, None]
    column = np.arange(W)[None, :]
    phase = np.float32(2.0 * np.pi / W) * (wavenum * column % W).astype(np.float32)
    scaling = (wavenum < W // 2 + 1).astype(np.float32) / np.sqrt(np.float32(W))
    double = np.where((wavenum == 0) | (2 * wavenum == W), 1.0, 2.0).astype(np.float32)
    cosine = np.cos(phase) * scaling
    sine = np.sin(phase) * scaling
    forward = np.stack([cosine, -sine])
    inverse = np.stack([double * cosine, -double * sine])
    return forward, inverse


def latitude_parts(sign):
    row = np.arange(H)[:, None]
    column = np.arange(H)[None, :]
    phase = np.float32(2.0 * np.pi / H) * (row * column % H).astype(np.float32)
    scaling = np.float32(1.0) / np.sqrt(np.float32(H))
    cosine = np.cos(phase) * scaling
    sine = np.float32(sign) * np.sin(phase) * scaling
    upper = np.stack([cosine, sine], -1)
    lower = np.stack([-sine, cosine], -1)
    return np.stack([upper, lower], 0)


def to_spectrum_table(part):
    out = np.zeros((3, 16, 2, 2, 2, WP, 2), np.float32)
    grouped = part.reshape(2, 16, 3, 2, W).transpose(2, 1, 0, 3, 4)
    for b in range(2):
        out[:, :, b, :, :, :W, b] = grouped
    return out.reshape(3, 128, 2 * WP)


def lat_tables():
    forward = latitude_parts(1.0)
    inverse = latitude_parts(-1.0)
    ahead = np.zeros((2, 2, 2, H, 3, 16, 2, 2, 2, 2), np.float32)
    back = np.zeros((3, 16, 2, 2, 2, 2, 2, 2, 2, H), np.float32)
    split = forward.reshape(2, H, 16, 2, 3, 2).transpose(0, 1, 4, 2, 3, 5)
    isplit = inverse.reshape(2, 16, 2, 3, H, 2).transpose(3, 1, 2, 0, 5, 4)
    for b in range(2):
        for kk in range(2):
            ahead[:, b, kk, :, :, :, :, b, :, kk] = split
            back[:, :, :, b, :, kk, :, b, kk, :] = isplit
    return ahead.reshape(768, 768), back.reshape(768, 768)


def gelu_both(value):
    tangent = jnp.tanh(gelu_scale * (value + gelu_cubic * value * value * value))
    inner = gelu_scale * (1.0 + 3.0 * gelu_cubic * value * value)
    half = 0.5 * (1.0 + tangent)
    return value * half, half + 0.5 * value * (1.0 - tangent * tangent) * inner


def dot(left, right):
    return jnp.dot(left, right, preferred_element_type=f32)


def kernel(
    x_in, c_in, kept_in, pad_in, w_one, w_two, b_one, b_two, ft_in, tt_in, lf_in, li_in,
    out_x, out_c, out_g,
    xs, fts, tts, lfs, lis, wraw, wd, kraw, keeps, brow,
    send, got, back, home, facc, spec, hid, slope, kt, tmp, fil, dtwo, gacc, bacc,
    gp, gr, s_two, gz, s_three, fin, fy,
    load_sem, xin, kept_sem, ssem, rsem, oloc, gsend, grecv, gloc,
):
    me = lax.axis_index("space")
    dp = lax.axis_index("dp")
    core = lax.rem(me, 2)
    other = 1 - core
    m = me // 2
    y = m // 4
    z = lax.rem(m, 4)
    zh = dp // 4
    x = lax.rem(dp, 4)
    depth = zh * 4 + z
    buddy = (dp, 2 * m + other)

    def greet(device):
        pl.semaphore_signal(barrier, inc=1, device_id=device, device_id_type=MESH)

    def greet_group(i, carry):
        greet((dp, lax.rem(me + i, DEVICES)))
        return carry

    def plane_device(i):
        row = lax.rem(y + i // 4, 4)
        return (zh * 4 + lax.rem(x + lax.rem(i, 4), 4), 2 * (row * 4 + z) + core)

    def greet_plane(i, carry):
        greet(plane_device(4 * (i // 3) + lax.rem(i, 3) + 1))
        return carry

    def load(src, dst, at):
        return pltpu.make_async_copy(src, dst, load_sem.at[at])

    def start_field(v, ref):
        for l in range(6):
            pltpu.make_async_copy(
                ref.at[:, :, :, pl.ds(128 * l, 128)], xs.at[v, l, :, pl.ds(0, W)], xin.at[v]
            ).start()

    def wait_field(v):
        whole = xs.at[v, :, :, pl.ds(0, W)]
        pltpu.make_async_copy(whole, whole, xin.at[v]).wait()

    kept_own = load(kept_in, kraw.at[pl.ds(3 * core, 3)], 0)
    lon_table = load(ft_in, fts, 1)
    tables = [
        load(lf_in, lfs, 2),
        load(w_one, wraw.at[0], 3),
        load(w_two, wraw.at[1], 4),
        load(li_in, lis, 5),
        load(tt_in, tts, 6),
    ]
    start_field(0, x_in)
    lon_table.start()
    start_field(1, c_in)

    barrier = pltpu.get_barrier_semaphore()
    lax.fori_loop(1, DEVICES, greet_group, 0)
    lax.fori_loop(0, 12, greet_plane, 0)
    for i in range(4):
        greet((lax.rem(dp + 4, 8), 2 * (y * 4 + lax.rem(z + i, 4)) + core))

    for copy in [kept_own] + tables:
        copy.start()
    xs[:, :, :, W:] = jnp.zeros((2, 6, 3, WP - W, 2, 128), bf16)

    kept_swap = pltpu.make_async_remote_copy(
        src_ref=kept_in,
        dst_ref=kraw.at[pl.ds(3 * core, 3)],
        send_sem=kept_sem.at[0],
        recv_sem=kept_sem.at[1],
        device_id=buddy,
        device_id_type=MESH,
    )

    def row_valid(j):
        return jnp.where(3 * me + j < H - pad_in[0], 1.0, 0.0).astype(f32)

    def transform(v, a):
        for j in range(3):
            field = jnp.concatenate(
                [xs.at[v, l, j].reshape(2 * WP, 128)[...] for l in range(6)], axis=1
            )
            result = (dot(fts[v, a], field) * row_valid(j)).astype(bf16)
            for l in range(6):
                send.at[v, a, l, j].reshape(128, 128)[...] = result[:, 128 * l : 128 * l + 128]

    def message(source, target, device, send_at, recv_at):
        pltpu.make_async_remote_copy(
            src_ref=source,
            dst_ref=target,
            send_sem=send_at,
            recv_sem=recv_at,
            device_id=device,
            device_id_type=MESH,
        ).start()

    def send_chunk(v, a):
        def one(i, carry):
            peer = lax.rem(me + i, DEVICES)
            pm, pc = peer // 2, lax.rem(peer, 2)
            message(
                send.at[v, a, pl.ds(3 * pc, 3), :, pm],
                got.at[v, a, :, :, m, core],
                (dp, peer),
                ssem.at[v, a, lax.rem(pc + core, 2)],
                rsem.at[v, a],
            )
            return carry

        lax.fori_loop(1, DEVICES, one, 0)
        pltpu.make_async_copy(
            send.at[v, a, pl.ds(3 * core, 3), :, m], got.at[v, a, :, :, m, core], rsem.at[v, a]
        ).start()

    def send_back(v, a, first=1, last=DEVICES, beside=None):
        def one(i, carry):
            peer = lax.rem(me + i, DEVICES)
            pm, pc = peer // 2, lax.rem(peer, 2)
            message(
                back.at[v, a, :, :, pm, pc],
                home.at[v, a, pl.ds(3 * core, 3), :, m],
                (dp, peer),
                ssem.at[2 + v, a, lax.rem(pc + core, 2)],
                rsem.at[2 + v, a],
            )
            if beside is not None:
                beside(i)
            return carry

        lax.fori_loop(first, last, one, 0)
        if last == DEVICES:
            pltpu.make_async_copy(
                back.at[v, a, :, :, m, core],
                home.at[v, a, pl.ds(3 * core, 3), :, m],
                rsem.at[2 + v, a],
            ).start()

    def wait_chunk(v, a):
        pltpu.make_async_copy(got.at[v, a], got.at[v, a], rsem.at[v, a]).wait()

    def wait_home(v, a):
        pltpu.make_async_copy(home.at[v, a], home.at[v, a], rsem.at[2 + v, a]).wait()

    wait_field(0)
    lon_table.wait()
    transform(0, 0)
    pl.semaphore_wait(barrier, 31 + 12 + 4)
    send_chunk(0, 0)

    def transform_and_send(i, carry):
        transform(i // 3, lax.rem(i, 3))
        send_chunk(i // 3, lax.rem(i, 3))
        return carry

    lax.fori_loop(1, 3, transform_and_send, 0)
    wait_field(1)
    lax.fori_loop(3, 6, transform_and_send, 0)
    kept_swap.start()

    gacc[...] = jnp.zeros_like(gacc)
    bacc[...] = jnp.zeros_like(bacc)
    for copy in [kept_own, kept_swap] + tables:
        copy.wait()
    lane = lax.broadcasted_iota(jnp.int32, (BS, HC), 1)
    line = lax.broadcasted_iota(jnp.int32, (BS, HC), 0)
    for mat in range(2):
        for n in range(4):
            select = jnp.where(lane == line + BS * n, 1.0, 0.0).astype(bf16)
            real = dot(wraw[mat, 0, 4 * core + n], select)
            imag = dot(wraw[mat, 1, 4 * core + n], select)
            up, down = BS * n, HC + BS * n
            wd[mat, up : up + BS, :HC] = real.astype(bf16)
            wd[mat, up : up + BS, HC:] = imag.astype(bf16)
            wd[mat, down : down + BS, :HC] = (-imag).astype(bf16)
            wd[mat, down : down + BS, HC:] = real.astype(bf16)

    lane = lax.broadcasted_iota(jnp.int32, (NB, HC), 1)
    block = lax.broadcasted_iota(jnp.int32, (NB, HC), 0) - 4 * core
    spread = (lane >= BS * block) & (lane < BS * block + BS)
    for slot in range(6):
        bits = kraw[slot].astype(f32).astype(bf16)
        wide = lax.dot_general(
            bits,
            jnp.where(spread, 1.0, 0.0).astype(bf16),
            (((0,), (0,)), ((), ())),
            preferred_element_type=f32,
        )
        real_mode = jnp.where(6 * m + slot < W // 2 + 1, 1.0, 0.0).astype(f32)
        keeps[slot] = (wide * real_mode).astype(bf16)
    lane = lax.broadcasted_iota(jnp.int32, (BS, HC), 1)
    tiled = sum(jnp.where(lane == line + BS * n, 1.0, 0.0).astype(f32) for n in range(4))
    for mat, ref in enumerate((b_one, b_two)):
        for p in range(2):
            copies = jnp.dot(
                ref[p], tiled, precision=lax.Precision.HIGHEST, preferred_element_type=f32
            )
            brow[mat, p] = jnp.where(spread, copies, 0.0).sum(0, keepdims=True)

    def spectral(phase, a, half):
        held = jnp.concatenate([got.at[phase, a, l].reshape(768, 128)[...] for l in range(3)], axis=1)
        return dot(lfs[half * HC : half * HC + HC, :], held)

    def unspectral(v, a):
        for t in range(2):
            rows = slice(t * HC, t * HC + HC)
            result = dot(lis[rows, :], fil[...]).astype(bf16)
            for l in range(3):
                back.at[v, a, l].reshape(768, 128)[rows, :] = result[:, 128 * l : 128 * l + 128]

    def product(left, mat):
        for n in range(3):
            tmp[:, 256 * n : 256 * n + 256] = dot(left, wd[mat, :, 256 * n : 256 * n + 256])

    def product_turned(left, mat):
        for n in range(3):
            tmp[:, 256 * n : 256 * n + 256] = lax.dot_general(
                left,
                wd[mat, 256 * n : 256 * n + 256, :],
                (((1,), (1,)), ((), ())),
                preferred_element_type=f32,
            )

    def rows_of(step):
        return pl.ds(pl.multiple_of(step * 32, 32), 32)

    def kept_rows(a, step):
        kk = lax.rem(step // 3, 2)
        q = pl.multiple_of(lax.rem(step, 3) * 32, 32)
        return keeps[2 * a + kk, pl.ds(q, 32), :].astype(f32)

    def forward(a, carry):
        wait_chunk(0, a)
        for p in range(2):
            spec[a, :, p * HC : p * HC + HC] = spectral(0, a, p).astype(bf16)
        product(spec[a], 0)

        def gelu_rows(step, carry):
            rows = rows_of(step)
            for p in range(2):
                part = slice(p * HC, p * HC + HC)
                value, tilt = gelu_both(tmp[rows, part] + brow[0, p])
                hid[a, rows, part] = value.astype(bf16)
                slope[a, rows, part] = tilt
            return carry

        lax.fori_loop(0, 12, gelu_rows, 0)
        product(hid[a], 1)

        def shrink_rows(step, carry):
            rows = rows_of(step)
            kept = kept_rows(a, step)
            for p in range(2):
                part = slice(p * HC, p * HC + HC)
                value = tmp[rows, part] + brow[1, p]
                tangent = jnp.tanh(value * (1.0 / shrink))
                filtered = (value - shrink * tangent) * kept
                fil[pl.ds(pl.multiple_of(p * HC + step * 32, 32), 32), :] = filtered.astype(bf16)
                kt[a, rows, part] = kept * (tangent * tangent)
            return carry

        lax.fori_loop(0, 12, shrink_rows, 0)
        unspectral(0, a)
        return carry

    lax.fori_loop(0, 3, forward, 0)
    send_back(0, 0)
    send_back(0, 1, 1, 16)

    def add_grad(mat, left, right):
        for n in range(3):
            part = slice(256 * n, 256 * n + 256)
            gacc[mat, :, part] += lax.dot_general(
                left, right[:, part], (((0,), (0,)), ((), ())), preferred_element_type=f32
            )

    def backward(a, carry):
        wait_chunk(1, a)
        for p in range(2):
            tmp[:, p * HC : p * HC + HC] = spectral(1, a, p)

        def scaled_rows(mat, scale):
            def one(step, carry):
                rows = rows_of(step)
                for p in range(2):
                    part = slice(p * HC, p * HC + HC)
                    value = (tmp[rows, part] * scale[a, rows, part]).astype(bf16)
                    dtwo[rows, part] = value
                    bacc[mat, :, part] += value.astype(f32).reshape(4, 8, HC).sum(0)
                return carry

            lax.fori_loop(0, 12, one, 0)

        scaled_rows(1, kt)
        add_grad(1, hid[a], dtwo[...])
        product_turned(dtwo[...], 1)
        scaled_rows(0, slope)
        add_grad(0, spec[a], dtwo[...])
        product_turned(dtwo[...], 0)
        for p in range(2):
            fil[p * HC : p * HC + HC, :] = tmp[:, p * HC : p * HC + HC].astype(bf16)
        unspectral(1, a)
        return carry

    lax.fori_loop(0, 3, backward, 0)

    first_row = lax.broadcasted_iota(jnp.int32, (128 - BS, 128), 0) == 0
    for mat in range(2):
        for n in range(4):
            start = BS * n // 128 * 128
            shift = BS * n - start
            window = 256 if shift + BS > 128 else 128
            up = slice(BS * n, BS * n + BS)
            down = slice(HC + BS * n, HC + BS * n + BS)
            left = slice(start, start + window)
            right = slice(HC + start, HC + start + window)

            def align(value):
                if shift:
                    value = pltpu.roll(value, window - shift, 1)
                return value[:, :128]

            gp[n, 2 * mat, :BS, :] = align(gacc[mat, up, left] + gacc[mat, down, right]).astype(bf16)
            gp[n, 2 * mat + 1, :BS, :] = align(gacc[mat, up, right] - gacc[mat, down, left]).astype(bf16)
            for p, part in enumerate((left, right)):
                summed = align(bacc[mat, :, part]).sum(0, keepdims=True)
                gp[n, 2 * mat + p, BS:, :] = jnp.where(first_row, summed, 0.0).astype(bf16)

    def to_depths(source, target, at):
        def one(i, carry):
            message(source(i), target, depth_device(i), gsend.at[at], grecv.at[at])
            return carry

        lax.fori_loop(1, 8, one, 0)

    def settle(part, at):
        pltpu.make_async_copy(part, part, grecv.at[at]).wait()

    def depth_of(i):
        return lax.rem(depth + i, 8)

    def depth_device(i):
        at = depth_of(i)
        return (4 * (at // 4) + x, 2 * (y * 4 + lax.rem(at, 4)) + core)

    def depth_rows(i):
        return pl.ds(pl.multiple_of(16 * i, 16), 16)

    def to_owner(i):
        row, column = lax.rem(y + i // 4, 4), lax.rem(x + lax.rem(i, 4), 4)
        message(gp.at[row, column], gr.at[4 * y + x], plane_device(i), gsend.at[0], grecv.at[0])

    def from_owner(i):
        message(fy.at[y, x], fy.at[y, x], plane_device(i), gsend.at[3], grecv.at[3])

    send_back(0, 1, 16, 31, lambda i: to_owner(i - 15))
    send_back(0, 1, 31)
    send_back(0, 2)
    gr[4 * y + x] = gp[y, x]
    settle(gr.at[pl.ds(0, 15)], 0)
    total = gr[0].astype(f32)
    for i in range(1, 16):
        total = total + gr[i].astype(f32)
    s_two[...] = total.astype(bf16)
    to_depths(lambda i: s_two.at[depth_rows(depth_of(i))], gz.at[depth], 1)
    send_back(1, 0)
    gz[depth] = s_two[depth_rows(depth), :]
    settle(gz.at[pl.ds(0, 7)], 1)
    total = gz[0].astype(f32)
    for i in range(1, 8):
        total = total + gz[i].astype(f32)
    s_three[...] = (total * (1.0 / (IMAGES * H))).astype(bf16)
    to_depths(lambda i: s_three, fin.at[depth], 2)
    send_back(1, 1)
    fin[depth] = s_three[...]
    settle(fin.at[pl.ds(0, 7)], 2)
    fy[y, x] = fin[...].reshape(128, 128)
    send_back(1, 2, 1, 16, from_owner)
    send_back(1, 2, 16)

    def leave(v):
        ref = (out_x, out_c)[v]

        def part(j, a, n):
            piece = jnp.concatenate(
                [home.at[v, a, l, j].reshape(128, 128)[...] for l in range(6)], axis=1
            )
            rows = slice(n * WP, n * WP + WP)
            return dot(tts[1 - v, rows, 128 * a : 128 * a + 128], piece)

        def begin(j, carry):
            for l in range(6):
                part = xs.at[v, l, j].reshape(2 * WP, 128)[...]
                facc[j, :, 128 * l : 128 * l + 128] = part.astype(f32)
            return carry

        lax.fori_loop(0, 3, begin, 0)
        for a in range(2):
            wait_home(v, a)

            def one(j, carry):
                for n in range(2):
                    facc[j, n * WP : n * WP + WP, :] += part(j, a, n)
                return carry

            lax.fori_loop(0, 3, one, 0)
        wait_home(v, 2)

        def last(j, carry):
            scale = row_valid(j)
            for n in range(2):
                rows = slice(n * WP, n * WP + WP)
                result = ((facc[j, rows, :] + part(j, 2, n)) * scale).astype(bf16)
                for l in range(6):
                    xs.at[v, l, j].reshape(2 * WP, 128)[rows, :] = result[
                        :, 128 * l : 128 * l + 128
                    ]
            for l in range(6):
                pltpu.make_async_copy(
                    xs.at[v, l, j, pl.ds(0, W)],
                    ref.at[j, :, :, pl.ds(128 * l, 128)],
                    oloc.at[v],
                ).start()
            return carry

        lax.fori_loop(0, 3, last, 0)

    def left(v):
        whole = xs.at[v, :, :, pl.ds(0, W)]
        pltpu.make_async_copy(whole, whole, oloc.at[v]).wait()

    leave(0)

    settle(gr.at[pl.ds(0, 15)], 3)
    fy_away = pltpu.make_async_remote_copy(
        src_ref=fy,
        dst_ref=out_g.at[core],
        send_sem=gsend.at[4],
        recv_sem=grecv.at[4],
        device_id=buddy,
        device_id_type=MESH,
    )
    fy_away.start()
    fy_stays = pltpu.make_async_copy(fy, out_g.at[core], gloc)
    fy_stays.start()

    leave(1)

    def sent(i, carry):
        phase, a = i // 3, lax.rem(i, 3)
        for at, part in ((0, got.at[0, 0, :, :, pl.ds(0, 15), 0]), (1, got.at[0, 0, :, :, :, 0])):
            pltpu.make_async_copy(part, part, ssem.at[phase, a, at]).wait()
        return carry

    lax.fori_loop(0, 12, sent, 0)
    for at, part in (
        (0, gr.at[pl.ds(0, 15)]),
        (1, gz.at[pl.ds(0, 7)]),
        (2, fin.at[pl.ds(0, 7)]),
        (3, gr.at[pl.ds(0, 15)]),
    ):
        pltpu.make_async_copy(part, part, gsend.at[at]).wait()
    left(0)
    left(1)
    fy_away.wait()
    fy_stays.wait()


def mix(x_wide, c_wide, kept, pad_rows, w_one, w_two, b_one, b_two):
    forward_lon, inverse_lon = longitude_parts()
    ahead = np.stack([to_spectrum_table(forward_lon), to_spectrum_table(inverse_lon)])
    turned = ahead.transpose(0, 3, 1, 2).reshape(2, 2 * WP, 3 * 128)
    lf, li = lat_tables()
    as_bf16 = lambda table: jnp.asarray(table.astype(jnp.bfloat16))
    tables = (as_bf16(ahead), as_bf16(turned), as_bf16(lf), as_bf16(li))
    anywhere = pl.BlockSpec(memory_space=pl.ANY)
    vmem = pl.BlockSpec(memory_space=pltpu.VMEM)
    dma = pltpu.SemaphoreType.DMA
    return pl.pallas_call(
        kernel,
        out_shape=(
            jax.ShapeDtypeStruct(x_wide.shape, bf16),
            jax.ShapeDtypeStruct(c_wide.shape, bf16),
            jax.ShapeDtypeStruct((2, 4, 4, 128, 128), bf16),
        ),
        in_specs=[anywhere] * 3
        + [pl.BlockSpec(memory_space=pltpu.SMEM)]
        + [anywhere] * 2
        + [vmem] * 2
        + [anywhere] * 4,
        out_specs=(anywhere, anywhere, anywhere),
        scratch_shapes=[
            pltpu.VMEM((2, 6, 3, WP, 2, 128), bf16),
            pltpu.VMEM((2, 3, 128, 2 * WP), bf16),
            pltpu.VMEM((2, 2 * WP, 3 * 128), bf16),
            pltpu.VMEM((768, 768), bf16),
            pltpu.VMEM((768, 768), bf16),
            pltpu.VMEM((2, 2, NB, BS, BS), bf16),
            pltpu.VMEM((2, 768, 768), bf16),
            pltpu.VMEM((6, NB, H), jnp.int32),
            pltpu.VMEM((6, H, HC), bf16),
            pltpu.VMEM((2, 2, 1, HC), f32),
            pltpu.VMEM((2, 3, 6, 3, CHIPS, 4, 2, 128), bf16),
            pltpu.VMEM((2, 3, 3, 3, CHIPS, 2, 4, 2, 128), bf16),
            pltpu.VMEM((2, 3, 3, 3, CHIPS, 2, 4, 2, 128), bf16),
            pltpu.VMEM((2, 3, 6, 3, CHIPS, 4, 2, 128), bf16),
            pltpu.VMEM((3, 2 * WP, C), f32),
            pltpu.VMEM((3, HC, 768), bf16),
            pltpu.VMEM((3, HC, 768), bf16),
            pltpu.VMEM((3, HC, 768), f32),
            pltpu.VMEM((3, HC, 768), f32),
            pltpu.VMEM((HC, 768), f32),
            pltpu.VMEM((768, HC), bf16),
            pltpu.VMEM((HC, 768), bf16),
            pltpu.VMEM((2, 768, 768), f32),
            pltpu.VMEM((2, 8, 768), f32),
            pltpu.VMEM((4, 4, 128, 128), bf16),
            pltpu.VMEM((16, 128, 128), bf16),
            pltpu.VMEM((128, 128), bf16),
            pltpu.VMEM((8, 16, 128), bf16),
            pltpu.VMEM((16, 128), bf16),
            pltpu.VMEM((8, 16, 128), bf16),
            pltpu.VMEM((4, 4, 128, 128), bf16),
            dma((7,)),
            dma((2,)),
            dma((2,)),
            dma((4, 3, 2)),
            dma((4, 3)),
            dma((2,)),
            dma((5,)),
            dma((5,)),
            dma,
        ],
        compiler_params=pltpu.CompilerParams(
            collective_id=0, has_side_effects=True, vmem_limit_bytes=61 * 2**20
        ),
    )(x_wide, c_wide, kept, pad_rows, w_one, w_two, b_one, b_two, *tables)


def finish(
    x_ref, c_ref, g_ref, out_x, out_c, gw_one, gb_one, gw_two, gb_two,
    held, parts, weights, biases, in_sem, out_sem, g_sem,
):
    loads, stores = [], []
    load_parts = pltpu.make_async_copy(g_ref, parts, g_sem.at[0])
    for v, (source, target) in enumerate(((x_ref, out_x), (c_ref, out_c))):
        for j in range(3):
            loads.append(pltpu.make_async_copy(source.at[j], held.at[v, j], in_sem.at[v, j]))
            stores.append(pltpu.make_async_copy(held.at[v, j], target.at[j], out_sem.at[v, j]))
            loads[-1].start()
    load_parts.start()
    for load, store in zip(loads, stores):
        load.wait()
        store.start()
    load_parts.wait()
    for mat, (weight, bias) in enumerate(((gw_one, gb_one), (gw_two, gb_two))):
        for p in range(2):
            for n in range(NB):
                block = parts[n // 4, n % 4, 2 * mat + p].astype(f32)
                weights[mat, p, n] = block[:BS, :BS]
                biases[mat, p, n : n + 1, :] = block[BS : BS + 1, :BS]
        stores.append(pltpu.make_async_copy(weights.at[mat], weight, g_sem.at[1 + mat]))
        stores[-1].start()
        stores.append(pltpu.make_async_copy(biases.at[mat], bias, g_sem.at[3 + mat]))
        stores[-1].start()
    for store in stores:
        store.wait()


def settle_outputs(out_x, out_c, out_g):
    anywhere = pl.BlockSpec(memory_space=pl.ANY)
    return pl.pallas_call(
        finish,
        out_shape=(
            jax.ShapeDtypeStruct(out_x.shape, bf16),
            jax.ShapeDtypeStruct(out_c.shape, bf16),
            jax.ShapeDtypeStruct((2, NB, BS, BS), f32),
            jax.ShapeDtypeStruct((2, NB, BS), f32),
            jax.ShapeDtypeStruct((2, NB, BS, BS), f32),
            jax.ShapeDtypeStruct((2, NB, BS), f32),
        ),
        in_specs=[anywhere] * 3,
        out_specs=(anywhere,) * 6,
        scratch_shapes=[
            pltpu.VMEM((2,) + out_x.shape, bf16),
            pltpu.VMEM(out_g.shape, bf16),
            pltpu.VMEM((2, 2, NB, BS, BS), f32),
            pltpu.VMEM((2, 2, NB, BS), f32),
            pltpu.SemaphoreType.DMA((2, 3)),
            pltpu.SemaphoreType.DMA((2, 3)),
            pltpu.SemaphoreType.DMA((5,)),
        ],
        compiler_params=pltpu.CompilerParams(vmem_limit_bytes=60 * 2**20),
    )(out_x, out_c, out_g)


def on_device(inputs, cotangent, kept_modes, pad_rows, weight_one, bias_one, weight_two, bias_two):
    wide = lambda array: jnp.transpose(array, (1, 2, 0, 3))
    out_x, out_c, gw_one, gb_one, gw_two, gb_two = settle_outputs(
        *mix(
            wide(inputs),
            wide(cotangent),
            jnp.transpose(kept_modes, (2, 0, 1)),
            pad_rows,
            weight_one,
            weight_two,
            bias_one,
            bias_two,
        )
    )
    narrow = lambda array: jnp.transpose(array, (2, 0, 1, 3))
    return narrow(out_x), narrow(out_c), gw_one, gb_one, gw_two, gb_two


def solution(mesh):
    placed = (
        P("dp", "space", None, None),
        P("dp", "space", None, None),
        P(None, None, "space"),
        P(),
        P(),
        P(),
        P(),
        P(),
    )
    return jax.shard_map(
        on_device,
        mesh=mesh,
        in_specs=placed,
        out_specs=(P("dp", "space", None, None), P("dp", "space", None, None), P(), P(), P(), P()),
        check_vma=False,
    )
```

```python
import numpy as np

import jax
import jax.numpy as jnp
from jax import lax
from jax.experimental import pallas as pl
from jax.experimental.pallas import tpu as pltpu
from jax.sharding import PartitionSpec as P

shrink = 0.25
gelu_scale = 0.7978845608028654
gelu_cubic = 0.044715

H = 96
W = 180
WP = 192
C = 768
HC = 384
NB = 8
BS = 96
KWP = 96
CHIPS = 16
DEVICES = 32
IMAGES = 16
MESH = pl.DeviceIdType.MESH
f32 = jnp.float32
bf16 = jnp.bfloat16


def longitude_parts():
    wavenum = np.arange(KWP)[:, None]
    column = np.arange(W)[None, :]
    phase = np.float32(2.0 * np.pi / W) * (wavenum * column % W).astype(np.float32)
    scaling = (wavenum < W // 2 + 1).astype(np.float32) / np.sqrt(np.float32(W))
    double = np.where((wavenum == 0) | (2 * wavenum == W), 1.0, 2.0).astype(np.float32)
    cosine = np.cos(phase) * scaling
    sine = np.sin(phase) * scaling
    forward = np.stack([cosine, -sine])
    inverse = np.stack([double * cosine, -double * sine])
    return forward, inverse


def latitude_parts(sign):
    row = np.arange(H)[:, None]
    column = np.arange(H)[None, :]
    phase = np.float32(2.0 * np.pi / H) * (row * column % H).astype(np.float32)
    scaling = np.float32(1.0) / np.sqrt(np.float32(H))
    cosine = np.cos(phase) * scaling
    sine = np.float32(sign) * np.sin(phase) * scaling
    upper = np.stack([cosine, sine], -1)
    lower = np.stack([-sine, cosine], -1)
    return np.stack([upper, lower], 0)


def wavenumber_slots():
    slots = np.arange(KWP).reshape(16, 3, 2)
    slots[15, 1] = slots[12, 2]
    slots[12, 2] = slots[15, 2] = KWP - 1
    return slots


def to_spectrum_table(part):
    out = np.zeros((3, 16, 2, 2, 2, WP, 2), np.float32)
    grouped = part[:, wavenumber_slots()].transpose(2, 1, 0, 3, 4)
    for b in range(2):
        out[:, :, b, :, :, :W, b] = grouped
    return out.reshape(3, 128, 2 * WP)


def lat_tables():
    forward = latitude_parts(1.0)
    inverse = latitude_parts(-1.0)
    ahead = np.zeros((2, 2, 2, H, 3, 16, 2, 2, 2, 2), np.float32)
    back = np.zeros((3, 16, 2, 2, 2, 2, 2, 2, 2, H), np.float32)
    split = forward.reshape(2, H, 16, 2, 3, 2).transpose(0, 1, 4, 2, 3, 5)
    isplit = inverse.reshape(2, 16, 2, 3, H, 2).transpose(3, 1, 2, 0, 5, 4)
    for b in range(2):
        for kk in range(2):
            ahead[:, b, kk, :, :, :, :, b, :, kk] = split
            back[:, :, :, b, :, kk, :, b, kk, :] = isplit
    return ahead.reshape(768, 768), back.reshape(768, 768)


def gelu_both(value):
    tangent = jnp.tanh(gelu_scale * (value + gelu_cubic * value * value * value))
    inner = gelu_scale * (1.0 + 3.0 * gelu_cubic * value * value)
    half = 0.5 * (1.0 + tangent)
    return value * half, half + 0.5 * value * (1.0 - tangent * tangent) * inner


def dot(left, right):
    return jnp.dot(left, right, preferred_element_type=f32)


def kernel(
    x_in, c_in, kept_in, pad_in, w_one, w_two, b_one, b_two, ft_in, tt_in, lf_in, li_in,
    out_x, out_c, out_g,
    xs, fts, tts, lfs, lis, wraw, wd, kraw, keeps, brow,
    send, got, back, home, facc, spec, hid, slope, kt, tmp, fil, dtwo, gacc, bacc,
    gp, gr, s_two, gz, s_three, fin, fy,
    load_sem, xin, kept_sem, ssem, rsem, oloc, gsend, grecv, gloc,
):
    me = lax.axis_index("space")
    dp = lax.axis_index("dp")
    core = lax.rem(me, 2)
    other = 1 - core
    m = me // 2
    y = m // 4
    z = lax.rem(m, 4)
    zh = dp // 4
    x = lax.rem(dp, 4)
    depth = zh * 4 + z
    buddy = (dp, 2 * m + other)

    def greet(device):
        pl.semaphore_signal(barrier, inc=1, device_id=device, device_id_type=MESH)

    def greet_group(i, carry):
        greet((dp, lax.rem(me + i, DEVICES)))
        return carry

    def plane_device(i):
        row = lax.rem(y + i // 4, 4)
        return (zh * 4 + lax.rem(x + lax.rem(i, 4), 4), 2 * (row * 4 + z) + core)

    def greet_plane(i, carry):
        greet(plane_device(4 * (i // 3) + lax.rem(i, 3) + 1))
        return carry

    def load(src, dst, at):
        return pltpu.make_async_copy(src, dst, load_sem.at[at])

    def start_field(v, ref):
        for j in range(3):
            for l in range(6):
                pltpu.make_async_copy(
                    ref.at[j, :, :, pl.ds(128 * l, 128)], xs.at[v, l, j, pl.ds(0, W)], xin.at[v, j]
                ).start()

    def wait_field(v, j):
        whole = xs.at[v, :, j, pl.ds(0, W)]
        pltpu.make_async_copy(whole, whole, xin.at[v, j]).wait()

    kept_own = load(kept_in, kraw.at[pl.ds(3 * core, 3)], 0)
    lon_table = load(ft_in, fts, 1)
    tables = [
        load(lf_in, lfs, 2),
        load(w_one, wraw.at[0], 3),
        load(w_two, wraw.at[1], 4),
        load(li_in, lis, 5),
        load(tt_in, tts, 6),
    ]
    start_field(0, x_in)
    lon_table.start()
    start_field(1, c_in)

    barrier = pltpu.get_barrier_semaphore()
    lax.fori_loop(1, DEVICES, greet_group, 0)
    lax.fori_loop(0, 12, greet_plane, 0)
    for i in range(4):
        greet((lax.rem(dp + 4, 8), 2 * (y * 4 + lax.rem(z + i, 4)) + core))

    for copy in [kept_own] + tables:
        copy.start()
    xs[:, :, :, W:] = jnp.zeros((2, 6, 3, WP - W, 2, 128), bf16)
    for chip in (12, 15):
        home[:, 2, :, :, chip] = jnp.zeros((2, 6, 3, 4, 2, 128), bf16)

    kept_swap = pltpu.make_async_remote_copy(
        src_ref=kept_in,
        dst_ref=kraw.at[pl.ds(3 * core, 3)],
        send_sem=kept_sem.at[0],
        recv_sem=kept_sem.at[1],
        device_id=buddy,
        device_id_type=MESH,
    )

    def row_valid(j):
        return jnp.where(3 * me + j < H - pad_in[0], 1.0, 0.0).astype(f32)

    def transform(v, a, loading=False):
        for j in range(3):
            if loading:
                wait_field(v, j)
            field = jnp.concatenate(
                [xs.at[v, l, j].reshape(2 * WP, 128)[...] for l in range(6)], axis=1
            )
            result = (dot(fts[v, a], field) * row_valid(j)).astype(bf16)
            for l in range(6):
                send.at[v, a, l, j].reshape(128, 128)[...] = result[:, 128 * l : 128 * l + 128]

    def message(source, target, device, send_at, recv_at):
        pltpu.make_async_remote_copy(
            src_ref=source,
            dst_ref=target,
            send_sem=send_at,
            recv_sem=recv_at,
            device_id=device,
            device_id_type=MESH,
        ).start()

    def is_short(chip):
        return jnp.logical_or(chip == 12, chip == 15)

    def where_held(chip, a, body):
        if isinstance(a, int) and a != 2:
            body()
        else:
            pl.when(jnp.logical_or(a != 2, jnp.logical_not(is_short(chip))))(body)

    def send_chunk(v, a):
        def one(i, carry):
            peer = lax.rem(me + i, DEVICES)
            pm, pc = peer // 2, lax.rem(peer, 2)
            where_held(
                pm,
                a,
                lambda: message(
                    send.at[v, a, pl.ds(3 * pc, 3), :, pm],
                    got.at[v, a, :, :, m, core],
                    (dp, peer),
                    ssem.at[v, a, lax.rem(pc + core, 2)],
                    rsem.at[v, a],
                ),
            )
            return carry

        def own():
            pltpu.make_async_copy(
                send.at[v, a, pl.ds(3 * core, 3), :, m], got.at[v, a, :, :, m, core], rsem.at[v, a]
            ).start()

        lax.fori_loop(1, DEVICES, one, 0)
        where_held(m, a, own)

    def send_back(v, a, first=1, last=DEVICES, beside=None):
        def one(i, carry):
            peer = lax.rem(me + i, DEVICES)
            pm, pc = peer // 2, lax.rem(peer, 2)
            where_held(
                m,
                a,
                lambda: message(
                    back.at[v, a, :, :, pm, pc],
                    home.at[v, a, pl.ds(3 * core, 3), :, m],
                    (dp, peer),
                    ssem.at[2 + v, a, lax.rem(pc + core, 2)],
                    rsem.at[2 + v, a],
                ),
            )
            if beside is not None:
                beside(i)
            return carry

        def own():
            pltpu.make_async_copy(
                back.at[v, a, :, :, m, core],
                home.at[v, a, pl.ds(3 * core, 3), :, m],
                rsem.at[2 + v, a],
            ).start()

        lax.fori_loop(first, last, one, 0)
        if last == DEVICES:
            where_held(m, a, own)

    def wait_chunk(v, a):
        pltpu.make_async_copy(got.at[v, a], got.at[v, a], rsem.at[v, a]).wait()

    def wait_home(v, a):
        part = home.at[v, a] if a != 2 else home.at[v, a, :, :, pl.ds(0, 14)]
        pltpu.make_async_copy(part, part, rsem.at[2 + v, a]).wait()

    lon_table.wait()
    transform(0, 0, True)
    pl.semaphore_wait(barrier, 31 + 12 + 4)
    send_chunk(0, 0)

    def transform_and_send(i, carry):
        transform(i // 3, lax.rem(i, 3))
        send_chunk(i // 3, lax.rem(i, 3))
        return carry

    lax.fori_loop(1, 3, transform_and_send, 0)
    transform(1, 0, True)
    send_chunk(1, 0)
    lax.fori_loop(4, 6, transform_and_send, 0)
    kept_swap.start()

    def kept_moves(i):
        return pltpu.make_async_remote_copy(
            src_ref=kept_in.at[pl.ds(1, 2)],
            dst_ref=kraw.at[pl.ds(6, 2)],
            send_sem=kept_sem.at[2 + i],
            recv_sem=kept_sem.at[4],
            device_id=(dp, 30 + i),
            device_id_type=MESH,
        )

    @pl.when(me == 25)
    def _():
        for i in range(2):
            kept_moves(i).start()
        for i in range(2):
            kept_moves(i).wait_send()

    @pl.when(m == 15)
    def _():
        moved = kraw.at[pl.ds(6, 2)]
        pltpu.make_async_copy(moved, moved, kept_sem.at[4]).wait()


    gacc[...] = jnp.zeros_like(gacc)
    bacc[...] = jnp.zeros_like(bacc)
    for copy in [kept_own, kept_swap] + tables:
        copy.wait()
    lane = lax.broadcasted_iota(jnp.int32, (BS, HC), 1)
    line = lax.broadcasted_iota(jnp.int32, (BS, HC), 0)
    for mat in range(2):
        for n in range(4):
            select = jnp.where(lane == line + BS * n, 1.0, 0.0).astype(bf16)
            real = dot(wraw[mat, 0, 4 * core + n], select)
            imag = dot(wraw[mat, 1, 4 * core + n], select)
            up, down = BS * n, HC + BS * n
            wd[mat, up : up + BS, :HC] = real.astype(bf16)
            wd[mat, up : up + BS, HC:] = imag.astype(bf16)
            wd[mat, down : down + BS, :HC] = (-imag).astype(bf16)
            wd[mat, down : down + BS, HC:] = real.astype(bf16)

    lane = lax.broadcasted_iota(jnp.int32, (NB, HC), 1)
    block = lax.broadcasted_iota(jnp.int32, (NB, HC), 0) - 4 * core
    spread = (lane >= BS * block) & (lane < BS * block + BS)
    for slot in range(6):
        moved = 2 <= slot < 4
        bits = kraw[slot + 4 * (m // 15) if moved else slot].astype(f32).astype(bf16)
        wide = lax.dot_general(
            bits,
            jnp.where(spread, 1.0, 0.0).astype(bf16),
            (((0,), (0,)), ((), ())),
            preferred_element_type=f32,
        )
        if not moved:
            wide = wide * jnp.where(6 * m + slot < W // 2 + 1, 1.0, 0.0).astype(f32)
        keeps[slot] = wide.astype(bf16)
    lane = lax.broadcasted_iota(jnp.int32, (BS, HC), 1)
    tiled = sum(jnp.where(lane == line + BS * n, 1.0, 0.0).astype(f32) for n in range(4))
    for mat, ref in enumerate((b_one, b_two)):
        for p in range(2):
            copies = jnp.dot(
                ref[p], tiled, precision=lax.Precision.HIGHEST, preferred_element_type=f32
            )
            brow[mat, p] = jnp.where(spread, copies, 0.0).sum(0, keepdims=True)

    def spectral(phase, a, half):
        held = jnp.concatenate([got.at[phase, a, l].reshape(768, 128)[...] for l in range(3)], axis=1)
        return dot(lfs[half * HC : half * HC + HC, :], held)

    def unspectral(v, a):
        for t in range(2):
            rows = slice(t * HC, t * HC + HC)
            result = dot(lis[rows, :], fil[...]).astype(bf16)
            for l in range(3):
                back.at[v, a, l].reshape(768, 128)[rows, :] = result[:, 128 * l : 128 * l + 128]

    def product(left, mat):
        for n in range(3):
            tmp[:, 256 * n : 256 * n + 256] = dot(left, wd[mat, :, 256 * n : 256 * n + 256])

    def product_turned(left, mat):
        for n in range(3):
            tmp[:, 256 * n : 256 * n + 256] = lax.dot_general(
                left,
                wd[mat, 256 * n : 256 * n + 256, :],
                (((1,), (1,)), ((), ())),
                preferred_element_type=f32,
            )

    def rows_of(step):
        return pl.ds(pl.multiple_of(step * 32, 32), 32)

    def kept_rows(a, step):
        kk = lax.rem(step // 3, 2)
        q = pl.multiple_of(lax.rem(step, 3) * 32, 32)
        return keeps[2 * a + kk, pl.ds(q, 32), :].astype(f32)

    def forward(a, carry):
        where_held(m, a, lambda: forward_chunk(a))
        return carry

    def forward_chunk(a):
        wait_chunk(0, a)
        for p in range(2):
            spec[a, :, p * HC : p * HC + HC] = spectral(0, a, p).astype(bf16)
        product(spec[a], 0)

        def gelu_rows(step, carry):
            rows = rows_of(step)
            for p in range(2):
                part = slice(p * HC, p * HC + HC)
                value, tilt = gelu_both(tmp[rows, part] + brow[0, p])
                hid[a, rows, part] = value.astype(bf16)
                slope[a, rows, part] = tilt
            return carry

        lax.fori_loop(0, 12, gelu_rows, 0)
        product(hid[a], 1)

        def shrink_rows(step, carry):
            rows = rows_of(step)
            kept = kept_rows(a, step)
            for p in range(2):
                part = slice(p * HC, p * HC + HC)
                value = tmp[rows, part] + brow[1, p]
                tangent = jnp.tanh(value * (1.0 / shrink))
                filtered = (value - shrink * tangent) * kept
                fil[pl.ds(pl.multiple_of(p * HC + step * 32, 32), 32), :] = filtered.astype(bf16)
                kt[a, rows, part] = kept * (tangent * tangent)
            return carry

        lax.fori_loop(0, 12, shrink_rows, 0)
        unspectral(0, a)

    lax.fori_loop(0, 3, forward, 0)
    send_back(0, 0)
    send_back(0, 1, 1, 16)

    def add_grad(mat, left, right):
        for n in range(3):
            part = slice(256 * n, 256 * n + 256)
            gacc[mat, :, part] += lax.dot_general(
                left, right[:, part], (((0,), (0,)), ((), ())), preferred_element_type=f32
            )

    def backward(a, carry):
        where_held(m, a, lambda: backward_chunk(a))
        return carry

    def backward_chunk(a):
        wait_chunk(1, a)
        for p in range(2):
            tmp[:, p * HC : p * HC + HC] = spectral(1, a, p)

        def scaled_rows(mat, scale):
            def one(step, carry):
                rows = rows_of(step)
                for p in range(2):
                    part = slice(p * HC, p * HC + HC)
                    value = (tmp[rows, part] * scale[a, rows, part]).astype(bf16)
                    dtwo[rows, part] = value
                    bacc[mat, :, part] += value.astype(f32).reshape(4, 8, HC).sum(0)
                return carry

            lax.fori_loop(0, 12, one, 0)

        scaled_rows(1, kt)
        add_grad(1, hid[a], dtwo[...])
        product_turned(dtwo[...], 1)
        scaled_rows(0, slope)
        add_grad(0, spec[a], dtwo[...])
        product_turned(dtwo[...], 0)
        for p in range(2):
            fil[p * HC : p * HC + HC, :] = tmp[:, p * HC : p * HC + HC].astype(bf16)
        unspectral(1, a)

    lax.fori_loop(0, 3, backward, 0)

    first_row = lax.broadcasted_iota(jnp.int32, (128 - BS, 128), 0) == 0
    for mat in range(2):
        for n in range(4):
            start = BS * n // 128 * 128
            shift = BS * n - start
            window = 256 if shift + BS > 128 else 128
            up = slice(BS * n, BS * n + BS)
            down = slice(HC + BS * n, HC + BS * n + BS)
            left = slice(start, start + window)
            right = slice(HC + start, HC + start + window)

            def align(value):
                if shift:
                    value = pltpu.roll(value, window - shift, 1)
                return value[:, :128]

            gp[n, 2 * mat, :BS, :] = align(gacc[mat, up, left] + gacc[mat, down, right]).astype(bf16)
            gp[n, 2 * mat + 1, :BS, :] = align(gacc[mat, up, right] - gacc[mat, down, left]).astype(bf16)
            for p, part in enumerate((left, right)):
                summed = align(bacc[mat, :, part]).sum(0, keepdims=True)
                gp[n, 2 * mat + p, BS:, :] = jnp.where(first_row, summed, 0.0).astype(bf16)

    def to_depths(source, target, at):
        def one(i, carry):
            message(source(i), target, depth_device(i), gsend.at[at], grecv.at[at])
            return carry

        lax.fori_loop(1, 8, one, 0)

    def settle(part, at):
        pltpu.make_async_copy(part, part, grecv.at[at]).wait()

    def depth_of(i):
        return lax.rem(depth + i, 8)

    def depth_device(i):
        at = depth_of(i)
        return (4 * (at // 4) + x, 2 * (y * 4 + lax.rem(at, 4)) + core)

    def depth_rows(i):
        return pl.ds(pl.multiple_of(16 * i, 16), 16)

    def to_owner(i):
        row, column = lax.rem(y + i // 4, 4), lax.rem(x + lax.rem(i, 4), 4)
        message(gp.at[row, column], gr.at[4 * y + x], plane_device(i), gsend.at[0], grecv.at[0])

    def from_owner(i):
        message(fy.at[y, x], fy.at[y, x], plane_device(i), gsend.at[3], grecv.at[3])

    send_back(0, 1, 16, 31, lambda i: to_owner(i - 15))
    send_back(0, 1, 31)
    send_back(0, 2)
    gr[4 * y + x] = gp[y, x]
    settle(gr.at[pl.ds(0, 15)], 0)
    total = gr[0].astype(f32)
    for i in range(1, 16):
        total = total + gr[i].astype(f32)
    s_two[...] = total.astype(bf16)
    to_depths(lambda i: s_two.at[depth_rows(depth_of(i))], gz.at[depth], 1)
    send_back(1, 0)
    gz[depth] = s_two[depth_rows(depth), :]
    settle(gz.at[pl.ds(0, 7)], 1)
    total = gz[0].astype(f32)
    for i in range(1, 8):
        total = total + gz[i].astype(f32)
    s_three[...] = (total * (1.0 / (IMAGES * H))).astype(bf16)
    to_depths(lambda i: s_three, fin.at[depth], 2)
    send_back(1, 1)
    fin[depth] = s_three[...]
    settle(fin.at[pl.ds(0, 7)], 2)
    fy[y, x] = fin[...].reshape(128, 128)
    send_back(1, 2, 1, 16, from_owner)
    send_back(1, 2, 16)

    def leave(v):
        ref = (out_x, out_c)[v]

        def part(j, a, n):
            piece = jnp.concatenate(
                [home.at[v, a, l, j].reshape(128, 128)[...] for l in range(6)], axis=1
            )
            rows = slice(n * WP, n * WP + WP)
            return dot(tts[1 - v, rows, 128 * a : 128 * a + 128], piece)

        def begin(j, carry):
            for l in range(6):
                part = xs.at[v, l, j].reshape(2 * WP, 128)[...]
                facc[j, :, 128 * l : 128 * l + 128] = part.astype(f32)
            return carry

        lax.fori_loop(0, 3, begin, 0)
        for a in range(2):
            wait_home(v, a)

            def one(j, carry):
                for n in range(2):
                    facc[j, n * WP : n * WP + WP, :] += part(j, a, n)
                return carry

            lax.fori_loop(0, 3, one, 0)
        wait_home(v, 2)

        def last(j, carry):
            scale = row_valid(j)
            for n in range(2):
                rows = slice(n * WP, n * WP + WP)
                result = ((facc[j, rows, :] + part(j, 2, n)) * scale).astype(bf16)
                for l in range(6):
                    xs.at[v, l, j].reshape(2 * WP, 128)[rows, :] = result[
                        :, 128 * l : 128 * l + 128
                    ]
            for l in range(6):
                pltpu.make_async_copy(
                    xs.at[v, l, j, pl.ds(0, W)],
                    ref.at[j, :, :, pl.ds(128 * l, 128)],
                    oloc.at[v],
                ).start()
            return carry

        lax.fori_loop(0, 3, last, 0)

    def left(v):
        whole = xs.at[v, :, :, pl.ds(0, W)]
        pltpu.make_async_copy(whole, whole, oloc.at[v]).wait()

    leave(0)

    settle(gr.at[pl.ds(0, 15)], 3)
    fy_away = pltpu.make_async_remote_copy(
        src_ref=fy,
        dst_ref=out_g.at[core],
        send_sem=gsend.at[4],
        recv_sem=grecv.at[4],
        device_id=buddy,
        device_id_type=MESH,
    )
    fy_away.start()
    fy_stays = pltpu.make_async_copy(fy, out_g.at[core], gloc)
    fy_stays.start()

    leave(1)

    def sent(phase, a, counts):
        for at in range(2):
            part = got.at[0, 0, :, :, pl.ds(0, counts[at]), 0]
            pltpu.make_async_copy(part, part, ssem.at[phase, a, at]).wait()

    for phase in range(4):
        for a in range(2):
            sent(phase, a, (15, 16))

    @pl.when(is_short(m))
    def _():
        for phase in range(2):
            sent(phase, 2, (14, 14))

    @pl.when(jnp.logical_not(is_short(m)))
    def _():
        for phase in range(2):
            sent(phase, 2, (13, 14))
            sent(2 + phase, 2, (15, 16))

    for at, part in (
        (0, gr.at[pl.ds(0, 15)]),
        (1, gz.at[pl.ds(0, 7)]),
        (2, fin.at[pl.ds(0, 7)]),
        (3, gr.at[pl.ds(0, 15)]),
    ):
        pltpu.make_async_copy(part, part, gsend.at[at]).wait()
    left(0)
    left(1)
    fy_away.wait()
    fy_stays.wait()


def mix(x_wide, c_wide, kept, pad_rows, w_one, w_two, b_one, b_two):
    forward_lon, inverse_lon = longitude_parts()
    ahead = np.stack([to_spectrum_table(forward_lon), to_spectrum_table(inverse_lon)])
    turned = ahead.transpose(0, 3, 1, 2).reshape(2, 2 * WP, 3 * 128)
    lf, li = lat_tables()
    as_bf16 = lambda table: jnp.asarray(table.astype(jnp.bfloat16))
    tables = (as_bf16(ahead), as_bf16(turned), as_bf16(lf), as_bf16(li))
    anywhere = pl.BlockSpec(memory_space=pl.ANY)
    vmem = pl.BlockSpec(memory_space=pltpu.VMEM)
    dma = pltpu.SemaphoreType.DMA
    return pl.pallas_call(
        kernel,
        out_shape=(
            jax.ShapeDtypeStruct(x_wide.shape, bf16),
            jax.ShapeDtypeStruct(c_wide.shape, bf16),
            jax.ShapeDtypeStruct((2, 4, 4, 128, 128), bf16),
        ),
        in_specs=[anywhere] * 3
        + [pl.BlockSpec(memory_space=pltpu.SMEM)]
        + [anywhere] * 2
        + [vmem] * 2
        + [anywhere] * 4,
        out_specs=(anywhere, anywhere, anywhere),
        scratch_shapes=[
            pltpu.VMEM((2, 6, 3, WP, 2, 128), bf16),
            pltpu.VMEM((2, 3, 128, 2 * WP), bf16),
            pltpu.VMEM((2, 2 * WP, 3 * 128), bf16),
            pltpu.VMEM((768, 768), bf16),
            pltpu.VMEM((768, 768), bf16),
            pltpu.VMEM((2, 2, NB, BS, BS), bf16),
            pltpu.VMEM((2, 768, 768), bf16),
            pltpu.VMEM((8, NB, H), jnp.int32),
            pltpu.VMEM((6, H, HC), bf16),
            pltpu.VMEM((2, 2, 1, HC), f32),
            pltpu.VMEM((2, 3, 6, 3, CHIPS, 4, 2, 128), bf16),
            pltpu.VMEM((2, 3, 3, 3, CHIPS, 2, 4, 2, 128), bf16),
            pltpu.VMEM((2, 3, 3, 3, CHIPS, 2, 4, 2, 128), bf16),
            pltpu.VMEM((2, 3, 6, 3, CHIPS, 4, 2, 128), bf16),
            pltpu.VMEM((3, 2 * WP, C), f32),
            pltpu.VMEM((3, HC, 768), bf16),
            pltpu.VMEM((3, HC, 768), bf16),
            pltpu.VMEM((3, HC, 768), f32),
            pltpu.VMEM((3, HC, 768), f32),
            pltpu.VMEM((HC, 768), f32),
            pltpu.VMEM((768, HC), bf16),
            pltpu.VMEM((HC, 768), bf16),
            pltpu.VMEM((2, 768, 768), f32),
            pltpu.VMEM((2, 8, 768), f32),
            pltpu.VMEM((4, 4, 128, 128), bf16),
            pltpu.VMEM((16, 128, 128), bf16),
            pltpu.VMEM((128, 128), bf16),
            pltpu.VMEM((8, 16, 128), bf16),
            pltpu.VMEM((16, 128), bf16),
            pltpu.VMEM((8, 16, 128), bf16),
            pltpu.VMEM((4, 4, 128, 128), bf16),
            dma((7,)),
            dma((2, 3)),
            dma((5,)),
            dma((4, 3, 2)),
            dma((4, 3)),
            dma((2,)),
            dma((5,)),
            dma((5,)),
            dma,
        ],
        compiler_params=pltpu.CompilerParams(
            collective_id=0, has_side_effects=True, vmem_limit_bytes=61 * 2**20
        ),
    )(x_wide, c_wide, kept, pad_rows, w_one, w_two, b_one, b_two, *tables)


def finish(
    x_ref, c_ref, g_ref, out_x, out_c, gw_one, gb_one, gw_two, gb_two,
    held, parts, weights, biases, in_sem, out_sem, g_sem,
):
    loads, stores = [], []
    load_parts = pltpu.make_async_copy(g_ref, parts, g_sem.at[0])
    for v, (source, target) in enumerate(((x_ref, out_x), (c_ref, out_c))):
        for j in range(3):
            loads.append(pltpu.make_async_copy(source.at[j], held.at[v, j], in_sem.at[v, j]))
            stores.append(pltpu.make_async_copy(held.at[v, j], target.at[j], out_sem.at[v, j]))
            loads[-1].start()
    load_parts.start()
    for load, store in zip(loads, stores):
        load.wait()
        store.start()
    load_parts.wait()
    for mat, (weight, bias) in enumerate(((gw_one, gb_one), (gw_two, gb_two))):
        for p in range(2):
            for n in range(NB):
                block = parts[n // 4, n % 4, 2 * mat + p].astype(f32)
                weights[mat, p, n] = block[:BS, :BS]
                biases[mat, p, n : n + 1, :] = block[BS : BS + 1, :BS]
        stores.append(pltpu.make_async_copy(weights.at[mat], weight, g_sem.at[1 + mat]))
        stores[-1].start()
        stores.append(pltpu.make_async_copy(biases.at[mat], bias, g_sem.at[3 + mat]))
        stores[-1].start()
    for store in stores:
        store.wait()


def settle_outputs(out_x, out_c, out_g):
    anywhere = pl.BlockSpec(memory_space=pl.ANY)
    return pl.pallas_call(
        finish,
        out_shape=(
            jax.ShapeDtypeStruct(out_x.shape, bf16),
            jax.ShapeDtypeStruct(out_c.shape, bf16),
            jax.ShapeDtypeStruct((2, NB, BS, BS), f32),
            jax.ShapeDtypeStruct((2, NB, BS), f32),
            jax.ShapeDtypeStruct((2, NB, BS, BS), f32),
            jax.ShapeDtypeStruct((2, NB, BS), f32),
        ),
        in_specs=[anywhere] * 3,
        out_specs=(anywhere,) * 6,
        scratch_shapes=[
            pltpu.VMEM((2,) + out_x.shape, bf16),
            pltpu.VMEM(out_g.shape, bf16),
            pltpu.VMEM((2, 2, NB, BS, BS), f32),
            pltpu.VMEM((2, 2, NB, BS), f32),
            pltpu.SemaphoreType.DMA((2, 3)),
            pltpu.SemaphoreType.DMA((2, 3)),
            pltpu.SemaphoreType.DMA((5,)),
        ],
        compiler_params=pltpu.CompilerParams(vmem_limit_bytes=60 * 2**20),
    )(out_x, out_c, out_g)


def on_device(inputs, cotangent, kept_modes, pad_rows, weight_one, bias_one, weight_two, bias_two):
    wide = lambda array: jnp.transpose(array, (1, 2, 0, 3))
    out_x, out_c, gw_one, gb_one, gw_two, gb_two = settle_outputs(
        *mix(
            wide(inputs),
            wide(cotangent),
            jnp.transpose(kept_modes, (2, 0, 1)),
            pad_rows,
            weight_one,
            weight_two,
            bias_one,
            bias_two,
        )
    )
    narrow = lambda array: jnp.transpose(array, (2, 0, 1, 3))
    return narrow(out_x), narrow(out_c), gw_one, gb_one, gw_two, gb_two


def solution(mesh):
    placed = (
        P("dp", "space", None, None),
        P("dp", "space", None, None),
        P(None, None, "space"),
        P(),
        P(),
        P(),
        P(),
        P(),
    )
    return jax.shard_map(
        on_device,
        mesh=mesh,
        in_specs=placed,
        out_specs=(P("dp", "space", None, None), P("dp", "space", None, None), P(), P(), P(), P()),
        check_vma=False,
    )
```

```python
import numpy as np

import jax
import jax.numpy as jnp
from jax import lax
from jax.experimental import pallas as pl
from jax.experimental.pallas import tpu as pltpu
from jax.sharding import PartitionSpec as P

shrink = 0.25
gelu_scale = 0.7978845608028654
gelu_cubic = 0.044715

H = 96
W = 180
WP = 192
C = 768
HC = 384
NB = 8
BS = 96
KWP = 96
CHIPS = 16
DEVICES = 32
IMAGES = 16
MESH = pl.DeviceIdType.MESH
f32 = jnp.float32
bf16 = jnp.bfloat16


def longitude_parts():
    wavenum = np.arange(KWP)[:, None]
    column = np.arange(W)[None, :]
    phase = np.float32(2.0 * np.pi / W) * (wavenum * column % W).astype(np.float32)
    scaling = (wavenum < W // 2 + 1).astype(np.float32) / np.sqrt(np.float32(W))
    double = np.where((wavenum == 0) | (2 * wavenum == W), 1.0, 2.0).astype(np.float32)
    cosine = np.cos(phase) * scaling
    sine = np.sin(phase) * scaling
    forward = np.stack([cosine, -sine])
    inverse = np.stack([double * cosine, -double * sine])
    return forward, inverse


def latitude_parts(sign):
    row = np.arange(H)[:, None]
    column = np.arange(H)[None, :]
    phase = np.float32(2.0 * np.pi / H) * (row * column % H).astype(np.float32)
    scaling = np.float32(1.0) / np.sqrt(np.float32(H))
    cosine = np.cos(phase) * scaling
    sine = np.float32(sign) * np.sin(phase) * scaling
    upper = np.stack([cosine, sine], -1)
    lower = np.stack([-sine, cosine], -1)
    return np.stack([upper, lower], 0)


def wavenumber_slots():
    slots = np.arange(KWP).reshape(16, 3, 2)
    slots[15, 1] = slots[12, 2]
    slots[12, 2] = slots[15, 2] = KWP - 1
    return slots


def to_spectrum_table(part):
    out = np.zeros((3, 16, 2, 2, 2, WP, 2), np.float32)
    grouped = part[:, wavenumber_slots()].transpose(2, 1, 0, 3, 4)
    for b in range(2):
        out[:, :, b, :, :, :W, b] = grouped
    return out.reshape(3, 128, 2 * WP)


def lat_tables():
    forward = latitude_parts(1.0)
    inverse = latitude_parts(-1.0)
    ahead = np.zeros((2, 2, 2, H, 3, 16, 2, 2, 2, 2), np.float32)
    back = np.zeros((3, 16, 2, 2, 2, 2, 2, 2, 2, H), np.float32)
    split = forward.reshape(2, H, 16, 2, 3, 2).transpose(0, 1, 4, 2, 3, 5)
    isplit = inverse.reshape(2, 16, 2, 3, H, 2).transpose(3, 1, 2, 0, 5, 4)
    for b in range(2):
        for kk in range(2):
            ahead[:, b, kk, :, :, :, :, b, :, kk] = split
            back[:, :, :, b, :, kk, :, b, kk, :] = isplit
    return ahead.reshape(768, 768), back.reshape(768, 768)


def gelu_both(value):
    tangent = jnp.tanh(gelu_scale * (value + gelu_cubic * value * value * value))
    inner = gelu_scale * (1.0 + 3.0 * gelu_cubic * value * value)
    half = 0.5 * (1.0 + tangent)
    return value * half, half + 0.5 * value * (1.0 - tangent * tangent) * inner


def dot(left, right):
    return jnp.dot(left, right, preferred_element_type=f32)


def kernel(
    x_in, c_in, kept_in, pad_in, w_one, w_two, b_one, b_two, ft_in, tt_in, lf_in, li_in,
    xs, out_g,
    fts, tts, lfs, lis, wraw, wd, kraw, keeps, brow,
    send, got, back, home, facc, spec, hid, slope, kt, tmp, fil, dtwo, gacc, bacc,
    gp, gr, s_two, gz, s_three, fin, fy,
    load_sem, xin, kept_sem, ssem, rsem, gsend, grecv, gloc,
):
    me = lax.axis_index("space")
    dp = lax.axis_index("dp")
    core = lax.rem(me, 2)
    other = 1 - core
    m = me // 2
    y = m // 4
    z = lax.rem(m, 4)
    zh = dp // 4
    x = lax.rem(dp, 4)
    depth = zh * 4 + z
    buddy = (dp, 2 * m + other)

    def greet(device):
        pl.semaphore_signal(barrier, inc=1, device_id=device, device_id_type=MESH)

    def greet_group(i, carry):
        greet((dp, lax.rem(me + i, DEVICES)))
        return carry

    def plane_device(i):
        row = lax.rem(y + i // 4, 4)
        return (zh * 4 + lax.rem(x + lax.rem(i, 4), 4), 2 * (row * 4 + z) + core)

    def greet_plane(i, carry):
        greet(plane_device(4 * (i // 3) + lax.rem(i, 3) + 1))
        return carry

    def load(src, dst, at):
        return pltpu.make_async_copy(src, dst, load_sem.at[at])

    def start_field(v, ref):
        for j in range(3):
            for l in range(6):
                pltpu.make_async_copy(
                    ref.at[j, :, :, pl.ds(128 * l, 128)], xs.at[v, l, j, pl.ds(0, W)], xin.at[v, j]
                ).start()

    def wait_field(v, j):
        whole = xs.at[v, :, j, pl.ds(0, W)]
        pltpu.make_async_copy(whole, whole, xin.at[v, j]).wait()

    kept_own = load(kept_in, kraw.at[pl.ds(3 * core, 3)], 0)
    lon_table = load(ft_in, fts, 1)
    tables = [
        load(lf_in, lfs, 2),
        load(w_one, wraw.at[0], 3),
        load(w_two, wraw.at[1], 4),
        load(li_in, lis, 5),
        load(tt_in, tts, 6),
    ]
    start_field(0, x_in)
    lon_table.start()
    start_field(1, c_in)

    barrier = pltpu.get_barrier_semaphore()
    lax.fori_loop(1, DEVICES, greet_group, 0)
    lax.fori_loop(0, 12, greet_plane, 0)
    for i in range(4):
        greet((lax.rem(dp + 4, 8), 2 * (y * 4 + lax.rem(z + i, 4)) + core))

    for copy in [kept_own] + tables:
        copy.start()
    xs[:, :, :, W:] = jnp.zeros((2, 6, 3, WP - W, 2, 128), bf16)
    for chip in (12, 15):
        home[:, 2, :, :, chip] = jnp.zeros((2, 6, 3, 4, 2, 128), bf16)

    kept_swap = pltpu.make_async_remote_copy(
        src_ref=kept_in,
        dst_ref=kraw.at[pl.ds(3 * core, 3)],
        send_sem=kept_sem.at[0],
        recv_sem=kept_sem.at[1],
        device_id=buddy,
        device_id_type=MESH,
    )

    def row_valid(j):
        return jnp.where(3 * me + j < H - pad_in[0], 1.0, 0.0).astype(f32)

    def transform(v, a, loading=False):
        for j in range(3):
            if loading:
                wait_field(v, j)
            field = jnp.concatenate(
                [xs.at[v, l, j].reshape(2 * WP, 128)[...] for l in range(6)], axis=1
            )
            result = (dot(fts[v, a], field) * row_valid(j)).astype(bf16)
            for l in range(6):
                send.at[v, a, l, j].reshape(128, 128)[...] = result[:, 128 * l : 128 * l + 128]

    def message(source, target, device, send_at, recv_at):
        pltpu.make_async_remote_copy(
            src_ref=source,
            dst_ref=target,
            send_sem=send_at,
            recv_sem=recv_at,
            device_id=device,
            device_id_type=MESH,
        ).start()

    def is_short(chip):
        return jnp.logical_or(chip == 12, chip == 15)

    def where_held(chip, a, body):
        if isinstance(a, int) and a != 2:
            body()
        else:
            pl.when(jnp.logical_or(a != 2, jnp.logical_not(is_short(chip))))(body)

    def send_chunk(v, a):
        def one(i, carry):
            peer = lax.rem(me + i, DEVICES)
            pm, pc = peer // 2, lax.rem(peer, 2)
            where_held(
                pm,
                a,
                lambda: message(
                    send.at[v, a, pl.ds(3 * pc, 3), :, pm],
                    got.at[v, a, :, :, m, core],
                    (dp, peer),
                    ssem.at[v, a, lax.rem(pc + core, 2)],
                    rsem.at[v, a],
                ),
            )
            return carry

        def own():
            pltpu.make_async_copy(
                send.at[v, a, pl.ds(3 * core, 3), :, m], got.at[v, a, :, :, m, core], rsem.at[v, a]
            ).start()

        lax.fori_loop(1, DEVICES, one, 0)
        where_held(m, a, own)

    def send_back(v, a, first=1, last=DEVICES, beside=None):
        def one(i, carry):
            peer = lax.rem(me + i, DEVICES)
            pm, pc = peer // 2, lax.rem(peer, 2)
            where_held(
                m,
                a,
                lambda: message(
                    back.at[v, a, :, :, pm, pc],
                    home.at[v, a, pl.ds(3 * core, 3), :, m],
                    (dp, peer),
                    ssem.at[2 + v, a, lax.rem(pc + core, 2)],
                    rsem.at[2 + v, a],
                ),
            )
            if beside is not None:
                beside(i)
            return carry

        def own():
            pltpu.make_async_copy(
                back.at[v, a, :, :, m, core],
                home.at[v, a, pl.ds(3 * core, 3), :, m],
                rsem.at[2 + v, a],
            ).start()

        lax.fori_loop(first, last, one, 0)
        if last == DEVICES:
            where_held(m, a, own)

    def wait_chunk(v, a):
        pltpu.make_async_copy(got.at[v, a], got.at[v, a], rsem.at[v, a]).wait()

    def wait_home(v, a):
        part = home.at[v, a] if a != 2 else home.at[v, a, :, :, pl.ds(0, 14)]
        pltpu.make_async_copy(part, part, rsem.at[2 + v, a]).wait()

    lon_table.wait()
    transform(0, 0, True)
    pl.semaphore_wait(barrier, 31 + 12 + 4)
    send_chunk(0, 0)

    def transform_and_send(i, carry):
        transform(i // 3, lax.rem(i, 3))
        send_chunk(i // 3, lax.rem(i, 3))
        return carry

    lax.fori_loop(1, 3, transform_and_send, 0)
    transform(1, 0, True)
    send_chunk(1, 0)
    lax.fori_loop(4, 6, transform_and_send, 0)
    kept_swap.start()

    def kept_moves(i):
        return pltpu.make_async_remote_copy(
            src_ref=kept_in.at[pl.ds(1, 2)],
            dst_ref=kraw.at[pl.ds(6, 2)],
            send_sem=kept_sem.at[2 + i],
            recv_sem=kept_sem.at[4],
            device_id=(dp, 30 + i),
            device_id_type=MESH,
        )

    @pl.when(me == 25)
    def _():
        for i in range(2):
            kept_moves(i).start()
        for i in range(2):
            kept_moves(i).wait_send()

    @pl.when(m == 15)
    def _():
        moved = kraw.at[pl.ds(6, 2)]
        pltpu.make_async_copy(moved, moved, kept_sem.at[4]).wait()


    gacc[...] = jnp.zeros_like(gacc)
    bacc[...] = jnp.zeros_like(bacc)
    for copy in [kept_own, kept_swap] + tables:
        copy.wait()
    lane = lax.broadcasted_iota(jnp.int32, (BS, HC), 1)
    line = lax.broadcasted_iota(jnp.int32, (BS, HC), 0)
    for mat in range(2):
        for n in range(4):
            select = jnp.where(lane == line + BS * n, 1.0, 0.0).astype(bf16)
            real = dot(wraw[mat, 0, 4 * core + n], select)
            imag = dot(wraw[mat, 1, 4 * core + n], select)
            up, down = BS * n, HC + BS * n
            wd[mat, up : up + BS, :HC] = real.astype(bf16)
            wd[mat, up : up + BS, HC:] = imag.astype(bf16)
            wd[mat, down : down + BS, :HC] = (-imag).astype(bf16)
            wd[mat, down : down + BS, HC:] = real.astype(bf16)

    lane = lax.broadcasted_iota(jnp.int32, (NB, HC), 1)
    block = lax.broadcasted_iota(jnp.int32, (NB, HC), 0) - 4 * core
    spread = (lane >= BS * block) & (lane < BS * block + BS)
    for slot in range(6):
        moved = 2 <= slot < 4
        bits = kraw[slot + 4 * (m // 15) if moved else slot].astype(f32).astype(bf16)
        wide = lax.dot_general(
            bits,
            jnp.where(spread, 1.0, 0.0).astype(bf16),
            (((0,), (0,)), ((), ())),
            preferred_element_type=f32,
        )
        if not moved:
            wide = wide * jnp.where(6 * m + slot < W // 2 + 1, 1.0, 0.0).astype(f32)
        keeps[slot] = wide.astype(bf16)
    lane = lax.broadcasted_iota(jnp.int32, (BS, HC), 1)
    tiled = sum(jnp.where(lane == line + BS * n, 1.0, 0.0).astype(f32) for n in range(4))
    for mat, ref in enumerate((b_one, b_two)):
        for p in range(2):
            copies = jnp.dot(
                ref[p], tiled, precision=lax.Precision.HIGHEST, preferred_element_type=f32
            )
            brow[mat, p] = jnp.where(spread, copies, 0.0).sum(0, keepdims=True)

    def spectral(phase, a, half):
        held = jnp.concatenate([got.at[phase, a, l].reshape(768, 128)[...] for l in range(3)], axis=1)
        return dot(lfs[half * HC : half * HC + HC, :], held)

    def unspectral(v, a):
        for t in range(2):
            rows = slice(t * HC, t * HC + HC)
            result = dot(lis[rows, :], fil[...]).astype(bf16)
            for l in range(3):
                back.at[v, a, l].reshape(768, 128)[rows, :] = result[:, 128 * l : 128 * l + 128]

    def product(left, mat):
        for n in range(3):
            tmp[:, 256 * n : 256 * n + 256] = dot(left, wd[mat, :, 256 * n : 256 * n + 256])

    def product_turned(left, mat):
        for n in range(3):
            tmp[:, 256 * n : 256 * n + 256] = lax.dot_general(
                left,
                wd[mat, 256 * n : 256 * n + 256, :],
                (((1,), (1,)), ((), ())),
                preferred_element_type=f32,
            )

    def rows_of(step):
        return pl.ds(pl.multiple_of(step * 32, 32), 32)

    def kept_rows(a, step):
        kk = lax.rem(step // 3, 2)
        q = pl.multiple_of(lax.rem(step, 3) * 32, 32)
        return keeps[2 * a + kk, pl.ds(q, 32), :].astype(f32)

    def forward(a, carry):
        where_held(m, a, lambda: forward_chunk(a))
        return carry

    def forward_chunk(a):
        wait_chunk(0, a)
        for p in range(2):
            spec[a, :, p * HC : p * HC + HC] = spectral(0, a, p).astype(bf16)
        product(spec[a], 0)

        def gelu_rows(step, carry):
            rows = rows_of(step)
            for p in range(2):
                part = slice(p * HC, p * HC + HC)
                value, tilt = gelu_both(tmp[rows, part] + brow[0, p])
                hid[a, rows, part] = value.astype(bf16)
                slope[a, rows, part] = tilt
            return carry

        lax.fori_loop(0, 12, gelu_rows, 0)
        product(hid[a], 1)

        def shrink_rows(step, carry):
            rows = rows_of(step)
            kept = kept_rows(a, step)
            for p in range(2):
                part = slice(p * HC, p * HC + HC)
                value = tmp[rows, part] + brow[1, p]
                tangent = jnp.tanh(value * (1.0 / shrink))
                filtered = (value - shrink * tangent) * kept
                fil[pl.ds(pl.multiple_of(p * HC + step * 32, 32), 32), :] = filtered.astype(bf16)
                kt[a, rows, part] = kept * (tangent * tangent)
            return carry

        lax.fori_loop(0, 12, shrink_rows, 0)
        unspectral(0, a)

    lax.fori_loop(0, 3, forward, 0)
    send_back(0, 0)
    send_back(0, 1, 1, 16)

    def add_grad(mat, left, right):
        for n in range(3):
            part = slice(256 * n, 256 * n + 256)
            gacc[mat, :, part] += lax.dot_general(
                left, right[:, part], (((0,), (0,)), ((), ())), preferred_element_type=f32
            )

    def backward(a, carry):
        where_held(m, a, lambda: backward_chunk(a))
        return carry

    def backward_chunk(a):
        wait_chunk(1, a)
        for p in range(2):
            tmp[:, p * HC : p * HC + HC] = spectral(1, a, p)

        def scaled_rows(mat, scale):
            def one(step, carry):
                rows = rows_of(step)
                for p in range(2):
                    part = slice(p * HC, p * HC + HC)
                    value = (tmp[rows, part] * scale[a, rows, part]).astype(bf16)
                    dtwo[rows, part] = value
                    bacc[mat, :, part] += value.astype(f32).reshape(4, 8, HC).sum(0)
                return carry

            lax.fori_loop(0, 12, one, 0)

        scaled_rows(1, kt)
        add_grad(1, hid[a], dtwo[...])
        product_turned(dtwo[...], 1)
        scaled_rows(0, slope)
        add_grad(0, spec[a], dtwo[...])
        product_turned(dtwo[...], 0)
        for p in range(2):
            fil[p * HC : p * HC + HC, :] = tmp[:, p * HC : p * HC + HC].astype(bf16)
        unspectral(1, a)

    lax.fori_loop(0, 3, backward, 0)

    first_row = lax.broadcasted_iota(jnp.int32, (128 - BS, 128), 0) == 0
    for mat in range(2):
        for n in range(4):
            start = BS * n // 128 * 128
            shift = BS * n - start
            window = 256 if shift + BS > 128 else 128
            up = slice(BS * n, BS * n + BS)
            down = slice(HC + BS * n, HC + BS * n + BS)
            left = slice(start, start + window)
            right = slice(HC + start, HC + start + window)

            def align(value):
                if shift:
                    value = pltpu.roll(value, window - shift, 1)
                return value[:, :128]

            gp[n, 2 * mat, :BS, :] = align(gacc[mat, up, left] + gacc[mat, down, right]).astype(bf16)
            gp[n, 2 * mat + 1, :BS, :] = align(gacc[mat, up, right] - gacc[mat, down, left]).astype(bf16)
            for p, part in enumerate((left, right)):
                summed = align(bacc[mat, :, part]).sum(0, keepdims=True)
                gp[n, 2 * mat + p, BS:, :] = jnp.where(first_row, summed, 0.0).astype(bf16)

    def to_depths(source, target, at):
        def one(i, carry):
            message(source(i), target, depth_device(i), gsend.at[at], grecv.at[at])
            return carry

        lax.fori_loop(1, 8, one, 0)

    def settle(part, at):
        pltpu.make_async_copy(part, part, grecv.at[at]).wait()

    def depth_of(i):
        return lax.rem(depth + i, 8)

    def depth_device(i):
        at = depth_of(i)
        return (4 * (at // 4) + x, 2 * (y * 4 + lax.rem(at, 4)) + core)

    def depth_rows(i):
        return pl.ds(pl.multiple_of(16 * i, 16), 16)

    def to_owner(i):
        row, column = lax.rem(y + i // 4, 4), lax.rem(x + lax.rem(i, 4), 4)
        message(gp.at[row, column], gr.at[4 * y + x], plane_device(i), gsend.at[0], grecv.at[0])

    def from_owner(i):
        message(fy.at[y, x], fy.at[y, x], plane_device(i), gsend.at[3], grecv.at[3])

    send_back(0, 1, 16, 31, lambda i: to_owner(i - 15))
    send_back(0, 1, 31)
    send_back(0, 2)
    gr[4 * y + x] = gp[y, x]
    settle(gr.at[pl.ds(0, 15)], 0)
    total = gr[0].astype(f32)
    for i in range(1, 16):
        total = total + gr[i].astype(f32)
    s_two[...] = total.astype(bf16)
    to_depths(lambda i: s_two.at[depth_rows(depth_of(i))], gz.at[depth], 1)
    send_back(1, 0)
    gz[depth] = s_two[depth_rows(depth), :]
    settle(gz.at[pl.ds(0, 7)], 1)
    total = gz[0].astype(f32)
    for i in range(1, 8):
        total = total + gz[i].astype(f32)
    s_three[...] = (total * (1.0 / (IMAGES * H))).astype(bf16)
    to_depths(lambda i: s_three, fin.at[depth], 2)
    send_back(1, 1)
    fin[depth] = s_three[...]
    settle(fin.at[pl.ds(0, 7)], 2)
    fy[y, x] = fin[...].reshape(128, 128)
    send_back(1, 2, 1, 16, from_owner)
    send_back(1, 2, 16)

    def leave(v):
        def part(j, a, n):
            piece = jnp.concatenate(
                [home.at[v, a, l, j].reshape(128, 128)[...] for l in range(6)], axis=1
            )
            rows = slice(n * WP, n * WP + WP)
            return dot(tts[1 - v, rows, 128 * a : 128 * a + 128], piece)

        def begin(j, carry):
            for l in range(6):
                part = xs.at[v, l, j].reshape(2 * WP, 128)[...]
                facc[j, :, 128 * l : 128 * l + 128] = part.astype(f32)
            return carry

        lax.fori_loop(0, 3, begin, 0)
        for a in range(2):
            wait_home(v, a)

            def one(j, carry):
                for n in range(2):
                    facc[j, n * WP : n * WP + WP, :] += part(j, a, n)
                return carry

            lax.fori_loop(0, 3, one, 0)
        wait_home(v, 2)

        def last(j, carry):
            scale = row_valid(j)
            for n in range(2):
                rows = slice(n * WP, n * WP + WP)
                result = ((facc[j, rows, :] + part(j, 2, n)) * scale).astype(bf16)
                for l in range(6):
                    xs.at[v, l, j].reshape(2 * WP, 128)[rows, :] = result[
                        :, 128 * l : 128 * l + 128
                    ]
            return carry

        lax.fori_loop(0, 3, last, 0)

    leave(0)

    settle(gr.at[pl.ds(0, 15)], 3)
    fy_away = pltpu.make_async_remote_copy(
        src_ref=fy,
        dst_ref=out_g.at[core],
        send_sem=gsend.at[4],
        recv_sem=grecv.at[4],
        device_id=buddy,
        device_id_type=MESH,
    )
    fy_away.start()
    fy_stays = pltpu.make_async_copy(fy, out_g.at[core], gloc)
    fy_stays.start()

    leave(1)

    def sent(phase, a, counts):
        for at in range(2):
            part = got.at[0, 0, :, :, pl.ds(0, counts[at]), 0]
            pltpu.make_async_copy(part, part, ssem.at[phase, a, at]).wait()

    for phase in range(4):
        for a in range(2):
            sent(phase, a, (15, 16))

    @pl.when(is_short(m))
    def _():
        for phase in range(2):
            sent(phase, 2, (14, 14))

    @pl.when(jnp.logical_not(is_short(m)))
    def _():
        for phase in range(2):
            sent(phase, 2, (13, 14))
            sent(2 + phase, 2, (15, 16))

    for at, part in (
        (0, gr.at[pl.ds(0, 15)]),
        (1, gz.at[pl.ds(0, 7)]),
        (2, fin.at[pl.ds(0, 7)]),
        (3, gr.at[pl.ds(0, 15)]),
    ):
        pltpu.make_async_copy(part, part, gsend.at[at]).wait()
    fy_away.wait()
    fy_stays.wait()


def mix(x_wide, c_wide, kept, pad_rows, w_one, w_two, b_one, b_two):
    forward_lon, inverse_lon = longitude_parts()
    ahead = np.stack([to_spectrum_table(forward_lon), to_spectrum_table(inverse_lon)])
    turned = ahead.transpose(0, 3, 1, 2).reshape(2, 2 * WP, 3 * 128)
    lf, li = lat_tables()
    as_bf16 = lambda table: jnp.asarray(table.astype(jnp.bfloat16))
    tables = (as_bf16(ahead), as_bf16(turned), as_bf16(lf), as_bf16(li))
    anywhere = pl.BlockSpec(memory_space=pl.ANY)
    vmem = pl.BlockSpec(memory_space=pltpu.VMEM)
    dma = pltpu.SemaphoreType.DMA
    return pl.pallas_call(
        kernel,
        out_shape=(
            pltpu.VMEM((2, 6, 3, WP, 2, 128), bf16),
            jax.ShapeDtypeStruct((2, 4, 4, 128, 128), bf16),
        ),
        in_specs=[anywhere] * 3
        + [pl.BlockSpec(memory_space=pltpu.SMEM)]
        + [anywhere] * 2
        + [vmem] * 2
        + [anywhere] * 4,
        out_specs=(vmem, anywhere),
        scratch_shapes=[
            pltpu.VMEM((2, 3, 128, 2 * WP), bf16),
            pltpu.VMEM((2, 2 * WP, 3 * 128), bf16),
            pltpu.VMEM((768, 768), bf16),
            pltpu.VMEM((768, 768), bf16),
            pltpu.VMEM((2, 2, NB, BS, BS), bf16),
            pltpu.VMEM((2, 768, 768), bf16),
            pltpu.VMEM((8, NB, H), jnp.int32),
            pltpu.VMEM((6, H, HC), bf16),
            pltpu.VMEM((2, 2, 1, HC), f32),
            pltpu.VMEM((2, 3, 6, 3, CHIPS, 4, 2, 128), bf16),
            pltpu.VMEM((2, 3, 3, 3, CHIPS, 2, 4, 2, 128), bf16),
            pltpu.VMEM((2, 3, 3, 3, CHIPS, 2, 4, 2, 128), bf16),
            pltpu.VMEM((2, 3, 6, 3, CHIPS, 4, 2, 128), bf16),
            pltpu.VMEM((3, 2 * WP, C), f32),
            pltpu.VMEM((3, HC, 768), bf16),
            pltpu.VMEM((3, HC, 768), bf16),
            pltpu.VMEM((3, HC, 768), f32),
            pltpu.VMEM((3, HC, 768), f32),
            pltpu.VMEM((HC, 768), f32),
            pltpu.VMEM((768, HC), bf16),
            pltpu.VMEM((HC, 768), bf16),
            pltpu.VMEM((2, 768, 768), f32),
            pltpu.VMEM((2, 8, 768), f32),
            pltpu.VMEM((4, 4, 128, 128), bf16),
            pltpu.VMEM((16, 128, 128), bf16),
            pltpu.VMEM((128, 128), bf16),
            pltpu.VMEM((8, 16, 128), bf16),
            pltpu.VMEM((16, 128), bf16),
            pltpu.VMEM((8, 16, 128), bf16),
            pltpu.VMEM((4, 4, 128, 128), bf16),
            dma((7,)),
            dma((2, 3)),
            dma((5,)),
            dma((4, 3, 2)),
            dma((4, 3)),
            dma((5,)),
            dma((5,)),
            dma,
        ],
        compiler_params=pltpu.CompilerParams(
            collective_id=0, has_side_effects=True, vmem_limit_bytes=56 * 2**20
        ),
    )(x_wide, c_wide, kept, pad_rows, w_one, w_two, b_one, b_two, *tables)


def finish(
    fields, g_ref, out_x, out_c, gw_one, gb_one, gw_two, gb_two,
    parts, weights, biases, out_sem, g_sem,
):
    load_parts = pltpu.make_async_copy(g_ref, parts, g_sem.at[0])
    load_parts.start()
    stores = []
    for v, target in enumerate((out_x, out_c)):
        for l in range(6):
            stores.append(
                pltpu.make_async_copy(
                    fields.at[v, l, :, pl.ds(0, W)],
                    target.at[:, :, :, pl.ds(128 * l, 128)],
                    out_sem.at[v, l],
                )
            )
            stores[-1].start()
    load_parts.wait()
    for mat, (weight, bias) in enumerate(((gw_one, gb_one), (gw_two, gb_two))):
        for p in range(2):
            for n in range(NB):
                block = parts[n // 4, n % 4, 2 * mat + p].astype(f32)
                weights[mat, p, n] = block[:BS, :BS]
                biases[mat, p, n : n + 1, :] = block[BS : BS + 1, :BS]
        stores.append(pltpu.make_async_copy(weights.at[mat], weight, g_sem.at[1 + mat]))
        stores[-1].start()
        stores.append(pltpu.make_async_copy(biases.at[mat], bias, g_sem.at[3 + mat]))
        stores[-1].start()
    for store in stores:
        store.wait()


def settle_outputs(fields, out_g):
    anywhere = pl.BlockSpec(memory_space=pl.ANY)
    vmem = pl.BlockSpec(memory_space=pltpu.VMEM)
    return pl.pallas_call(
        finish,
        out_shape=(
            jax.ShapeDtypeStruct((3, W, 2, C), bf16),
            jax.ShapeDtypeStruct((3, W, 2, C), bf16),
            jax.ShapeDtypeStruct((2, NB, BS, BS), f32),
            jax.ShapeDtypeStruct((2, NB, BS), f32),
            jax.ShapeDtypeStruct((2, NB, BS, BS), f32),
            jax.ShapeDtypeStruct((2, NB, BS), f32),
        ),
        in_specs=[vmem, anywhere],
        out_specs=(anywhere,) * 6,
        scratch_shapes=[
            pltpu.VMEM(out_g.shape, bf16),
            pltpu.VMEM((2, 2, NB, BS, BS), f32),
            pltpu.VMEM((2, 2, NB, BS), f32),
            pltpu.SemaphoreType.DMA((2, 6)),
            pltpu.SemaphoreType.DMA((5,)),
        ],
        compiler_params=pltpu.CompilerParams(vmem_limit_bytes=56 * 2**20),
    )(pltpu.with_memory_space_constraint(fields, pltpu.VMEM), out_g)


def on_device(inputs, cotangent, kept_modes, pad_rows, weight_one, bias_one, weight_two, bias_two):
    wide = lambda array: jnp.transpose(array, (1, 2, 0, 3))
    out_x, out_c, gw_one, gb_one, gw_two, gb_two = settle_outputs(
        *mix(
            wide(inputs),
            wide(cotangent),
            jnp.transpose(kept_modes, (2, 0, 1)),
            pad_rows,
            weight_one,
            weight_two,
            bias_one,
            bias_two,
        )
    )
    narrow = lambda array: jnp.transpose(array, (2, 0, 1, 3))
    return narrow(out_x), narrow(out_c), gw_one, gb_one, gw_two, gb_two


def solution(mesh):
    placed = (
        P("dp", "space", None, None),
        P("dp", "space", None, None),
        P(None, None, "space"),
        P(),
        P(),
        P(),
        P(),
        P(),
    )
    return jax.shard_map(
        on_device,
        mesh=mesh,
        in_specs=placed,
        out_specs=(P("dp", "space", None, None), P("dp", "space", None, None), P(), P(), P(), P()),
        check_vma=False,
    )
```

```python
import numpy as np

import jax
import jax.numpy as jnp
from jax import lax
from jax.experimental import pallas as pl
from jax.experimental.pallas import tpu as pltpu
from jax.sharding import PartitionSpec as P

shrink = 0.25
gelu_scale = 0.7978845608028654
gelu_cubic = 0.044715

H = 96
W = 180
WP = 192
C = 768
HC = 384
NB = 8
BS = 96
KWP = 96
CHIPS = 16
DEVICES = 32
IMAGES = 16
MESH = pl.DeviceIdType.MESH
f32 = jnp.float32
bf16 = jnp.bfloat16


def longitude_parts():
    wavenum = np.arange(KWP)[:, None]
    column = np.arange(W)[None, :]
    phase = np.float32(2.0 * np.pi / W) * (wavenum * column % W).astype(np.float32)
    scaling = (wavenum < W // 2 + 1).astype(np.float32) / np.sqrt(np.float32(W))
    double = np.where((wavenum == 0) | (2 * wavenum == W), 1.0, 2.0).astype(np.float32)
    cosine = np.cos(phase) * scaling
    sine = np.sin(phase) * scaling
    forward = np.stack([cosine, -sine])
    inverse = np.stack([double * cosine, -double * sine])
    return forward, inverse


def latitude_parts(sign):
    row = np.arange(H)[:, None]
    column = np.arange(H)[None, :]
    phase = np.float32(2.0 * np.pi / H) * (row * column % H).astype(np.float32)
    scaling = np.float32(1.0) / np.sqrt(np.float32(H))
    cosine = np.cos(phase) * scaling
    sine = np.float32(sign) * np.sin(phase) * scaling
    upper = np.stack([cosine, sine], -1)
    lower = np.stack([-sine, cosine], -1)
    return np.stack([upper, lower], 0)


def wavenumber_slots():
    slots = np.arange(KWP).reshape(16, 3, 2)
    slots[15, 1] = slots[12, 2]
    slots[12, 2] = slots[15, 2] = KWP - 1
    return slots


def to_spectrum_table(part):
    out = np.zeros((3, 16, 2, 2, 2, WP, 2), np.float32)
    grouped = part[:, wavenumber_slots()].transpose(2, 1, 0, 3, 4)
    for b in range(2):
        out[:, :, b, :, :, :W, b] = grouped
    return out.reshape(3, 128, 2 * WP)


def lat_tables():
    forward = latitude_parts(1.0)
    inverse = latitude_parts(-1.0)
    ahead = np.zeros((2, 2, 2, H, 3, 16, 2, 2, 2, 2), np.float32)
    back = np.zeros((3, 16, 2, 2, 2, 2, 2, 2, 2, H), np.float32)
    split = forward.reshape(2, H, 16, 2, 3, 2).transpose(0, 1, 4, 2, 3, 5)
    isplit = inverse.reshape(2, 16, 2, 3, H, 2).transpose(3, 1, 2, 0, 5, 4)
    for b in range(2):
        for kk in range(2):
            ahead[:, b, kk, :, :, :, :, b, :, kk] = split
            back[:, :, :, b, :, kk, :, b, kk, :] = isplit
    return ahead.reshape(768, 768), back.reshape(768, 768)


def gelu_both(value):
    tangent = jnp.tanh(gelu_scale * (value + gelu_cubic * value * value * value))
    inner = gelu_scale * (1.0 + 3.0 * gelu_cubic * value * value)
    half = 0.5 * (1.0 + tangent)
    return value * half, half + 0.5 * value * (1.0 - tangent * tangent) * inner


def dot(left, right):
    return jnp.dot(left, right, preferred_element_type=f32)


def kernel(
    x_in, c_in, kept_in, pad_in, w_one, w_two, b_one, b_two, ft_in, tt_in, lf_in, li_in,
    xs, out_g,
    fts, tts, lfs, lis, wraw, wd, kraw, keeps, brow,
    send, got, back, home, facc, spec, hid, slope, kt, tmp, fil, dtwo, gacc, bacc,
    gp, gr, s_two, gz, s_three, fin, fy,
    load_sem, xin, kept_sem, ssem, rsem, gsend, grecv, gloc,
):
    me = lax.axis_index("space")
    dp = lax.axis_index("dp")
    core = lax.rem(me, 2)
    other = 1 - core
    m = me // 2
    y = m // 4
    z = lax.rem(m, 4)
    zh = dp // 4
    x = lax.rem(dp, 4)
    depth = zh * 4 + z
    buddy = (dp, 2 * m + other)

    def greet(device):
        pl.semaphore_signal(barrier, inc=1, device_id=device, device_id_type=MESH)

    def greet_group(i, carry):
        greet((dp, lax.rem(me + i, DEVICES)))
        return carry

    def plane_device(i):
        row = lax.rem(y + i // 4, 4)
        return (zh * 4 + lax.rem(x + lax.rem(i, 4), 4), 2 * (row * 4 + z) + core)

    def greet_plane(i, carry):
        greet(plane_device(4 * (i // 3) + lax.rem(i, 3) + 1))
        return carry

    barrier = pltpu.get_barrier_semaphore()
    lax.fori_loop(1, DEVICES, greet_group, 0)
    lax.fori_loop(0, 12, greet_plane, 0)
    for i in range(4):
        greet((lax.rem(dp + 4, 8), 2 * (y * 4 + lax.rem(z + i, 4)) + core))

    def load(src, dst, at):
        return pltpu.make_async_copy(src, dst, load_sem.at[at])

    def start_field(v, ref):
        for j in range(3):
            for l in range(6):
                pltpu.make_async_copy(
                    ref.at[j, :, :, pl.ds(128 * l, 128)], xs.at[v, l, j, pl.ds(0, W)], xin.at[v, j]
                ).start()

    def wait_field(v, j):
        whole = xs.at[v, :, j, pl.ds(0, W)]
        pltpu.make_async_copy(whole, whole, xin.at[v, j]).wait()

    kept_own = load(kept_in, kraw.at[pl.ds(3 * core, 3)], 0)
    lon_table = load(ft_in, fts, 1)
    tables = [
        load(lf_in, lfs, 2),
        load(w_one, wraw.at[0], 3),
        load(w_two, wraw.at[1], 4),
        load(li_in, lis, 5),
        load(tt_in, tts, 6),
    ]
    lon_table.start()
    start_field(0, x_in)

    start_field(1, c_in)
    for copy in [kept_own] + tables:
        copy.start()
    xs[:, :, :, W:] = jnp.zeros((2, 6, 3, WP - W, 2, 128), bf16)
    for chip in (12, 15):
        home[:, 2, :, :, chip] = jnp.zeros((2, 6, 3, 4, 2, 128), bf16)

    kept_swap = pltpu.make_async_remote_copy(
        src_ref=kept_in,
        dst_ref=kraw.at[pl.ds(3 * core, 3)],
        send_sem=kept_sem.at[0],
        recv_sem=kept_sem.at[1],
        device_id=buddy,
        device_id_type=MESH,
    )

    def row_valid(j):
        return jnp.where(3 * me + j < H - pad_in[0], 1.0, 0.0).astype(f32)

    def transform(v, a, loading=False):
        for j in range(3):
            if loading:
                wait_field(v, j)
            field = jnp.concatenate(
                [xs.at[v, l, j].reshape(2 * WP, 128)[...] for l in range(6)], axis=1
            )
            result = (dot(fts[v, a], field) * row_valid(j)).astype(bf16)
            for l in range(6):
                send.at[v, a, l, j].reshape(128, 128)[...] = result[:, 128 * l : 128 * l + 128]

    def message(source, target, device, send_at, recv_at):
        pltpu.make_async_remote_copy(
            src_ref=source,
            dst_ref=target,
            send_sem=send_at,
            recv_sem=recv_at,
            device_id=device,
            device_id_type=MESH,
        ).start()

    def is_short(chip):
        return jnp.logical_or(chip == 12, chip == 15)

    def where_held(chip, a, body):
        if isinstance(a, int) and a != 2:
            body()
        else:
            pl.when(jnp.logical_or(a != 2, jnp.logical_not(is_short(chip))))(body)

    def send_chunk(v, a):
        def one(i, carry):
            peer = lax.rem(me + i, DEVICES)
            pm, pc = peer // 2, lax.rem(peer, 2)
            where_held(
                pm,
                a,
                lambda: message(
                    send.at[v, a, pl.ds(3 * pc, 3), :, pm],
                    got.at[v, a, :, :, m, core],
                    (dp, peer),
                    ssem.at[v, a, lax.rem(pc + core, 2)],
                    rsem.at[v, a],
                ),
            )
            return carry

        def own():
            pltpu.make_async_copy(
                send.at[v, a, pl.ds(3 * core, 3), :, m], got.at[v, a, :, :, m, core], rsem.at[v, a]
            ).start()

        lax.fori_loop(1, DEVICES, one, 0)
        where_held(m, a, own)

    def send_back(v, a, first=1, last=DEVICES, beside=None):
        def one(i, carry):
            peer = lax.rem(me + i, DEVICES)
            pm, pc = peer // 2, lax.rem(peer, 2)
            where_held(
                m,
                a,
                lambda: message(
                    back.at[v, a, :, :, pm, pc],
                    home.at[v, a, pl.ds(3 * core, 3), :, m],
                    (dp, peer),
                    ssem.at[2 + v, a, lax.rem(pc + core, 2)],
                    rsem.at[2 + v, a],
                ),
            )
            if beside is not None:
                beside(i)
            return carry

        def own():
            pltpu.make_async_copy(
                back.at[v, a, :, :, m, core],
                home.at[v, a, pl.ds(3 * core, 3), :, m],
                rsem.at[2 + v, a],
            ).start()

        lax.fori_loop(first, last, one, 0)
        if last == DEVICES:
            where_held(m, a, own)

    def wait_chunk(v, a):
        pltpu.make_async_copy(got.at[v, a], got.at[v, a], rsem.at[v, a]).wait()

    def wait_home(v, a):
        part = home.at[v, a] if a != 2 else home.at[v, a, :, :, pl.ds(0, 14)]
        pltpu.make_async_copy(part, part, rsem.at[2 + v, a]).wait()

    lon_table.wait()
    transform(0, 0, True)
    pl.semaphore_wait(barrier, 31 + 12 + 4)
    send_chunk(0, 0)

    def transform_and_send(i, carry):
        transform(i // 3, lax.rem(i, 3))
        send_chunk(i // 3, lax.rem(i, 3))
        return carry

    lax.fori_loop(1, 3, transform_and_send, 0)
    transform(1, 0, True)
    send_chunk(1, 0)
    lax.fori_loop(4, 6, transform_and_send, 0)
    kept_swap.start()

    def kept_moves(i):
        return pltpu.make_async_remote_copy(
            src_ref=kept_in.at[pl.ds(1, 2)],
            dst_ref=kraw.at[pl.ds(6, 2)],
            send_sem=kept_sem.at[2 + i],
            recv_sem=kept_sem.at[4],
            device_id=(dp, 30 + i),
            device_id_type=MESH,
        )

    @pl.when(me == 25)
    def _():
        for i in range(2):
            kept_moves(i).start()
        for i in range(2):
            kept_moves(i).wait_send()

    @pl.when(m == 15)
    def _():
        moved = kraw.at[pl.ds(6, 2)]
        pltpu.make_async_copy(moved, moved, kept_sem.at[4]).wait()


    gacc[...] = jnp.zeros_like(gacc)
    bacc[...] = jnp.zeros_like(bacc)
    for copy in [kept_own, kept_swap] + tables:
        copy.wait()
    lane = lax.broadcasted_iota(jnp.int32, (BS, HC), 1)
    line = lax.broadcasted_iota(jnp.int32, (BS, HC), 0)
    for mat in range(2):
        for n in range(4):
            select = jnp.where(lane == line + BS * n, 1.0, 0.0).astype(bf16)
            real = dot(wraw[mat, 0, 4 * core + n], select)
            imag = dot(wraw[mat, 1, 4 * core + n], select)
            up, down = BS * n, HC + BS * n
            wd[mat, up : up + BS, :HC] = real.astype(bf16)
            wd[mat, up : up + BS, HC:] = imag.astype(bf16)
            wd[mat, down : down + BS, :HC] = (-imag).astype(bf16)
            wd[mat, down : down + BS, HC:] = real.astype(bf16)

    lane = lax.broadcasted_iota(jnp.int32, (NB, HC), 1)
    block = lax.broadcasted_iota(jnp.int32, (NB, HC), 0) - 4 * core
    spread = (lane >= BS * block) & (lane < BS * block + BS)
    for slot in range(6):
        moved = 2 <= slot < 4
        bits = kraw[slot + 4 * (m // 15) if moved else slot].astype(f32).astype(bf16)
        wide = lax.dot_general(
            bits,
            jnp.where(spread, 1.0, 0.0).astype(bf16),
            (((0,), (0,)), ((), ())),
            preferred_element_type=f32,
        )
        if not moved:
            wide = wide * jnp.where(6 * m + slot < W // 2 + 1, 1.0, 0.0).astype(f32)
        keeps[slot] = wide.astype(bf16)
    lane = lax.broadcasted_iota(jnp.int32, (BS, HC), 1)
    tiled = sum(jnp.where(lane == line + BS * n, 1.0, 0.0).astype(f32) for n in range(4))
    for mat, ref in enumerate((b_one, b_two)):
        for p in range(2):
            copies = jnp.dot(
                ref[p], tiled, precision=lax.Precision.HIGHEST, preferred_element_type=f32
            )
            brow[mat, p] = jnp.where(spread, copies, 0.0).sum(0, keepdims=True)

    def spectral(phase, a, half):
        held = jnp.concatenate([got.at[phase, a, l].reshape(768, 128)[...] for l in range(3)], axis=1)
        return dot(lfs[half * HC : half * HC + HC, :], held)

    def unspectral(v, a):
        for t in range(2):
            rows = slice(t * HC, t * HC + HC)
            result = dot(lis[rows, :], fil[...]).astype(bf16)
            for l in range(3):
                back.at[v, a, l].reshape(768, 128)[rows, :] = result[:, 128 * l : 128 * l + 128]

    def product(left, mat):
        for n in range(3):
            tmp[:, 256 * n : 256 * n + 256] = dot(left, wd[mat, :, 256 * n : 256 * n + 256])

    def product_turned(left, mat):
        for n in range(3):
            tmp[:, 256 * n : 256 * n + 256] = lax.dot_general(
                left,
                wd[mat, 256 * n : 256 * n + 256, :],
                (((1,), (1,)), ((), ())),
                preferred_element_type=f32,
            )

    def rows_of(step):
        return pl.ds(pl.multiple_of(step * 32, 32), 32)

    def kept_rows(a, step):
        kk = lax.rem(step // 3, 2)
        q = pl.multiple_of(lax.rem(step, 3) * 32, 32)
        return keeps[2 * a + kk, pl.ds(q, 32), :].astype(f32)

    def forward(a, carry):
        where_held(m, a, lambda: forward_chunk(a))
        return carry

    def forward_chunk(a):
        wait_chunk(0, a)
        for p in range(2):
            spec[a, :, p * HC : p * HC + HC] = spectral(0, a, p).astype(bf16)
        product(spec[a], 0)

        def gelu_rows(step, carry):
            rows = rows_of(step)
            for p in range(2):
                part = slice(p * HC, p * HC + HC)
                value, tilt = gelu_both(tmp[rows, part] + brow[0, p])
                hid[a, rows, part] = value.astype(bf16)
                slope[a, rows, part] = tilt
            return carry

        lax.fori_loop(0, 12, gelu_rows, 0)
        product(hid[a], 1)

        def shrink_rows(step, carry):
            rows = rows_of(step)
            kept = kept_rows(a, step)
            for p in range(2):
                part = slice(p * HC, p * HC + HC)
                value = tmp[rows, part] + brow[1, p]
                tangent = jnp.tanh(value * (1.0 / shrink))
                filtered = (value - shrink * tangent) * kept
                fil[pl.ds(pl.multiple_of(p * HC + step * 32, 32), 32), :] = filtered.astype(bf16)
                kt[a, rows, part] = kept * (tangent * tangent)
            return carry

        lax.fori_loop(0, 12, shrink_rows, 0)
        unspectral(0, a)

    lax.fori_loop(0, 3, forward, 0)
    send_back(0, 0)
    send_back(0, 1, 1, 16)

    def add_grad(mat, left, right):
        for n in range(3):
            part = slice(256 * n, 256 * n + 256)
            gacc[mat, :, part] += lax.dot_general(
                left, right[:, part], (((0,), (0,)), ((), ())), preferred_element_type=f32
            )

    def backward(a, carry):
        where_held(m, a, lambda: backward_chunk(a))
        return carry

    def backward_chunk(a):
        wait_chunk(1, a)
        for p in range(2):
            tmp[:, p * HC : p * HC + HC] = spectral(1, a, p)

        def scaled_rows(mat, scale):
            def one(step, carry):
                rows = rows_of(step)
                for p in range(2):
                    part = slice(p * HC, p * HC + HC)
                    value = (tmp[rows, part] * scale[a, rows, part]).astype(bf16)
                    dtwo[rows, part] = value
                    bacc[mat, :, part] += value.astype(f32).reshape(4, 8, HC).sum(0)
                return carry

            lax.fori_loop(0, 12, one, 0)

        scaled_rows(1, kt)
        add_grad(1, hid[a], dtwo[...])
        product_turned(dtwo[...], 1)
        scaled_rows(0, slope)
        add_grad(0, spec[a], dtwo[...])
        product_turned(dtwo[...], 0)
        for p in range(2):
            fil[p * HC : p * HC + HC, :] = tmp[:, p * HC : p * HC + HC].astype(bf16)
        unspectral(1, a)

    lax.fori_loop(0, 3, backward, 0)

    first_row = lax.broadcasted_iota(jnp.int32, (128 - BS, 128), 0) == 0
    for mat in range(2):
        for n in range(4):
            start = BS * n // 128 * 128
            shift = BS * n - start
            window = 256 if shift + BS > 128 else 128
            up = slice(BS * n, BS * n + BS)
            down = slice(HC + BS * n, HC + BS * n + BS)
            left = slice(start, start + window)
            right = slice(HC + start, HC + start + window)

            def align(value):
                if shift:
                    value = pltpu.roll(value, window - shift, 1)
                return value[:, :128]

            gp[n, 2 * mat, :BS, :] = align(gacc[mat, up, left] + gacc[mat, down, right]).astype(bf16)
            gp[n, 2 * mat + 1, :BS, :] = align(gacc[mat, up, right] - gacc[mat, down, left]).astype(bf16)
            for p, part in enumerate((left, right)):
                summed = align(bacc[mat, :, part]).sum(0, keepdims=True)
                gp[n, 2 * mat + p, BS:, :] = jnp.where(first_row, summed, 0.0).astype(bf16)

    def to_depths(source, target, at):
        def one(i, carry):
            message(source(i), target, depth_device(i), gsend.at[at], grecv.at[at])
            return carry

        lax.fori_loop(1, 8, one, 0)

    def settle(part, at):
        pltpu.make_async_copy(part, part, grecv.at[at]).wait()

    def depth_of(i):
        return lax.rem(depth + i, 8)

    def depth_device(i):
        at = depth_of(i)
        return (4 * (at // 4) + x, 2 * (y * 4 + lax.rem(at, 4)) + core)

    def depth_rows(i):
        return pl.ds(pl.multiple_of(16 * i, 16), 16)

    def to_owner(i):
        row, column = lax.rem(y + i // 4, 4), lax.rem(x + lax.rem(i, 4), 4)
        message(gp.at[row, column], gr.at[4 * y + x], plane_device(i), gsend.at[0], grecv.at[0])

    def from_owner(i):
        message(fy.at[y, x], fy.at[y, x], plane_device(i), gsend.at[3], grecv.at[3])

    send_back(0, 1, 16, 31, lambda i: to_owner(i - 15))
    send_back(0, 1, 31)
    send_back(0, 2)
    gr[4 * y + x] = gp[y, x]
    settle(gr.at[pl.ds(0, 15)], 0)
    total = gr[0].astype(f32)
    for i in range(1, 16):
        total = total + gr[i].astype(f32)
    s_two[...] = total.astype(bf16)
    to_depths(lambda i: s_two.at[depth_rows(depth_of(i))], gz.at[depth], 1)
    send_back(1, 0)
    gz[depth] = s_two[depth_rows(depth), :]
    settle(gz.at[pl.ds(0, 7)], 1)
    total = gz[0].astype(f32)
    for i in range(1, 8):
        total = total + gz[i].astype(f32)
    s_three[...] = (total * (1.0 / (IMAGES * H))).astype(bf16)
    to_depths(lambda i: s_three, fin.at[depth], 2)
    send_back(1, 1, 1, 16)
    fin[depth] = s_three[...]
    settle(fin.at[pl.ds(0, 7)], 2)
    fy[y, x] = fin[...].reshape(128, 128)
    send_back(1, 1, 16, 31, lambda i: from_owner(i - 15))
    send_back(1, 1, 31)
    send_back(1, 2)

    def leave(v):
        def part(j, a, n):
            piece = jnp.concatenate(
                [home.at[v, a, l, j].reshape(128, 128)[...] for l in range(6)], axis=1
            )
            rows = slice(n * WP, n * WP + WP)
            return dot(tts[1 - v, rows, 128 * a : 128 * a + 128], piece)

        def begin(j, carry):
            for l in range(6):
                part = xs.at[v, l, j].reshape(2 * WP, 128)[...]
                facc[j, :, 128 * l : 128 * l + 128] = part.astype(f32)
            return carry

        lax.fori_loop(0, 3, begin, 0)
        for a in range(2):
            wait_home(v, a)

            def one(j, carry):
                for n in range(2):
                    facc[j, n * WP : n * WP + WP, :] += part(j, a, n)
                return carry

            lax.fori_loop(0, 3, one, 0)
        wait_home(v, 2)

        def last(j, carry):
            scale = row_valid(j)
            for n in range(2):
                rows = slice(n * WP, n * WP + WP)
                result = ((facc[j, rows, :] + part(j, 2, n)) * scale).astype(bf16)
                for l in range(6):
                    xs.at[v, l, j].reshape(2 * WP, 128)[rows, :] = result[
                        :, 128 * l : 128 * l + 128
                    ]
            return carry

        lax.fori_loop(0, 3, last, 0)

    leave(0)

    settle(gr.at[pl.ds(0, 15)], 3)
    fy_away = pltpu.make_async_remote_copy(
        src_ref=fy,
        dst_ref=out_g.at[core],
        send_sem=gsend.at[4],
        recv_sem=grecv.at[4],
        device_id=buddy,
        device_id_type=MESH,
    )
    fy_away.start()
    fy_stays = pltpu.make_async_copy(fy, out_g.at[core], gloc)
    fy_stays.start()

    leave(1)

    def sent(phase, a, counts):
        for at in range(2):
            part = got.at[0, 0, :, :, pl.ds(0, counts[at]), 0]
            pltpu.make_async_copy(part, part, ssem.at[phase, a, at]).wait()

    for phase in range(4):
        for a in range(2):
            sent(phase, a, (15, 16))

    @pl.when(is_short(m))
    def _():
        for phase in range(2):
            sent(phase, 2, (14, 14))

    @pl.when(jnp.logical_not(is_short(m)))
    def _():
        for phase in range(2):
            sent(phase, 2, (13, 14))
            sent(2 + phase, 2, (15, 16))

    for at, part in (
        (0, gr.at[pl.ds(0, 15)]),
        (1, gz.at[pl.ds(0, 7)]),
        (2, fin.at[pl.ds(0, 7)]),
        (3, gr.at[pl.ds(0, 15)]),
    ):
        pltpu.make_async_copy(part, part, gsend.at[at]).wait()
    fy_away.wait()
    fy_stays.wait()


def mix(x_wide, c_wide, kept, pad_rows, w_one, w_two, b_one, b_two):
    forward_lon, inverse_lon = longitude_parts()
    ahead = np.stack([to_spectrum_table(forward_lon), to_spectrum_table(inverse_lon)])
    turned = ahead.transpose(0, 3, 1, 2).reshape(2, 2 * WP, 3 * 128)
    lf, li = lat_tables()
    as_bf16 = lambda table: jnp.asarray(table.astype(jnp.bfloat16))
    tables = (as_bf16(ahead), as_bf16(turned), as_bf16(lf), as_bf16(li))
    anywhere = pl.BlockSpec(memory_space=pl.ANY)
    vmem = pl.BlockSpec(memory_space=pltpu.VMEM)
    dma = pltpu.SemaphoreType.DMA
    return pl.pallas_call(
        kernel,
        out_shape=(
            pltpu.VMEM((2, 6, 3, WP, 2, 128), bf16),
            pltpu.VMEM((2, 4, 4, 128, 128), bf16),
        ),
        in_specs=[anywhere] * 3
        + [pl.BlockSpec(memory_space=pltpu.SMEM)]
        + [anywhere] * 2
        + [vmem] * 2
        + [anywhere] * 4,
        out_specs=(vmem, vmem),
        scratch_shapes=[
            pltpu.VMEM((2, 3, 128, 2 * WP), bf16),
            pltpu.VMEM((2, 2 * WP, 3 * 128), bf16),
            pltpu.VMEM((768, 768), bf16),
            pltpu.VMEM((768, 768), bf16),
            pltpu.VMEM((2, 2, NB, BS, BS), bf16),
            pltpu.VMEM((2, 768, 768), bf16),
            pltpu.VMEM((8, NB, H), jnp.int32),
            pltpu.VMEM((6, H, HC), bf16),
            pltpu.VMEM((2, 2, 1, HC), f32),
            pltpu.VMEM((2, 3, 6, 3, CHIPS, 4, 2, 128), bf16),
            pltpu.VMEM((2, 3, 3, 3, CHIPS, 2, 4, 2, 128), bf16),
            pltpu.VMEM((2, 3, 3, 3, CHIPS, 2, 4, 2, 128), bf16),
            pltpu.VMEM((2, 3, 6, 3, CHIPS, 4, 2, 128), bf16),
            pltpu.VMEM((3, 2 * WP, C), f32),
            pltpu.VMEM((3, HC, 768), bf16),
            pltpu.VMEM((3, HC, 768), bf16),
            pltpu.VMEM((3, HC, 768), f32),
            pltpu.VMEM((3, HC, 768), f32),
            pltpu.VMEM((HC, 768), f32),
            pltpu.VMEM((768, HC), bf16),
            pltpu.VMEM((HC, 768), bf16),
            pltpu.VMEM((2, 768, 768), f32),
            pltpu.VMEM((2, 8, 768), f32),
            pltpu.VMEM((4, 4, 128, 128), bf16),
            pltpu.VMEM((16, 128, 128), bf16),
            pltpu.VMEM((128, 128), bf16),
            pltpu.VMEM((8, 16, 128), bf16),
            pltpu.VMEM((16, 128), bf16),
            pltpu.VMEM((8, 16, 128), bf16),
            pltpu.VMEM((4, 4, 128, 128), bf16),
            dma((7,)),
            dma((2, 3)),
            dma((5,)),
            dma((4, 3, 2)),
            dma((4, 3)),
            dma((5,)),
            dma((5,)),
            dma,
        ],
        compiler_params=pltpu.CompilerParams(
            collective_id=0, has_side_effects=True, vmem_limit_bytes=56 * 2**20
        ),
    )(x_wide, c_wide, kept, pad_rows, w_one, w_two, b_one, b_two, *tables)


def finish(
    fields, parts, out_x, out_c, gw_one, gb_one, gw_two, gb_two,
    weights, biases, out_sem, g_sem,
):
    stores = []
    for v, target in enumerate((out_x, out_c)):
        for l in range(6):
            stores.append(
                pltpu.make_async_copy(
                    fields.at[v, l, :, pl.ds(0, W)],
                    target.at[:, :, :, pl.ds(128 * l, 128)],
                    out_sem.at[v, l],
                )
            )
            stores[-1].start()
    for mat, (weight, bias) in enumerate(((gw_one, gb_one), (gw_two, gb_two))):
        for p in range(2):
            for n in range(NB):
                block = parts[n // 4, n % 4, 2 * mat + p].astype(f32)
                weights[mat, p, n] = block[:BS, :BS]
                biases[mat, p, n : n + 1, :] = block[BS : BS + 1, :BS]
        stores.append(pltpu.make_async_copy(weights.at[mat], weight, g_sem.at[mat]))
        stores[-1].start()
        stores.append(pltpu.make_async_copy(biases.at[mat], bias, g_sem.at[2 + mat]))
        stores[-1].start()
    for store in stores:
        store.wait()


def settle_outputs(fields, out_g):
    anywhere = pl.BlockSpec(memory_space=pl.ANY)
    vmem = pl.BlockSpec(memory_space=pltpu.VMEM)
    return pl.pallas_call(
        finish,
        out_shape=(
            jax.ShapeDtypeStruct((3, W, 2, C), bf16),
            jax.ShapeDtypeStruct((3, W, 2, C), bf16),
            jax.ShapeDtypeStruct((2, NB, BS, BS), f32),
            jax.ShapeDtypeStruct((2, NB, BS), f32),
            jax.ShapeDtypeStruct((2, NB, BS, BS), f32),
            jax.ShapeDtypeStruct((2, NB, BS), f32),
        ),
        in_specs=[vmem, vmem],
        out_specs=(anywhere,) * 6,
        scratch_shapes=[
            pltpu.VMEM((2, 2, NB, BS, BS), f32),
            pltpu.VMEM((2, 2, NB, BS), f32),
            pltpu.SemaphoreType.DMA((2, 6)),
            pltpu.SemaphoreType.DMA((4,)),
        ],
        compiler_params=pltpu.CompilerParams(vmem_limit_bytes=56 * 2**20),
    )(
        pltpu.with_memory_space_constraint(fields, pltpu.VMEM),
        pltpu.with_memory_space_constraint(out_g, pltpu.VMEM),
    )


def on_device(inputs, cotangent, kept_modes, pad_rows, weight_one, bias_one, weight_two, bias_two):
    wide = lambda array: jnp.transpose(array, (1, 2, 0, 3))
    out_x, out_c, gw_one, gb_one, gw_two, gb_two = settle_outputs(
        *mix(
            wide(inputs),
            wide(cotangent),
            jnp.transpose(kept_modes, (2, 0, 1)),
            pad_rows,
            weight_one,
            weight_two,
            bias_one,
            bias_two,
        )
    )
    narrow = lambda array: jnp.transpose(array, (2, 0, 1, 3))
    return narrow(out_x), narrow(out_c), gw_one, gb_one, gw_two, gb_two


def solution(mesh):
    placed = (
        P("dp", "space", None, None),
        P("dp", "space", None, None),
        P(None, None, "space"),
        P(),
        P(),
        P(),
        P(),
        P(),
    )
    return jax.shard_map(
        on_device,
        mesh=mesh,
        in_specs=placed,
        out_specs=(P("dp", "space", None, None), P("dp", "space", None, None), P(), P(), P(), P()),
        check_vma=False,
    )
```

```python
import numpy as np

import jax
import jax.numpy as jnp
from jax import lax
from jax.experimental import pallas as pl
from jax.experimental.pallas import tpu as pltpu
from jax.sharding import PartitionSpec as P

shrink = 0.25
gelu_scale = 0.7978845608028654
gelu_cubic = 0.044715

H = 96
W = 180
WP = 192
C = 768
HC = 384
NB = 8
BS = 96
KWP = 96
CHIPS = 16
DEVICES = 32
IMAGES = 16
MESH = pl.DeviceIdType.MESH
f32 = jnp.float32
bf16 = jnp.bfloat16


def longitude_parts():
    wavenum = np.arange(KWP)[:, None]
    column = np.arange(W)[None, :]
    phase = np.float32(2.0 * np.pi / W) * (wavenum * column % W).astype(np.float32)
    scaling = (wavenum < W // 2 + 1).astype(np.float32) / np.sqrt(np.float32(W))
    double = np.where((wavenum == 0) | (2 * wavenum == W), 1.0, 2.0).astype(np.float32)
    cosine = np.cos(phase) * scaling
    sine = np.sin(phase) * scaling
    forward = np.stack([cosine, -sine])
    inverse = np.stack([double * cosine, -double * sine])
    return forward, inverse


def latitude_parts(sign):
    row = np.arange(H)[:, None]
    column = np.arange(H)[None, :]
    phase = np.float32(2.0 * np.pi / H) * (row * column % H).astype(np.float32)
    scaling = np.float32(1.0) / np.sqrt(np.float32(H))
    cosine = np.cos(phase) * scaling
    sine = np.float32(sign) * np.sin(phase) * scaling
    upper = np.stack([cosine, sine], -1)
    lower = np.stack([-sine, cosine], -1)
    return np.stack([upper, lower], 0)


def wavenumber_slots():
    slots = np.arange(KWP).reshape(16, 3, 2)
    slots[15, 1] = slots[12, 2]
    slots[12, 2] = slots[15, 2] = KWP - 1
    return slots


def to_spectrum_table(part):
    out = np.zeros((3, 16, 2, 2, 2, WP, 2), np.float32)
    grouped = part[:, wavenumber_slots()].transpose(2, 1, 0, 3, 4)
    for b in range(2):
        out[:, :, b, :, :, :W, b] = grouped
    return out.reshape(3, 128, 2 * WP)


def lat_tables():
    forward = latitude_parts(1.0)
    inverse = latitude_parts(-1.0)
    ahead = np.zeros((2, 2, 2, H, 3, 16, 2, 2, 2, 2), np.float32)
    back = np.zeros((3, 16, 2, 2, 2, 2, 2, 2, 2, H), np.float32)
    split = forward.reshape(2, H, 16, 2, 3, 2).transpose(0, 1, 4, 2, 3, 5)
    isplit = inverse.reshape(2, 16, 2, 3, H, 2).transpose(3, 1, 2, 0, 5, 4)
    for b in range(2):
        for kk in range(2):
            ahead[:, b, kk, :, :, :, :, b, :, kk] = split
            back[:, :, :, b, :, kk, :, b, kk, :] = isplit
    return ahead.reshape(768, 768), back.reshape(768, 768)


def gelu_both(value):
    tangent = jnp.tanh(gelu_scale * (value + gelu_cubic * value * value * value))
    inner = gelu_scale * (1.0 + 3.0 * gelu_cubic * value * value)
    half = 0.5 * (1.0 + tangent)
    return value * half, half + 0.5 * value * (1.0 - tangent * tangent) * inner


def dot(left, right):
    return jnp.dot(left, right, preferred_element_type=f32)


def kernel(
    x_in, c_in, kept_in, pad_in, w_one, w_two, b_one, b_two, ft_in, tt_in, lf_in, li_in,
    xs, out_g,
    fts, tts, lfs, lis, wraw, wd, kraw, keeps, brow,
    send, got, back, home, facc, spec, hid, slope, kt, tmp, fil, dtwo, gacc, bacc,
    gp, gr, s_two, gz, s_three, fin, fy,
    load_sem, xin, kept_sem, ssem, rsem, gsend, grecv, gloc,
):
    me = lax.axis_index("space")
    dp = lax.axis_index("dp")
    core = lax.rem(me, 2)
    other = 1 - core
    m = me // 2
    y = m // 4
    z = lax.rem(m, 4)
    zh = dp // 4
    x = lax.rem(dp, 4)
    depth = zh * 4 + z
    buddy = (dp, 2 * m + other)

    def greet(device):
        pl.semaphore_signal(barrier, inc=1, device_id=device, device_id_type=MESH)

    def greet_group(i, carry):
        greet((dp, lax.rem(me + i, DEVICES)))
        return carry

    def plane_device(i):
        row = lax.rem(y + i // 4, 4)
        return (zh * 4 + lax.rem(x + lax.rem(i, 4), 4), 2 * (row * 4 + z) + core)

    def greet_plane(i, carry):
        greet(plane_device(4 * (i // 3) + lax.rem(i, 3) + 1))
        return carry

    barrier = pltpu.get_barrier_semaphore()
    lax.fori_loop(1, DEVICES, greet_group, 0)
    lax.fori_loop(0, 12, greet_plane, 0)
    for i in range(4):
        greet((lax.rem(dp + 4, 8), 2 * (y * 4 + lax.rem(z + i, 4)) + core))

    def load(src, dst, at):
        return pltpu.make_async_copy(src, dst, load_sem.at[at])

    def start_field(v, ref):
        for j in range(3):
            for l in range(6):
                pltpu.make_async_copy(
                    ref.at[j, :, :, pl.ds(128 * l, 128)], xs.at[v, l, j, pl.ds(0, W)], xin.at[v, j]
                ).start()

    def wait_field(v, j):
        whole = xs.at[v, :, j, pl.ds(0, W)]
        pltpu.make_async_copy(whole, whole, xin.at[v, j]).wait()

    kept_own = load(kept_in, kraw.at[pl.ds(3 * core, 3)], 0)
    lon_table = load(ft_in, fts, 1)
    tables = [
        load(lf_in, lfs, 2),
        load(w_one, wraw.at[0], 3),
        load(w_two, wraw.at[1], 4),
        load(li_in, lis, 5),
        load(tt_in, tts, 6),
    ]
    lon_table.start()
    start_field(0, x_in)

    start_field(1, c_in)
    for copy in [kept_own] + tables:
        copy.start()
    xs[:, :, :, W:] = jnp.zeros((2, 6, 3, WP - W, 2, 128), bf16)
    for chip in (12, 15):
        home[:, 2, :, :, chip] = jnp.zeros((2, 6, 3, 4, 2, 128), bf16)

    kept_swap = pltpu.make_async_remote_copy(
        src_ref=kept_in,
        dst_ref=kraw.at[pl.ds(3 * core, 3)],
        send_sem=kept_sem.at[0],
        recv_sem=kept_sem.at[1],
        device_id=buddy,
        device_id_type=MESH,
    )

    def row_valid(j):
        return jnp.where(3 * me + j < H - pad_in[0], 1.0, 0.0).astype(f32)

    def transform(v, a, loading=False):
        for j in range(3):
            if loading:
                wait_field(v, j)
            field = jnp.concatenate(
                [xs.at[v, l, j].reshape(2 * WP, 128)[...] for l in range(6)], axis=1
            )
            result = (dot(fts[v, a], field) * row_valid(j)).astype(bf16)
            for l in range(6):
                send.at[v, a, l, j].reshape(128, 128)[...] = result[:, 128 * l : 128 * l + 128]

    def message(source, target, device, send_at, recv_at):
        pltpu.make_async_remote_copy(
            src_ref=source,
            dst_ref=target,
            send_sem=send_at,
            recv_sem=recv_at,
            device_id=device,
            device_id_type=MESH,
        ).start()

    def is_short(chip):
        return jnp.logical_or(chip == 12, chip == 15)

    def where_held(chip, a, body):
        if isinstance(a, int) and a != 2:
            body()
        else:
            pl.when(jnp.logical_or(a != 2, jnp.logical_not(is_short(chip))))(body)

    def send_chunk(v, a):
        def one(i, carry):
            peer = lax.rem(me + i, DEVICES)
            pm, pc = peer // 2, lax.rem(peer, 2)
            where_held(
                pm,
                a,
                lambda: message(
                    send.at[v, a, pl.ds(3 * pc, 3), :, pm],
                    got.at[v, a, :, :, m, core],
                    (dp, peer),
                    ssem.at[v, a, lax.rem(pc + core, 2)],
                    rsem.at[v, a],
                ),
            )
            return carry

        def own():
            pltpu.make_async_copy(
                send.at[v, a, pl.ds(3 * core, 3), :, m], got.at[v, a, :, :, m, core], rsem.at[v, a]
            ).start()

        lax.fori_loop(1, DEVICES, one, 0)
        where_held(m, a, own)

    def send_back(v, a, first=1, last=DEVICES, beside=None):
        def one(i, carry):
            peer = lax.rem(me + i, DEVICES)
            pm, pc = peer // 2, lax.rem(peer, 2)
            where_held(
                m,
                a,
                lambda: message(
                    back.at[v, a, :, :, pm, pc],
                    home.at[v, a, pl.ds(3 * core, 3), :, m],
                    (dp, peer),
                    ssem.at[2 + v, a, lax.rem(pc + core, 2)],
                    rsem.at[2 + v, a],
                ),
            )
            if beside is not None:
                beside(i)
            return carry

        def own():
            pltpu.make_async_copy(
                back.at[v, a, :, :, m, core],
                home.at[v, a, pl.ds(3 * core, 3), :, m],
                rsem.at[2 + v, a],
            ).start()

        lax.fori_loop(first, last, one, 0)
        if last == DEVICES:
            where_held(m, a, own)

    def wait_chunk(v, a):
        pltpu.make_async_copy(got.at[v, a], got.at[v, a], rsem.at[v, a]).wait()

    def wait_home(v, a):
        part = home.at[v, a] if a != 2 else home.at[v, a, :, :, pl.ds(0, 14)]
        pltpu.make_async_copy(part, part, rsem.at[2 + v, a]).wait()

    lon_table.wait()
    transform(0, 0, True)
    pl.semaphore_wait(barrier, 31 + 12 + 4)
    send_chunk(0, 0)

    def transform_and_send(i, carry):
        transform(i // 3, lax.rem(i, 3))
        send_chunk(i // 3, lax.rem(i, 3))
        return carry

    lax.fori_loop(1, 3, transform_and_send, 0)
    transform(1, 0, True)
    send_chunk(1, 0)
    lax.fori_loop(4, 6, transform_and_send, 0)
    kept_swap.start()

    def kept_moves(i):
        return pltpu.make_async_remote_copy(
            src_ref=kept_in.at[pl.ds(1, 2)],
            dst_ref=kraw.at[pl.ds(6, 2)],
            send_sem=kept_sem.at[2 + i],
            recv_sem=kept_sem.at[4],
            device_id=(dp, 30 + i),
            device_id_type=MESH,
        )

    @pl.when(me == 25)
    def _():
        for i in range(2):
            kept_moves(i).start()
        for i in range(2):
            kept_moves(i).wait_send()

    @pl.when(m == 15)
    def _():
        moved = kraw.at[pl.ds(6, 2)]
        pltpu.make_async_copy(moved, moved, kept_sem.at[4]).wait()


    gacc[...] = jnp.zeros_like(gacc)
    bacc[...] = jnp.zeros_like(bacc)
    for copy in [kept_own, kept_swap] + tables:
        copy.wait()
    lane = lax.broadcasted_iota(jnp.int32, (BS, HC), 1)
    line = lax.broadcasted_iota(jnp.int32, (BS, HC), 0)
    for mat in range(2):
        for n in range(4):
            select = jnp.where(lane == line + BS * n, 1.0, 0.0).astype(bf16)
            real = dot(wraw[mat, 0, 4 * core + n], select)
            imag = dot(wraw[mat, 1, 4 * core + n], select)
            up, down = BS * n, HC + BS * n
            wd[mat, up : up + BS, :HC] = real.astype(bf16)
            wd[mat, up : up + BS, HC:] = imag.astype(bf16)
            wd[mat, down : down + BS, :HC] = (-imag).astype(bf16)
            wd[mat, down : down + BS, HC:] = real.astype(bf16)

    lane = lax.broadcasted_iota(jnp.int32, (NB, HC), 1)
    block = lax.broadcasted_iota(jnp.int32, (NB, HC), 0) - 4 * core
    spread = (lane >= BS * block) & (lane < BS * block + BS)
    for slot in range(6):
        moved = 2 <= slot < 4
        bits = kraw[slot + 4 * (m // 15) if moved else slot].astype(f32).astype(bf16)
        wide = lax.dot_general(
            bits,
            jnp.where(spread, 1.0, 0.0).astype(bf16),
            (((0,), (0,)), ((), ())),
            preferred_element_type=f32,
        )
        if not moved:
            wide = wide * jnp.where(6 * m + slot < W // 2 + 1, 1.0, 0.0).astype(f32)
        keeps[slot] = wide.astype(bf16)
    lane = lax.broadcasted_iota(jnp.int32, (BS, HC), 1)
    tiled = sum(jnp.where(lane == line + BS * n, 1.0, 0.0).astype(f32) for n in range(4))
    for mat, ref in enumerate((b_one, b_two)):
        for p in range(2):
            copies = jnp.dot(
                ref[p], tiled, precision=lax.Precision.HIGHEST, preferred_element_type=f32
            )
            brow[mat, p] = jnp.where(spread, copies, 0.0).sum(0, keepdims=True)

    def spectral(phase, a, half):
        held = jnp.concatenate([got.at[phase, a, l].reshape(768, 128)[...] for l in range(3)], axis=1)
        return dot(lfs[half * HC : half * HC + HC, :], held)

    def unspectral(v, a):
        for t in range(2):
            rows = slice(t * HC, t * HC + HC)
            result = dot(lis[rows, :], fil[...]).astype(bf16)
            for l in range(3):
                back.at[v, a, l].reshape(768, 128)[rows, :] = result[:, 128 * l : 128 * l + 128]

    def product(left, mat):
        for n in range(3):
            tmp[:, 256 * n : 256 * n + 256] = dot(left, wd[mat, :, 256 * n : 256 * n + 256])

    def product_turned(left, mat):
        for n in range(3):
            tmp[:, 256 * n : 256 * n + 256] = lax.dot_general(
                left,
                wd[mat, 256 * n : 256 * n + 256, :],
                (((1,), (1,)), ((), ())),
                preferred_element_type=f32,
            )

    def rows_of(step):
        return pl.ds(pl.multiple_of(step * 32, 32), 32)

    def kept_rows(a, step):
        kk = lax.rem(step // 3, 2)
        q = pl.multiple_of(lax.rem(step, 3) * 32, 32)
        return keeps[2 * a + kk, pl.ds(q, 32), :].astype(f32)

    def forward(a, carry):
        where_held(m, a, lambda: forward_chunk(a))
        return carry

    def forward_chunk(a):
        wait_chunk(0, a)
        for p in range(2):
            spec[a, :, p * HC : p * HC + HC] = spectral(0, a, p).astype(bf16)
        product(spec[a], 0)

        def gelu_rows(step, carry):
            rows = rows_of(step)
            for p in range(2):
                part = slice(p * HC, p * HC + HC)
                value, tilt = gelu_both(tmp[rows, part] + brow[0, p])
                hid[a, rows, part] = value.astype(bf16)
                slope[a, rows, part] = tilt
            return carry

        lax.fori_loop(0, 12, gelu_rows, 0)
        product(hid[a], 1)

        def shrink_rows(step, carry):
            rows = rows_of(step)
            kept = kept_rows(a, step)
            for p in range(2):
                part = slice(p * HC, p * HC + HC)
                value = tmp[rows, part] + brow[1, p]
                tangent = jnp.tanh(value * (1.0 / shrink))
                filtered = (value - shrink * tangent) * kept
                fil[pl.ds(pl.multiple_of(p * HC + step * 32, 32), 32), :] = filtered.astype(bf16)
                kt[a, rows, part] = kept * (tangent * tangent)
            return carry

        lax.fori_loop(0, 12, shrink_rows, 0)
        unspectral(0, a)

    lax.fori_loop(0, 3, forward, 0)
    send_back(0, 0)
    send_back(0, 1)

    def add_grad(mat, left, right):
        for n in range(3):
            part = slice(256 * n, 256 * n + 256)
            gacc[mat, :, part] += lax.dot_general(
                left, right[:, part], (((0,), (0,)), ((), ())), preferred_element_type=f32
            )

    def backward(a, carry):
        where_held(m, a, lambda: backward_chunk(a))
        return carry

    def backward_chunk(a):
        wait_chunk(1, a)
        for p in range(2):
            tmp[:, p * HC : p * HC + HC] = spectral(1, a, p)

        def scaled_rows(mat, scale):
            def one(step, carry):
                rows = rows_of(step)
                for p in range(2):
                    part = slice(p * HC, p * HC + HC)
                    value = (tmp[rows, part] * scale[a, rows, part]).astype(bf16)
                    dtwo[rows, part] = value
                    bacc[mat, :, part] += value.astype(f32).reshape(4, 8, HC).sum(0)
                return carry

            lax.fori_loop(0, 12, one, 0)

        scaled_rows(1, kt)
        add_grad(1, hid[a], dtwo[...])
        product_turned(dtwo[...], 1)
        scaled_rows(0, slope)
        add_grad(0, spec[a], dtwo[...])
        product_turned(dtwo[...], 0)
        for p in range(2):
            fil[p * HC : p * HC + HC, :] = tmp[:, p * HC : p * HC + HC].astype(bf16)
        unspectral(1, a)

    lax.fori_loop(0, 3, backward, 0)

    first_row = lax.broadcasted_iota(jnp.int32, (128 - BS, 128), 0) == 0
    for mat in range(2):
        for n in range(4):
            start = BS * n // 128 * 128
            shift = BS * n - start
            window = 256 if shift + BS > 128 else 128
            up = slice(BS * n, BS * n + BS)
            down = slice(HC + BS * n, HC + BS * n + BS)
            left = slice(start, start + window)
            right = slice(HC + start, HC + start + window)

            def align(value):
                if shift:
                    value = pltpu.roll(value, window - shift, 1)
                return value[:, :128]

            gp[n, 2 * mat, :BS, :] = align(gacc[mat, up, left] + gacc[mat, down, right]).astype(bf16)
            gp[n, 2 * mat + 1, :BS, :] = align(gacc[mat, up, right] - gacc[mat, down, left]).astype(bf16)
            for p, part in enumerate((left, right)):
                summed = align(bacc[mat, :, part]).sum(0, keepdims=True)
                gp[n, 2 * mat + p, BS:, :] = jnp.where(first_row, summed, 0.0).astype(bf16)

    def to_depths(source, target, at):
        def one(i, carry):
            message(source(i), target, depth_device(i), gsend.at[at], grecv.at[at])
            return carry

        lax.fori_loop(1, 8, one, 0)

    def settle(part, at):
        pltpu.make_async_copy(part, part, grecv.at[at]).wait()

    def depth_of(i):
        return lax.rem(depth + i, 8)

    def depth_device(i):
        at = depth_of(i)
        return (4 * (at // 4) + x, 2 * (y * 4 + lax.rem(at, 4)) + core)

    def depth_rows(i):
        return pl.ds(pl.multiple_of(16 * i, 16), 16)

    def to_owner(i):
        row, column = lax.rem(y + i // 4, 4), lax.rem(x + lax.rem(i, 4), 4)
        message(gp.at[row, column], gr.at[4 * y + x], plane_device(i), gsend.at[0], grecv.at[0])

    def from_owner(i):
        message(fy.at[y, x], fy.at[y, x], plane_device(i), gsend.at[3], grecv.at[3])

    send_back(0, 2, 1, 16, to_owner)
    send_back(0, 2, 16)
    gr[4 * y + x] = gp[y, x]
    settle(gr.at[pl.ds(0, 15)], 0)
    total = gr[0].astype(f32)
    for i in range(1, 16):
        total = total + gr[i].astype(f32)
    s_two[...] = total.astype(bf16)
    to_depths(lambda i: s_two.at[depth_rows(depth_of(i))], gz.at[depth], 1)
    send_back(1, 0)
    gz[depth] = s_two[depth_rows(depth), :]
    settle(gz.at[pl.ds(0, 7)], 1)
    total = gz[0].astype(f32)
    for i in range(1, 8):
        total = total + gz[i].astype(f32)
    s_three[...] = (total * (1.0 / (IMAGES * H))).astype(bf16)
    to_depths(lambda i: s_three, fin.at[depth], 2)
    send_back(1, 1, 1, 16)
    fin[depth] = s_three[...]
    settle(fin.at[pl.ds(0, 7)], 2)
    fy[y, x] = fin[...].reshape(128, 128)
    send_back(1, 1, 16)
    send_back(1, 2, 1, 16, from_owner)
    send_back(1, 2, 16)

    def leave(v):
        def part(j, a, n):
            piece = jnp.concatenate(
                [home.at[v, a, l, j].reshape(128, 128)[...] for l in range(6)], axis=1
            )
            rows = slice(n * WP, n * WP + WP)
            return dot(tts[1 - v, rows, 128 * a : 128 * a + 128], piece)

        def begin(j, carry):
            for l in range(6):
                part = xs.at[v, l, j].reshape(2 * WP, 128)[...]
                facc[j, :, 128 * l : 128 * l + 128] = part.astype(f32)
            return carry

        lax.fori_loop(0, 3, begin, 0)
        for a in range(2):
            wait_home(v, a)

            def one(j, carry):
                for n in range(2):
                    facc[j, n * WP : n * WP + WP, :] += part(j, a, n)
                return carry

            lax.fori_loop(0, 3, one, 0)
        wait_home(v, 2)

        def last(j, carry):
            scale = row_valid(j)
            for n in range(2):
                rows = slice(n * WP, n * WP + WP)
                result = ((facc[j, rows, :] + part(j, 2, n)) * scale).astype(bf16)
                for l in range(6):
                    xs.at[v, l, j].reshape(2 * WP, 128)[rows, :] = result[
                        :, 128 * l : 128 * l + 128
                    ]
            return carry

        lax.fori_loop(0, 3, last, 0)

    leave(0)

    settle(gr.at[pl.ds(0, 15)], 3)
    fy_away = pltpu.make_async_remote_copy(
        src_ref=fy,
        dst_ref=out_g.at[core],
        send_sem=gsend.at[4],
        recv_sem=grecv.at[4],
        device_id=buddy,
        device_id_type=MESH,
    )
    fy_away.start()
    fy_stays = pltpu.make_async_copy(fy, out_g.at[core], gloc)
    fy_stays.start()

    leave(1)

    def sent(phase, a, counts):
        for at in range(2):
            part = got.at[0, 0, :, :, pl.ds(0, counts[at]), 0]
            pltpu.make_async_copy(part, part, ssem.at[phase, a, at]).wait()

    for phase in range(4):
        for a in range(2):
            sent(phase, a, (15, 16))

    @pl.when(is_short(m))
    def _():
        for phase in range(2):
            sent(phase, 2, (14, 14))

    @pl.when(jnp.logical_not(is_short(m)))
    def _():
        for phase in range(2):
            sent(phase, 2, (13, 14))
            sent(2 + phase, 2, (15, 16))

    for at, part in (
        (0, gr.at[pl.ds(0, 15)]),
        (1, gz.at[pl.ds(0, 7)]),
        (2, fin.at[pl.ds(0, 7)]),
        (3, gr.at[pl.ds(0, 15)]),
    ):
        pltpu.make_async_copy(part, part, gsend.at[at]).wait()
    fy_away.wait()
    fy_stays.wait()


def mix(x_wide, c_wide, kept, pad_rows, w_one, w_two, b_one, b_two):
    forward_lon, inverse_lon = longitude_parts()
    ahead = np.stack([to_spectrum_table(forward_lon), to_spectrum_table(inverse_lon)])
    turned = ahead.transpose(0, 3, 1, 2).reshape(2, 2 * WP, 3 * 128)
    lf, li = lat_tables()
    as_bf16 = lambda table: jnp.asarray(table.astype(jnp.bfloat16))
    tables = (as_bf16(ahead), as_bf16(turned), as_bf16(lf), as_bf16(li))
    anywhere = pl.BlockSpec(memory_space=pl.ANY)
    vmem = pl.BlockSpec(memory_space=pltpu.VMEM)
    dma = pltpu.SemaphoreType.DMA
    return pl.pallas_call(
        kernel,
        out_shape=(
            pltpu.VMEM((2, 6, 3, WP, 2, 128), bf16),
            pltpu.VMEM((2, 4, 4, 128, 128), bf16),
        ),
        in_specs=[anywhere] * 3
        + [pl.BlockSpec(memory_space=pltpu.SMEM)]
        + [anywhere] * 2
        + [vmem] * 2
        + [anywhere] * 4,
        out_specs=(vmem, vmem),
        scratch_shapes=[
            pltpu.VMEM((2, 3, 128, 2 * WP), bf16),
            pltpu.VMEM((2, 2 * WP, 3 * 128), bf16),
            pltpu.VMEM((768, 768), bf16),
            pltpu.VMEM((768, 768), bf16),
            pltpu.VMEM((2, 2, NB, BS, BS), bf16),
            pltpu.VMEM((2, 768, 768), bf16),
            pltpu.VMEM((8, NB, H), jnp.int32),
            pltpu.VMEM((6, H, HC), bf16),
            pltpu.VMEM((2, 2, 1, HC), f32),
            pltpu.VMEM((2, 3, 6, 3, CHIPS, 4, 2, 128), bf16),
            pltpu.VMEM((2, 3, 3, 3, CHIPS, 2, 4, 2, 128), bf16),
            pltpu.VMEM((2, 3, 3, 3, CHIPS, 2, 4, 2, 128), bf16),
            pltpu.VMEM((2, 3, 6, 3, CHIPS, 4, 2, 128), bf16),
            pltpu.VMEM((3, 2 * WP, C), f32),
            pltpu.VMEM((3, HC, 768), bf16),
            pltpu.VMEM((3, HC, 768), bf16),
            pltpu.VMEM((3, HC, 768), f32),
            pltpu.VMEM((3, HC, 768), f32),
            pltpu.VMEM((HC, 768), f32),
            pltpu.VMEM((768, HC), bf16),
            pltpu.VMEM((HC, 768), bf16),
            pltpu.VMEM((2, 768, 768), f32),
            pltpu.VMEM((2, 8, 768), f32),
            pltpu.VMEM((4, 4, 128, 128), bf16),
            pltpu.VMEM((16, 128, 128), bf16),
            pltpu.VMEM((128, 128), bf16),
            pltpu.VMEM((8, 16, 128), bf16),
            pltpu.VMEM((16, 128), bf16),
            pltpu.VMEM((8, 16, 128), bf16),
            pltpu.VMEM((4, 4, 128, 128), bf16),
            dma((7,)),
            dma((2, 3)),
            dma((5,)),
            dma((4, 3, 2)),
            dma((4, 3)),
            dma((5,)),
            dma((5,)),
            dma,
        ],
        compiler_params=pltpu.CompilerParams(
            collective_id=0, has_side_effects=True, vmem_limit_bytes=56 * 2**20
        ),
    )(x_wide, c_wide, kept, pad_rows, w_one, w_two, b_one, b_two, *tables)


def finish(
    fields, parts, out_x, out_c, gw_one, gb_one, gw_two, gb_two,
    weights, biases, out_sem, g_sem,
):
    stores = []
    for v, target in enumerate((out_x, out_c)):
        for l in range(6):
            stores.append(
                pltpu.make_async_copy(
                    fields.at[v, l, :, pl.ds(0, W)],
                    target.at[:, :, :, pl.ds(128 * l, 128)],
                    out_sem.at[v, l],
                )
            )
            stores[-1].start()
    for mat, (weight, bias) in enumerate(((gw_one, gb_one), (gw_two, gb_two))):
        for p in range(2):
            for n in range(NB):
                block = parts[n // 4, n % 4, 2 * mat + p].astype(f32)
                weights[mat, p, n] = block[:BS, :BS]
                biases[mat, p, n : n + 1, :] = block[BS : BS + 1, :BS]
        stores.append(pltpu.make_async_copy(weights.at[mat], weight, g_sem.at[mat]))
        stores[-1].start()
        stores.append(pltpu.make_async_copy(biases.at[mat], bias, g_sem.at[2 + mat]))
        stores[-1].start()
    for store in stores:
        store.wait()


def settle_outputs(fields, out_g):
    anywhere = pl.BlockSpec(memory_space=pl.ANY)
    vmem = pl.BlockSpec(memory_space=pltpu.VMEM)
    return pl.pallas_call(
        finish,
        out_shape=(
            jax.ShapeDtypeStruct((3, W, 2, C), bf16),
            jax.ShapeDtypeStruct((3, W, 2, C), bf16),
            jax.ShapeDtypeStruct((2, NB, BS, BS), f32),
            jax.ShapeDtypeStruct((2, NB, BS), f32),
            jax.ShapeDtypeStruct((2, NB, BS, BS), f32),
            jax.ShapeDtypeStruct((2, NB, BS), f32),
        ),
        in_specs=[vmem, vmem],
        out_specs=(anywhere,) * 6,
        scratch_shapes=[
            pltpu.VMEM((2, 2, NB, BS, BS), f32),
            pltpu.VMEM((2, 2, NB, BS), f32),
            pltpu.SemaphoreType.DMA((2, 6)),
            pltpu.SemaphoreType.DMA((4,)),
        ],
        compiler_params=pltpu.CompilerParams(vmem_limit_bytes=56 * 2**20),
    )(
        pltpu.with_memory_space_constraint(fields, pltpu.VMEM),
        pltpu.with_memory_space_constraint(out_g, pltpu.VMEM),
    )


def on_device(inputs, cotangent, kept_modes, pad_rows, weight_one, bias_one, weight_two, bias_two):
    wide = lambda array: jnp.transpose(array, (1, 2, 0, 3))
    out_x, out_c, gw_one, gb_one, gw_two, gb_two = settle_outputs(
        *mix(
            wide(inputs),
            wide(cotangent),
            jnp.transpose(kept_modes, (2, 0, 1)),
            pad_rows,
            weight_one,
            weight_two,
            bias_one,
            bias_two,
        )
    )
    narrow = lambda array: jnp.transpose(array, (2, 0, 1, 3))
    return narrow(out_x), narrow(out_c), gw_one, gb_one, gw_two, gb_two


def solution(mesh):
    placed = (
        P("dp", "space", None, None),
        P("dp", "space", None, None),
        P(None, None, "space"),
        P(),
        P(),
        P(),
        P(),
        P(),
    )
    return jax.shard_map(
        on_device,
        mesh=mesh,
        in_specs=placed,
        out_specs=(P("dp", "space", None, None), P("dp", "space", None, None), P(), P(), P(), P()),
        check_vma=False,
    )
```
